32 devices in a mesh: dp: 16 (over z, y, x), tensor: 2 (over core).
Axes of the slice: x: 2, y: 2, z: 4, core: 2. Of those that a mesh axis runs over, the one named last changes fastest.
Arguments:
- tokens: bfloat16 [6144, 1536], P(('dp', 'tensor')), may hold values from -6 to 6
- out_grad: bfloat16 [6144, 1536], P(('dp', 'tensor')), may hold values from -6 to 6
- lengths: int32 [16, 7], P('dp'), may hold values from 1 to 240, as said below
- attn_gain: bfloat16 [1536], replicated, may hold values from 0.5 to 1.5
- q_weight: bfloat16 [1536, 1536], P('dp', 'tensor'), may hold values from -0.21875 to 0.21875
- q_bias: bfloat16 [1536], P('tensor'), may hold values from -3 to 3
- k_weight: bfloat16 [1536, 256], P('dp', 'tensor'), may hold values from -0.21875 to 0.21875
- k_bias: bfloat16 [256], P('tensor'), may hold values from -3 to 3
- v_weight: bfloat16 [1536, 256], P('dp', 'tensor'), may hold values from -0.15625 to 0.15625
- v_bias: bfloat16 [256], P('tensor'), may hold values from -3 to 3
- o_weight: bfloat16 [1536, 1536], P('dp', 'tensor'), may hold values from -0.875 to 0.875
- mlp_gain: bfloat16 [1536], replicated, may hold values from 0.5 to 1.5
- gate_weight: bfloat16 [1536, 8960], P('dp', 'tensor'), may hold values from -0.15625 to 0.15625
- up_weight: bfloat16 [1536, 8960], P('dp', 'tensor'), may hold values from -0.15625 to 0.15625
- down_weight: bfloat16 [1536, 8960], P('dp', 'tensor'), may hold values from -0.0625 to 0.0625
Outputs:
- block_out: bfloat16 [6144, 1536], P(('dp', 'tensor'))
- tokens_grad: bfloat16 [6144, 1536], P(('dp', 'tensor'))
- attn_gain_grad: float32 [1536], replicated
- q_weight_grad: float32 [1536, 1536], P('dp', 'tensor')
- q_bias_grad: float32 [1536], P('tensor')
- k_weight_grad: float32 [1536, 256], P('dp', 'tensor')
- k_bias_grad: float32 [256], P('tensor')
- v_weight_grad: float32 [1536, 256], P('dp', 'tensor')
- v_bias_grad: float32 [256], P('tensor')
- o_weight_grad: float32 [1536, 1536], P('dp', 'tensor')
- mlp_gain_grad: float32 [1536], replicated
- gate_weight_grad: float32 [1536, 8960], P('dp', 'tensor')
- up_weight_grad: float32 [1536, 8960], P('dp', 'tensor')
- down_weight_grad: float32 [1536, 8960], P('dp', 'tensor')
The draws below stay inside these ranges and needn't reach their ends.
Inputs may be any that keep to these rules, and one draw needn't show every extreme that they name: Each row holds the lengths of the 7 sequences packed, in order, into the 384 tokens of one index of dp; they sum to 384, and the longest is exactly 240 tokens.
All inputs are finite; a program needn't handle non-finite values.
Results may differ from the reference program's by a relative error of at most 0.022.
Values may be sent and summed in bfloat16 or wider, within the bound.
No kernel may reach another device: no remote copies, remote signals or barrier semaphores. Data moves between devices by JAX's collectives and lax.ppermute only.
A program may use at most 320 MiB of HBM per device.

```python
import math
import jax
import jax.numpy as jnp
from jax import lax

D = 1536
HEADS = 12
KV_HEADS = 2
HEAD_DIM = 128
FF = 8960
TOK_GRP = 384
SLOTS = 7
GROUPS = 16
TOKENS = 6144
MOST = 240


def split_region(key, region):
    shares = jax.random.randint(key, (GROUPS, 3), 1, 100, dtype=jnp.int32)
    running = jnp.cumsum(shares, axis=1)
    boundaries = (region[:, None] - 3) * running // running[:, 2:3]
    before = jnp.concatenate([jnp.zeros((GROUPS, 1), jnp.int32), boundaries[:, :2]], axis=1)
    return boundaries - before + 1


def draw_lengths(key, part):
    key = jax.random.fold_in(key, 7)
    key_open, key_lead, key_trail = jax.random.split(key, 3)
    margin = TOK_GRP // 8
    opening = jax.random.randint(key_open, (GROUPS,), margin, TOK_GRP - MOST - margin + 1, dtype=jnp.int32)
    leading = split_region(key_lead, opening)
    trailing = split_region(key_trail, TOK_GRP - MOST - opening)
    longest = jnp.full((GROUPS, 1), MOST, jnp.int32)
    return jnp.concatenate([leading, longest, trailing], axis=1).astype(jnp.int32)


def raised(entries, own_key, source, target, blocks, factor):
    def block_of(dim):
        return (jnp.arange(entries.shape[dim]) // (entries.shape[dim] // blocks)).reshape((-1,) + (1,) * (entries.ndim - 1 - dim))

    near = jax.random.permutation(own_key, blocks)[block_of(target)]
    far = (block_of(target) + blocks // 2) % blocks
    return jnp.where((block_of(source) == near) | (block_of(source) == far), factor * entries, entries)


def block_levels(stream_key, shape, cuts, smallest, high):
    gain, own = 1.0, jax.random.fold_in(stream_key, 6)
    for dim, blocks in cuts:
        draws = jnp.exp(jax.random.uniform(jax.random.fold_in(own, dim), (blocks,), jnp.float32, smallest / len(cuts), high / len(cuts)))
        gain = gain * jnp.repeat(draws, shape[dim] // blocks).reshape([-1 if axis == dim else 1 for axis in range(len(shape))])
    return gain


def normal_values(key, dims, deviation, limit, cuts=(), kind=jnp.bfloat16):
    factor_of = block_levels(key, dims, cuts, -0.22, 0.18) if cuts else 1.0
    drawn = jax.random.normal(key, dims, jnp.float32) * deviation * factor_of
    return jnp.minimum(jnp.maximum(drawn, -limit), limit).astype(kind)


def noise_with(stream_key, dims, spread, limit, cuts, heavy, held_as=jnp.bfloat16):
    result = spread * jax.random.normal(stream_key, dims, jnp.float32)
    if cuts:
        result = result * block_levels(stream_key, dims, cuts, -0.22, 0.18)
    return jnp.clip(raised(result, jax.random.fold_in(stream_key, 3), *heavy), -limit, limit).astype(held_as)


def setup_inputs(seed: int = 0) -> dict:
    key_list = jax.random.split(jax.random.key(seed), 16)
    return {
        "tokens": noise_with(key_list[0], (TOKENS, D), 1.0, 6.0, ((0, 32),), (0, 1, 32, 2.75)),
        "out_grad": noise_with(key_list[1], (TOKENS, D), 1.0, 6.0, ((0, 32),), (0, 1, 32, 2.75)),
        "lengths": draw_lengths(jax.random.fold_in(key_list[15], 71), 0),
        "attn_gain": jnp.clip(1.0 + 0.1 * jax.random.normal(key_list[3], (D,), jnp.float32), 0.5, 1.5).astype(jnp.bfloat16),
        "q_weight": normal_values(key_list[4], (D, HEADS * HEAD_DIM), (D // 2) ** -0.5, 0.21875, ((0, 16), (1, 2))),
        "q_bias": normal_values(key_list[5], (HEADS * HEAD_DIM,), 0.5, 3.0, ((0, 2),)),
        "k_weight": normal_values(key_list[6], (D, KV_HEADS * HEAD_DIM), (D // 2) ** -0.5, 0.21875, ((0, 16), (1, 2))),
        "k_bias": normal_values(key_list[7], (KV_HEADS * HEAD_DIM,), 0.5, 3.0, ((0, 2),)),
        "v_weight": normal_values(key_list[8], (D, KV_HEADS * HEAD_DIM), D ** -0.5, 0.15625, ((0, 16), (1, 2))),
        "v_bias": normal_values(key_list[9], (KV_HEADS * HEAD_DIM,), 0.5, 3.0, ((0, 2),)),
        "o_weight": normal_values(key_list[10], (D, HEADS * HEAD_DIM), (HEADS * HEAD_DIM // 32) ** -0.5, 0.875, ((0, 16), (1, 2))),
        "mlp_gain": jnp.clip(1.0 + 0.1 * jax.random.normal(key_list[11], (D,), jnp.float32), 0.5, 1.5).astype(jnp.bfloat16),
        "gate_weight": normal_values(key_list[12], (D, FF), D ** -0.5, 0.15625, ((0, 16), (1, 2))),
        "up_weight": normal_values(key_list[13], (D, FF), D ** -0.5, 0.15625, ((0, 16), (1, 2))),
        "down_weight": normal_values(key_list[14], (D, FF), FF ** -0.5, 0.0625, ((0, 16), (1, 2))),
    }


EPSILON = 1e-06
ROPE_BASE = 1000000.0
MASKED = -1e+30
HIGH = lax.Precision.HIGHEST

@jax.custom_vjp
def low(v):
    return lax.optimization_barrier(v.astype(jnp.bfloat16)).astype(jnp.float32)

@jax.custom_vjp
def low_back(v):
    return v

def low_keep(v):
    return (low(v), None)

def low_pass(kept, grad):
    return (grad,)

def back_keep(v):
    return (v, None)

def back_low(kept, grad):
    return (low(grad),)
low.defvjp(low_keep, low_pass)
low_back.defvjp(back_keep, back_low)

def product(left_rows, right_rows):
    return jnp.dot(left_rows, right_rows, precision=HIGH)

def product_t(left_rows, right_rows):
    return jnp.dot(left_rows, right_rows.T, precision=HIGH)

def rms_norm(values, gain_vec):
    return values * lax.rsqrt(lax.optimization_barrier(jnp.mean(values * values, axis=1, keepdims=True)) + EPSILON) * gain_vec[None, :]

def rope_tables(positions, width):
    half_width = width // 2
    frequency = jnp.power(ROPE_BASE, -2.0 * jnp.arange(half_width, dtype=jnp.float32) / width)
    angles = positions.astype(jnp.float32)[:, None] * frequency[None, :]
    return (jnp.cos(angles), jnp.sin(angles))

def rotate(values, cosine_table, sine_table):
    half_width = values.shape[-1] // 2
    lower_half = values[..., :half_width]
    upper_half = values[..., half_width:]
    return jnp.concatenate([lower_half * cosine_table - upper_half * sine_table, upper_half * cosine_table + lower_half * sine_table], axis=-1)

def block_layer(inputs, params, segment, positions):
    attn_gain, q_weight, q_bias, k_weight, k_bias, v_weight, v_bias, o_weight, mlp_gain, gate_weight, up_weight, down_weight = params
    group_rows = inputs.shape[0]
    per_group = HEADS // KV_HEADS
    score_scale = 1.0 / math.sqrt(HEAD_DIM)
    cosine_table, sine_table = rope_tables(positions, HEAD_DIM)
    attn_in = low(rms_norm(inputs, attn_gain))
    q_lin = low_back(product(attn_in, q_weight) + q_bias[None, :])
    k_lin = low_back(product(attn_in, k_weight) + k_bias[None, :])
    values = low(low_back(product(attn_in, v_weight) + v_bias[None, :])).reshape(group_rows, KV_HEADS, HEAD_DIM)
    queries = low(rotate(q_lin.reshape(group_rows, KV_HEADS, per_group, HEAD_DIM), cosine_table[:, None, None, :], sine_table[:, None, None, :]))
    key_rows = low(rotate(k_lin.reshape(group_rows, KV_HEADS, HEAD_DIM), cosine_table[:, None, :], sine_table[:, None, :]))
    places = jnp.arange(group_rows, dtype=jnp.int32)
    allowed = (segment[:, None] == segment[None, :]) & (places[None, :] <= places[:, None])
    raw_scores = low_back(jnp.einsum('qgpd,kgd->gpqk', queries, key_rows, precision=HIGH))
    scores = jnp.where(allowed[None, None], raw_scores * score_scale, MASKED)
    row_peak = lax.optimization_barrier(jnp.max(scores, axis=-1, keepdims=True))
    exponent = jnp.exp(scores - row_peak)
    prob_rows = low(exponent / lax.optimization_barrier(jnp.sum(exponent, axis=-1, keepdims=True)))
    mixed_heads = jnp.einsum('gpqk,kgd->qgpd', prob_rows, values, precision=HIGH).reshape(group_rows, HEADS * HEAD_DIM)
    mixed_heads = low(low_back(mixed_heads))
    hidden_state = inputs + low_back(product_t(mixed_heads, o_weight))
    mlp_in = low(rms_norm(hidden_state, mlp_gain))
    gate_val = low_back(product(mlp_in, gate_weight))
    up_val = low_back(product(mlp_in, up_weight))
    hidden_units = low(gate_val * jax.nn.sigmoid(gate_val) * up_val)
    return hidden_state + low_back(product_t(hidden_units, down_weight))

def reference(tokens, out_grad, lengths, attn_gain, q_weight, q_bias, k_weight, k_bias, v_weight, v_bias, o_weight, mlp_gain, gate_weight, up_weight, down_weight):
    params = tuple((weight_arg.astype(jnp.float32) for weight_arg in (attn_gain, q_weight, q_bias, k_weight, k_bias, v_weight, v_bias, o_weight, mlp_gain, gate_weight, up_weight, down_weight)))
    inputs = tokens.astype(jnp.float32).reshape(GROUPS, TOK_GRP, D)
    cotangent = out_grad.astype(jnp.float32).reshape(GROUPS, TOK_GRP, D)
    seq_ends = jnp.cumsum(lengths, axis=1).astype(jnp.int32)
    starts = seq_ends - lengths
    places = jnp.arange(TOK_GRP, dtype=jnp.int32)
    segment = lax.optimization_barrier(jnp.sum((places[None, :, None] >= seq_ends[:, None, :]).astype(jnp.int32), axis=2))
    slot_ids = jnp.arange(SLOTS, dtype=jnp.int32)
    offset = lax.optimization_barrier(jnp.sum(jnp.where(segment[:, :, None] == slot_ids[None, None, :], starts[:, None, :], 0), axis=2))
    positions = (places[None, :] - offset).astype(jnp.int32)

    def group_step(summed, group_items):
        group_in, group_grad, group_segment, group_positions = group_items

        def forward(layer_in, weights):
            return block_layer(layer_in, weights, group_segment, group_positions)
        group_out, pullback = jax.vjp(forward, group_in, params)
        input_grad, weight_grads = pullback(group_grad)
        return (tuple((earlier + update for earlier, update in zip(summed, weight_grads))), (group_out, input_grad))
    zero_grads = tuple((jnp.zeros_like(weight_arg) for weight_arg in params))
    totals, (outputs, input_grads) = lax.scan(group_step, zero_grads, (inputs, cotangent, segment, positions))
    return (outputs.reshape(TOKENS, D).astype(jnp.bfloat16), input_grads.reshape(TOKENS, D).astype(jnp.bfloat16), totals[0], totals[1], totals[2], totals[3], totals[4], totals[5], totals[6], totals[7], totals[8], totals[9], totals[10], totals[11])
```

```python
import math

import jax
import jax.numpy as jnp
from jax import lax
from jax.sharding import PartitionSpec as P

HEAD_DIM = 128
EPSILON = 1e-06
ROPE_BASE = 1000000.0
MASKED = -1e30
LINE = 4
LANES = 128
BF = jnp.bfloat16
F32 = jnp.float32


def normalize(values):
    factor = lax.rsqrt(jnp.mean(values * values, axis=1, keepdims=True) + EPSILON)
    return (values * factor, factor)


def norm_back(grad_normed, normed, factor, gain_vec):
    scaled = grad_normed * gain_vec[None, :]
    row_inner = jnp.mean(scaled * normed, axis=1, keepdims=True)
    return (factor * (scaled - normed * row_inner), jnp.sum(grad_normed * normed, axis=0))


def rope_tables(positions, width):
    half_width = width // 2
    frequency = jnp.power(ROPE_BASE, -2.0 * jnp.arange(half_width, dtype=F32) / width)
    angles = positions.astype(F32)[:, None] * frequency[None, :]
    return (jnp.cos(angles), jnp.sin(angles))


def rotate(values, cosine_table, sine_table):
    half_width = values.shape[-1] // 2
    lower_half = values[..., :half_width]
    upper_half = values[..., half_width:]
    return jnp.concatenate(
        [
            lower_half * cosine_table - upper_half * sine_table,
            upper_half * cosine_table + lower_half * sine_table,
        ],
        axis=-1,
    )


def unrotate(values, cosine_table, sine_table):
    return rotate(values, cosine_table, -sine_table)


def segment_info(length_row, places):
    seq_ends = jnp.cumsum(length_row)
    starts = seq_ends - length_row
    segment = jnp.sum((places[:, None] >= seq_ends[None, :]).astype(jnp.int32), axis=1)
    slot_ids = jnp.arange(length_row.shape[0], dtype=jnp.int32)
    offset = jnp.sum(jnp.where(segment[:, None] == slot_ids[None, :], starts[None, :], 0), axis=1)
    return (segment, places - offset)


class Topo:
    def __init__(self):
        self.dp = lax.axis_size("dp")
        self.square = self.dp // LINE
        self.me = lax.axis_index("dp")
        self.core = lax.axis_index("tensor")
        self.line_at = self.me // self.square
        self.square_at = self.me % self.square
        line_bits = [self.square << i for i in range(LINE.bit_length() - 1)]
        square_bits = [1 << i for i in range(self.square.bit_length() - 1)]
        self.line = (line_bits, line_bits[::-1])
        self.squares = (square_bits, square_bits[::-1])

    def swap(self, array, bits, phase):
        perm = []
        for place in range(self.dp):
            for core in range(2):
                perm.append((place * 2 + core, (place ^ bits[core][phase]) * 2 + core))
        return lax.ppermute(array, ("dp", "tensor"), perm)

    def other_core(self, array):
        return lax.ppermute(array, "tensor", [(0, 1), (1, 0)])

    def offset(self, bits, index, unit):
        totals = [0, 0]
        for core in range(2):
            for phase, bit in enumerate(bits[core]):
                if index >> phase & 1:
                    totals[core] ^= bit // unit
        return jnp.where(self.core == 0, totals[0], totals[1])

    def gather(self, own, bits):
        pieces = [own]
        for phase in range(len(bits[0])):
            pieces = pieces + [self.swap(piece, bits, phase) for piece in pieces]
        return pieces

    def gather_joined(self, own, bits):
        joined = own
        for phase in range(len(bits[0])):
            joined = jnp.concatenate([joined, self.swap(joined, bits, phase)], axis=0)
        return joined

    def scatter_sum(self, array, bits):
        for phase in reversed(range(len(bits[0]))):
            half = array.shape[0] // 2
            got = self.swap(array[half:], bits, phase)
            array = (array[:half].astype(F32) + got.astype(F32)).astype(BF)
        return array

    def total(self, array):
        for bits in (self.line, self.squares):
            for phase in range(len(bits[0])):
                array = array + self.swap(array, bits, phase)
        return array

    def exchange(self, chunks, bits):
        rows = chunks[0].shape[0]
        held = [chunk for chunk in chunks]
        for phase in range(len(bits[0])):
            step = 1 << phase
            keep = [i for i in range(len(chunks)) if not i & step]
            keep = [i for i in keep if held[i] is not None]
            sent = jnp.concatenate([held[i + step] for i in keep], axis=0)
            got = self.swap(sent, bits, phase)
            parts = jnp.split(got, len(keep), axis=0)
            for i, part in zip(keep, parts):
                held[i] = jnp.concatenate([held[i], part], axis=0)
                held[i + step] = None
        return jnp.split(held[0], len(chunks), axis=0)

    def ordered(self, pieces, bits, unit, at):
        count = len(pieces)
        tables = []
        for core in range(2):
            table = [0] * count
            for index in range(count):
                total = 0
                for phase, bit in enumerate(bits[core]):
                    if index >> phase & 1:
                        total ^= bit // unit
                table[total] = index
            tables.append(table)
        tables = jnp.asarray(tables, jnp.int32)[self.core]
        stacked = jnp.stack(pieces)
        return [
            lax.dynamic_index_in_dim(
                stacked, lax.dynamic_index_in_dim(tables, place ^ at, 0, False), 0, False
            )
            for place in range(count)
        ]


def to_inner(rows, topo):
    count, width = rows.shape
    rest = width // topo.dp
    cut = rows.reshape(count, LINE, topo.square, rest).transpose(2, 0, 1, 3)
    cut = cut.reshape(topo.square, count, LINE * rest)
    return jnp.concatenate(
        [
            lax.dynamic_index_in_dim(cut, topo.square_at ^ i, 0, False)
            for i in range(topo.square)
        ],
        axis=1,
    )


def to_outer(rows, topo):
    count, width = rows.shape
    rest = width // topo.dp
    cut = rows.reshape(count, topo.square, LINE * rest).transpose(1, 0, 2)
    cut = jnp.stack(
        [
            lax.dynamic_index_in_dim(cut, topo.square_at ^ i, 0, False)
            for i in range(topo.square)
        ]
    )
    cut = cut.reshape(topo.square, count, LINE, rest).transpose(1, 2, 0, 3)
    return cut.reshape(count, width)


def dot(left, right):
    return jnp.dot(left, right, preferred_element_type=F32)


def dot_t(left, right):
    return lax.dot_general(left, right, (((1,), (1,)), ((), ())), preferred_element_type=F32)


def t_dot(left, right):
    return lax.dot_general(left, right, (((0,), (0,)), ((), ())), preferred_element_type=F32)


def attention_scores(queries, key_rows, allowed):
    score_scale = 1.0 / math.sqrt(queries.shape[-1])
    raw_scores = jnp.einsum("qgpd,kgd->gpqk", queries, key_rows, preferred_element_type=F32)
    return jnp.where(allowed[None, None], raw_scores * score_scale, MASKED)


def per_device(
    tokens,
    out_grad,
    lengths,
    attn_gain,
    q_weight,
    q_bias,
    k_weight,
    k_bias,
    v_weight,
    v_bias,
    o_weight,
    mlp_gain,
    gate_weight,
    up_weight,
    down_weight,
):
    topo = Topo()
    local_rows, width = tokens.shape
    group_rows = 2 * local_rows
    q_cols = q_weight.shape[1]
    kv_cols = k_weight.shape[1]
    qkv_cols = q_cols + 2 * kv_cols
    ff_cols = gate_weight.shape[1]
    part = -(-ff_cols // (LINE * LANES)) * LANES
    kv_groups = kv_cols // HEAD_DIM
    per_group = q_cols // HEAD_DIM // kv_groups
    score_scale = 1.0 / math.sqrt(HEAD_DIM)

    def line_gather(shard):
        pieces = jnp.split(topo.gather_joined(shard, topo.line), LINE, axis=0)
        return jnp.concatenate(topo.ordered(pieces, topo.line, topo.square, topo.line_at), axis=0)

    def square_gather(shard):
        pieces = topo.gather(shard, topo.squares)
        return jnp.concatenate(topo.ordered(pieces, topo.squares, 1, 0), axis=0)

    def square_scatter(grads):
        pieces = jnp.split(grads.astype(BF), topo.square, axis=0)
        by_index = topo.ordered(pieces, tuple(b for b in topo.squares), 1, 0)
        return topo.scatter_sum(jnp.concatenate(by_index, axis=0), topo.squares)

    def line_offset(index):
        return topo.line_at ^ topo.offset(topo.line, index, topo.square)

    def columns_in(shards):
        padded = [jnp.pad(s, ((0, 0), (0, LINE * part - ff_cols))) for s in shards]
        chunks = []
        for index in range(LINE):
            start = line_offset(index) * part
            chunks.append(
                jnp.concatenate(
                    [lax.dynamic_slice_in_dim(s, start, part, axis=1) for s in padded], axis=1
                )
            )
        got = topo.exchange(chunks, topo.line)
        return jnp.concatenate(topo.ordered(got, topo.line, topo.square, topo.line_at), axis=0)

    def columns_out(piece, count):
        rows = piece.shape[0] // LINE
        chunks = [
            lax.dynamic_slice_in_dim(piece, line_offset(index) * rows, rows, axis=0)
            for index in range(LINE)
        ]
        got = topo.ordered(
            topo.exchange(chunks, topo.line), topo.line, topo.square, topo.line_at
        )
        return [
            jnp.concatenate([g[:, i * part : (i + 1) * part] for g in got], axis=1)[
                :, :ff_cols
            ].astype(F32)
            for i in range(count)
        ]

    def rows_out(piece):
        rows = piece.shape[0] // LINE
        chunks = [
            lax.dynamic_slice_in_dim(piece, line_offset(index) * rows, rows, axis=0)
            for index in range(LINE)
        ]
        return topo.scatter_sum(jnp.concatenate(chunks, axis=0), topo.line).astype(F32)

    def both_cores(rows):
        return jnp.concatenate([rows, topo.other_core(rows)], axis=0)

    def core_sum(rows):
        half = rows.shape[0] // 2
        return rows[:half] + topo.other_core(rows[half:].astype(BF)).astype(F32)

    def line_tokens(rows):
        return both_cores(topo.gather_joined(rows, topo.line))

    def line_sum(partial):
        return topo.scatter_sum(core_sum(partial).astype(BF), topo.line).astype(F32)

    row_ids = jnp.arange(local_rows, dtype=jnp.int32)
    places = jnp.concatenate(
        [topo.core * local_rows + row_ids, (1 - topo.core) * local_rows + row_ids]
    )
    segment, positions = segment_info(lengths[0], places)
    allowed = (segment[:, None] == segment[None, :]) & (places[None, :] <= places[:, None])
    cosine_table, sine_table = rope_tables(positions, HEAD_DIM)
    q_cosine = cosine_table[:, None, None, :]
    q_sine = sine_table[:, None, None, :]
    k_cosine = cosine_table[:, None, :]
    k_sine = sine_table[:, None, :]

    inputs_low = to_inner(tokens, topo)
    out_grad_low = to_inner(out_grad, topo)
    gains = to_inner(jnp.stack([attn_gain, mlp_gain]), topo).astype(F32)
    gain_one, gain_two = gains[0], gains[1]
    inputs = inputs_low.astype(F32)
    bias_all = jnp.concatenate([q_bias, k_bias, v_bias]).astype(F32)

    qkv_local = jnp.concatenate([q_weight, k_weight, v_weight], axis=1)
    qkv_all = square_gather(line_gather(qkv_local))
    o_all = square_gather(line_gather(o_weight))
    down_all = square_gather(columns_in([down_weight]))
    grad_out_all = line_tokens(out_grad_low)
    gate_up = square_gather(columns_in([gate_weight, up_weight]))

    normed_one, factor_one = normalize(inputs)
    attn_in = both_cores((normed_one * gain_one[None, :]).astype(BF))
    linear = dot(attn_in, qkv_all) + bias_all[None, :]
    queries = rotate(
        linear[:, :q_cols].reshape(group_rows, kv_groups, per_group, HEAD_DIM), q_cosine, q_sine
    ).astype(BF)
    key_rows = rotate(
        linear[:, q_cols : q_cols + kv_cols].reshape(group_rows, kv_groups, HEAD_DIM),
        k_cosine,
        k_sine,
    ).astype(BF)
    values = linear[:, q_cols + kv_cols :].reshape(group_rows, kv_groups, HEAD_DIM).astype(BF)
    scores = attention_scores(queries, key_rows, allowed)
    row_peak = jnp.max(scores, axis=-1, keepdims=True)
    exponent = jnp.exp(scores - row_peak)
    row_mass = jnp.sum(exponent, axis=-1, keepdims=True)
    log_mass = row_peak + jnp.log(row_mass)
    probs_low = (exponent / row_mass).astype(BF)
    mixed_heads = jnp.einsum("gpqk,kgd->qgpd", probs_low, values, preferred_element_type=F32)
    mixed_heads = mixed_heads.reshape(group_rows, q_cols).astype(BF)
    hidden_state = inputs + core_sum(dot_t(mixed_heads, o_all))
    normed_two, factor_two = normalize(hidden_state)

    mlp_in = line_tokens((normed_two * gain_two[None, :]).astype(BF))
    grad_hidden = dot(grad_out_all, down_all)
    gate_up_out = dot(mlp_in, gate_up)
    gate_val = gate_up_out[:, :part]
    up_val = gate_up_out[:, part:]
    sigmoid_gate = jax.nn.sigmoid(gate_val)
    activated = gate_val * sigmoid_gate
    hidden_units = (activated * up_val).astype(BF)
    grad_gate = (
        grad_hidden * up_val * sigmoid_gate * (1.0 + gate_val * (1.0 - sigmoid_gate))
    ).astype(BF)
    grad_up = (grad_hidden * activated).astype(BF)
    grad_gate_up = jnp.concatenate([grad_gate, grad_up], axis=1)
    grad_normed_two = line_sum(dot_t(grad_gate_up, gate_up))
    block_out = (hidden_state + line_sum(dot_t(hidden_units, down_all))).astype(BF)
    gate_grads, up_grads = columns_out(square_scatter(t_dot(mlp_in, grad_gate_up)), 2)
    (down_grads,) = columns_out(square_scatter(t_dot(grad_out_all, hidden_units)), 1)

    back_two, gain_two_grad = norm_back(grad_normed_two, normed_two, factor_two, gain_two)
    grad_state = out_grad_low.astype(F32) + back_two
    grad_state_all = both_cores(grad_state.astype(BF))
    o_grads = rows_out(square_scatter(t_dot(grad_state_all, mixed_heads)))
    grad_mixed = dot(grad_state_all, o_all)
    grad_heads = grad_mixed.astype(BF).reshape(group_rows, kv_groups, per_group, HEAD_DIM)
    scores_again = attention_scores(queries, key_rows, allowed)
    prob_rows = jnp.exp(scores_again - log_mass)
    grad_probs = jnp.einsum("qgpd,kgd->gpqk", grad_heads, values, preferred_element_type=F32)
    row_inner = jnp.sum(prob_rows * grad_probs, axis=-1, keepdims=True)
    grad_scores = (prob_rows * (grad_probs - row_inner) * score_scale).astype(BF)
    grad_values = jnp.einsum(
        "gpqk,qgpd->kgd", prob_rows.astype(BF), grad_heads, preferred_element_type=F32
    )
    grad_queries = jnp.einsum("gpqk,kgd->qgpd", grad_scores, key_rows, preferred_element_type=F32)
    grad_keys = jnp.einsum("gpqk,qgpd->kgd", grad_scores, queries, preferred_element_type=F32)
    grad_linear = jnp.concatenate(
        [
            unrotate(grad_queries, q_cosine, q_sine).reshape(group_rows, q_cols),
            unrotate(grad_keys, k_cosine, k_sine).reshape(group_rows, kv_cols),
            grad_values.reshape(group_rows, kv_cols),
        ],
        axis=1,
    ).astype(BF)
    bias_grad = jnp.sum(grad_linear.astype(F32), axis=0)
    qkv_grads = rows_out(square_scatter(t_dot(attn_in, grad_linear)))
    grad_normed_one = core_sum(dot_t(grad_linear, qkv_all))
    back_one, gain_one_grad = norm_back(grad_normed_one, normed_one, factor_one, gain_one)
    tokens_grad = (grad_state + back_one).astype(BF)
    gain_grads = to_outer(jnp.stack([gain_one_grad, gain_two_grad]), topo)
    gain_grads = gain_grads + topo.other_core(gain_grads)
    small = topo.total(jnp.concatenate([bias_grad, gain_grads.reshape(-1)]).reshape(-1, LANES))
    small = small.reshape(-1)
    own_bias = small[:qkv_cols]
    gain_sum = small[qkv_cols:].reshape(2, width)
    return (
        to_outer(block_out, topo),
        to_outer(tokens_grad, topo),
        gain_sum[0],
        qkv_grads[:, :q_cols],
        own_bias[:q_cols],
        qkv_grads[:, q_cols : q_cols + kv_cols],
        own_bias[q_cols : q_cols + kv_cols],
        qkv_grads[:, q_cols + kv_cols : qkv_cols],
        own_bias[q_cols + kv_cols :],
        o_grads,
        gain_sum[1],
        gate_grads,
        up_grads,
        down_grads,
    )


def solution(mesh):
    rows = P(("dp", "tensor"), None)
    both = P("dp", "tensor")
    half = P("tensor")
    in_specs = (
        rows, rows, P("dp", None), P(), both, half, both, half, both, half, both, P(), both, both, both,
    )
    out_specs = (
        rows, rows, P(), both, half, both, half, both, half, both, P(), both, both, both,
    )
    return jax.shard_map(
        per_device, mesh=mesh, in_specs=in_specs, out_specs=out_specs, check_vma=False
    )
```

```python
import functools
import math

import jax
import jax.numpy as jnp
from jax import lax
from jax.experimental import pallas as pl
from jax.experimental.pallas import tpu as pltpu
from jax.sharding import PartitionSpec as P

HEAD_DIM = 128
EPSILON = 1e-06
ROPE_BASE = 1000000.0
MASKED = -1e30
LINE = 4
LANES = 128
BF = jnp.bfloat16
F32 = jnp.float32
VMEM_BYTES = 56 * 2**20
ANY = pl.BlockSpec(memory_space=pl.ANY)


def normalize(values):
    factor = lax.rsqrt(jnp.mean(values * values, axis=1, keepdims=True) + EPSILON)
    return (values * factor, factor)


def plain_norm_back(grad_normed, normed, factor, gain_vec):
    scaled = grad_normed * gain_vec[None, :]
    row_inner = jnp.mean(scaled * normed, axis=1, keepdims=True)
    return (factor * (scaled - normed * row_inner), jnp.sum(grad_normed * normed, axis=0))


def rope_tables(positions, width):
    half_width = width // 2
    frequency = jnp.power(ROPE_BASE, -2.0 * jnp.arange(half_width, dtype=F32) / width)
    angles = positions.astype(F32)[:, None] * frequency[None, :]
    return (jnp.cos(angles), jnp.sin(angles))


def rotate(values, cosine_table, sine_table):
    half_width = values.shape[-1] // 2
    lower_half = values[..., :half_width]
    upper_half = values[..., half_width:]
    return jnp.concatenate(
        [
            lower_half * cosine_table - upper_half * sine_table,
            upper_half * cosine_table + lower_half * sine_table,
        ],
        axis=-1,
    )


def unrotate(values, cosine_table, sine_table):
    return rotate(values, cosine_table, -sine_table)


def segment_info(length_row, places):
    seq_ends = jnp.cumsum(length_row)
    starts = seq_ends - length_row
    segment = jnp.sum((places[:, None] >= seq_ends[None, :]).astype(jnp.int32), axis=1)
    slot_ids = jnp.arange(length_row.shape[0], dtype=jnp.int32)
    offset = jnp.sum(jnp.where(segment[:, None] == slot_ids[None, :], starts[None, :], 0), axis=1)
    return (segment, places - offset)


class PlainTopo:
    def __init__(self):
        self.dp = lax.axis_size("dp")
        self.square = self.dp // LINE
        self.me = lax.axis_index("dp")
        self.core = lax.axis_index("tensor")
        self.line_at = self.me // self.square
        self.square_at = self.me % self.square
        line_bits = [self.square << i for i in range(LINE.bit_length() - 1)]
        square_bits = [1 << i for i in range(self.square.bit_length() - 1)]
        self.line = (line_bits, line_bits[::-1])
        self.squares = (square_bits, square_bits[::-1])

    def swap(self, array, bits, phase):
        perm = []
        for place in range(self.dp):
            for core in range(2):
                perm.append((place * 2 + core, (place ^ bits[core][phase]) * 2 + core))
        return lax.ppermute(array, ("dp", "tensor"), perm)

    def other_core(self, array):
        return lax.ppermute(array, "tensor", [(0, 1), (1, 0)])

    def offset(self, bits, index, unit):
        totals = [0, 0]
        for core in range(2):
            for phase, bit in enumerate(bits[core]):
                if index >> phase & 1:
                    totals[core] ^= bit // unit
        return jnp.where(self.core == 0, totals[0], totals[1])

    def gather(self, own, bits):
        pieces = [own]
        for phase in range(len(bits[0])):
            pieces = pieces + [self.swap(piece, bits, phase) for piece in pieces]
        return pieces

    def gather_joined(self, own, bits):
        joined = own
        for phase in range(len(bits[0])):
            joined = jnp.concatenate([joined, self.swap(joined, bits, phase)], axis=0)
        return joined

    def scatter_sum(self, array, bits):
        for phase in reversed(range(len(bits[0]))):
            half = array.shape[0] // 2
            got = self.swap(array[half:], bits, phase)
            array = (array[:half].astype(F32) + got.astype(F32)).astype(BF)
        return array

    def total(self, array):
        for bits in (self.line, self.squares):
            for phase in range(len(bits[0])):
                array = array + self.swap(array, bits, phase)
        return array

    def exchange(self, chunks, bits):
        rows = chunks[0].shape[0]
        held = [chunk for chunk in chunks]
        for phase in range(len(bits[0])):
            step = 1 << phase
            keep = [i for i in range(len(chunks)) if not i & step]
            keep = [i for i in keep if held[i] is not None]
            sent = jnp.concatenate([held[i + step] for i in keep], axis=0)
            got = self.swap(sent, bits, phase)
            parts = jnp.split(got, len(keep), axis=0)
            for i, part in zip(keep, parts):
                held[i] = jnp.concatenate([held[i], part], axis=0)
                held[i + step] = None
        return jnp.split(held[0], len(chunks), axis=0)

    def ordered(self, pieces, bits, unit, at):
        count = len(pieces)
        tables = []
        for core in range(2):
            table = [0] * count
            for index in range(count):
                total = 0
                for phase, bit in enumerate(bits[core]):
                    if index >> phase & 1:
                        total ^= bit // unit
                table[total] = index
            tables.append(table)
        tables = jnp.asarray(tables, jnp.int32)[self.core]
        stacked = jnp.stack(pieces)
        return [
            lax.dynamic_index_in_dim(
                stacked, lax.dynamic_index_in_dim(tables, place ^ at, 0, False), 0, False
            )
            for place in range(count)
        ]


def to_inner(rows, topo):
    count, width = rows.shape
    rest = width // topo.dp
    cut = rows.reshape(count, LINE, topo.square, rest).transpose(2, 0, 1, 3)
    cut = cut.reshape(topo.square, count, LINE * rest)
    return jnp.concatenate(
        [
            lax.dynamic_index_in_dim(cut, topo.square_at ^ i, 0, False)
            for i in range(topo.square)
        ],
        axis=1,
    )


def to_outer(rows, topo):
    count, width = rows.shape
    rest = width // topo.dp
    cut = rows.reshape(count, topo.square, LINE * rest).transpose(1, 0, 2)
    cut = jnp.stack(
        [
            lax.dynamic_index_in_dim(cut, topo.square_at ^ i, 0, False)
            for i in range(topo.square)
        ]
    )
    cut = cut.reshape(topo.square, count, LINE, rest).transpose(1, 2, 0, 3)
    return cut.reshape(count, width)


def dot(left, right):
    return jnp.dot(left, right, preferred_element_type=F32)


def dot_t(left, right):
    return lax.dot_general(left, right, (((1,), (1,)), ((), ())), preferred_element_type=F32)


def t_dot(left, right):
    return lax.dot_general(left, right, (((0,), (0,)), ((), ())), preferred_element_type=F32)


def attention_scores(queries, key_rows, allowed):
    score_scale = 1.0 / math.sqrt(queries.shape[-1])
    raw_scores = jnp.einsum("qgpd,kgd->gpqk", queries, key_rows, preferred_element_type=F32)
    return jnp.where(allowed[None, None], raw_scores * score_scale, MASKED)


def plain_device(
    tokens,
    out_grad,
    lengths,
    attn_gain,
    q_weight,
    q_bias,
    k_weight,
    k_bias,
    v_weight,
    v_bias,
    o_weight,
    mlp_gain,
    gate_weight,
    up_weight,
    down_weight,
):
    topo = PlainTopo()
    local_rows, width = tokens.shape
    group_rows = 2 * local_rows
    q_cols = q_weight.shape[1]
    kv_cols = k_weight.shape[1]
    qkv_cols = q_cols + 2 * kv_cols
    ff_cols = gate_weight.shape[1]
    part = -(-ff_cols // (LINE * LANES)) * LANES
    kv_groups = kv_cols // HEAD_DIM
    per_group = q_cols // HEAD_DIM // kv_groups
    score_scale = 1.0 / math.sqrt(HEAD_DIM)

    def line_gather(shard):
        pieces = jnp.split(topo.gather_joined(shard, topo.line), LINE, axis=0)
        return jnp.concatenate(topo.ordered(pieces, topo.line, topo.square, topo.line_at), axis=0)

    def square_gather(shard):
        pieces = topo.gather(shard, topo.squares)
        return jnp.concatenate(topo.ordered(pieces, topo.squares, 1, 0), axis=0)

    def square_scatter(grads):
        pieces = jnp.split(grads.astype(BF), topo.square, axis=0)
        by_index = topo.ordered(pieces, tuple(b for b in topo.squares), 1, 0)
        return topo.scatter_sum(jnp.concatenate(by_index, axis=0), topo.squares)

    def line_offset(index):
        return topo.line_at ^ topo.offset(topo.line, index, topo.square)

    def columns_in(shards):
        padded = [jnp.pad(s, ((0, 0), (0, LINE * part - ff_cols))) for s in shards]
        chunks = []
        for index in range(LINE):
            start = line_offset(index) * part
            chunks.append(
                jnp.concatenate(
                    [lax.dynamic_slice_in_dim(s, start, part, axis=1) for s in padded], axis=1
                )
            )
        got = topo.exchange(chunks, topo.line)
        return jnp.concatenate(topo.ordered(got, topo.line, topo.square, topo.line_at), axis=0)

    def columns_out(piece, count):
        rows = piece.shape[0] // LINE
        chunks = [
            lax.dynamic_slice_in_dim(piece, line_offset(index) * rows, rows, axis=0)
            for index in range(LINE)
        ]
        got = topo.ordered(
            topo.exchange(chunks, topo.line), topo.line, topo.square, topo.line_at
        )
        return [
            jnp.concatenate([g[:, i * part : (i + 1) * part] for g in got], axis=1)[
                :, :ff_cols
            ].astype(F32)
            for i in range(count)
        ]

    def rows_out(piece):
        rows = piece.shape[0] // LINE
        chunks = [
            lax.dynamic_slice_in_dim(piece, line_offset(index) * rows, rows, axis=0)
            for index in range(LINE)
        ]
        return topo.scatter_sum(jnp.concatenate(chunks, axis=0), topo.line).astype(F32)

    def both_cores(rows):
        return jnp.concatenate([rows, topo.other_core(rows)], axis=0)

    def core_sum(rows):
        half = rows.shape[0] // 2
        return rows[:half] + topo.other_core(rows[half:].astype(BF)).astype(F32)

    def line_tokens(rows):
        return both_cores(topo.gather_joined(rows, topo.line))

    def line_sum(partial):
        return topo.scatter_sum(core_sum(partial).astype(BF), topo.line).astype(F32)

    row_ids = jnp.arange(local_rows, dtype=jnp.int32)
    places = jnp.concatenate(
        [topo.core * local_rows + row_ids, (1 - topo.core) * local_rows + row_ids]
    )
    segment, positions = segment_info(lengths[0], places)
    allowed = (segment[:, None] == segment[None, :]) & (places[None, :] <= places[:, None])
    cosine_table, sine_table = rope_tables(positions, HEAD_DIM)
    q_cosine = cosine_table[:, None, None, :]
    q_sine = sine_table[:, None, None, :]
    k_cosine = cosine_table[:, None, :]
    k_sine = sine_table[:, None, :]

    inputs_low = to_inner(tokens, topo)
    out_grad_low = to_inner(out_grad, topo)
    gains = to_inner(jnp.stack([attn_gain, mlp_gain]), topo).astype(F32)
    gain_one, gain_two = gains[0], gains[1]
    inputs = inputs_low.astype(F32)
    bias_all = jnp.concatenate([q_bias, k_bias, v_bias]).astype(F32)

    qkv_local = jnp.concatenate([q_weight, k_weight, v_weight], axis=1)
    qkv_all = square_gather(line_gather(qkv_local))
    o_all = square_gather(line_gather(o_weight))
    down_all = square_gather(columns_in([down_weight]))
    grad_out_all = line_tokens(out_grad_low)
    gate_up = square_gather(columns_in([gate_weight, up_weight]))

    normed_one, factor_one = normalize(inputs)
    attn_in = both_cores((normed_one * gain_one[None, :]).astype(BF))
    linear = dot(attn_in, qkv_all) + bias_all[None, :]
    queries = rotate(
        linear[:, :q_cols].reshape(group_rows, kv_groups, per_group, HEAD_DIM), q_cosine, q_sine
    ).astype(BF)
    key_rows = rotate(
        linear[:, q_cols : q_cols + kv_cols].reshape(group_rows, kv_groups, HEAD_DIM),
        k_cosine,
        k_sine,
    ).astype(BF)
    values = linear[:, q_cols + kv_cols :].reshape(group_rows, kv_groups, HEAD_DIM).astype(BF)
    scores = attention_scores(queries, key_rows, allowed)
    row_peak = jnp.max(scores, axis=-1, keepdims=True)
    exponent = jnp.exp(scores - row_peak)
    row_mass = jnp.sum(exponent, axis=-1, keepdims=True)
    log_mass = row_peak + jnp.log(row_mass)
    probs_low = (exponent / row_mass).astype(BF)
    mixed_heads = jnp.einsum("gpqk,kgd->qgpd", probs_low, values, preferred_element_type=F32)
    mixed_heads = mixed_heads.reshape(group_rows, q_cols).astype(BF)
    hidden_state = inputs + core_sum(dot_t(mixed_heads, o_all))
    normed_two, factor_two = normalize(hidden_state)

    mlp_in = line_tokens((normed_two * gain_two[None, :]).astype(BF))
    grad_hidden = dot(grad_out_all, down_all)
    gate_up_out = dot(mlp_in, gate_up)
    gate_val = gate_up_out[:, :part]
    up_val = gate_up_out[:, part:]
    sigmoid_gate = jax.nn.sigmoid(gate_val)
    activated = gate_val * sigmoid_gate
    hidden_units = (activated * up_val).astype(BF)
    grad_gate = (
        grad_hidden * up_val * sigmoid_gate * (1.0 + gate_val * (1.0 - sigmoid_gate))
    ).astype(BF)
    grad_up = (grad_hidden * activated).astype(BF)
    grad_gate_up = jnp.concatenate([grad_gate, grad_up], axis=1)
    grad_normed_two = line_sum(dot_t(grad_gate_up, gate_up))
    block_out = (hidden_state + line_sum(dot_t(hidden_units, down_all))).astype(BF)
    gate_grads, up_grads = columns_out(square_scatter(t_dot(mlp_in, grad_gate_up)), 2)
    (down_grads,) = columns_out(square_scatter(t_dot(grad_out_all, hidden_units)), 1)

    back_two, gain_two_grad = plain_norm_back(grad_normed_two, normed_two, factor_two, gain_two)
    grad_state = out_grad_low.astype(F32) + back_two
    grad_state_all = both_cores(grad_state.astype(BF))
    o_grads = rows_out(square_scatter(t_dot(grad_state_all, mixed_heads)))
    grad_mixed = dot(grad_state_all, o_all)
    grad_heads = grad_mixed.astype(BF).reshape(group_rows, kv_groups, per_group, HEAD_DIM)
    scores_again = attention_scores(queries, key_rows, allowed)
    prob_rows = jnp.exp(scores_again - log_mass)
    grad_probs = jnp.einsum("qgpd,kgd->gpqk", grad_heads, values, preferred_element_type=F32)
    row_inner = jnp.sum(prob_rows * grad_probs, axis=-1, keepdims=True)
    grad_scores = (prob_rows * (grad_probs - row_inner) * score_scale).astype(BF)
    grad_values = jnp.einsum(
        "gpqk,qgpd->kgd", prob_rows.astype(BF), grad_heads, preferred_element_type=F32
    )
    grad_queries = jnp.einsum("gpqk,kgd->qgpd", grad_scores, key_rows, preferred_element_type=F32)
    grad_keys = jnp.einsum("gpqk,qgpd->kgd", grad_scores, queries, preferred_element_type=F32)
    grad_linear = jnp.concatenate(
        [
            unrotate(grad_queries, q_cosine, q_sine).reshape(group_rows, q_cols),
            unrotate(grad_keys, k_cosine, k_sine).reshape(group_rows, kv_cols),
            grad_values.reshape(group_rows, kv_cols),
        ],
        axis=1,
    ).astype(BF)
    bias_grad = jnp.sum(grad_linear.astype(F32), axis=0)
    qkv_grads = rows_out(square_scatter(t_dot(attn_in, grad_linear)))
    grad_normed_one = core_sum(dot_t(grad_linear, qkv_all))
    back_one, gain_one_grad = plain_norm_back(grad_normed_one, normed_one, factor_one, gain_one)
    tokens_grad = (grad_state + back_one).astype(BF)
    gain_grads = to_outer(jnp.stack([gain_one_grad, gain_two_grad]), topo)
    gain_grads = gain_grads + topo.other_core(gain_grads)
    small = topo.total(jnp.concatenate([bias_grad, gain_grads.reshape(-1)]).reshape(-1, LANES))
    small = small.reshape(-1)
    own_bias = small[:qkv_cols]
    gain_sum = small[qkv_cols:].reshape(2, width)
    return (
        to_outer(block_out, topo),
        to_outer(tokens_grad, topo),
        gain_sum[0],
        qkv_grads[:, :q_cols],
        own_bias[:q_cols],
        qkv_grads[:, q_cols : q_cols + kv_cols],
        own_bias[q_cols : q_cols + kv_cols],
        qkv_grads[:, q_cols + kv_cols : qkv_cols],
        own_bias[q_cols + kv_cols :],
        o_grads,
        gain_sum[1],
        gate_grads,
        up_grads,
        down_grads,
    )


def nn(left, right):
    return jnp.dot(left, right, preferred_element_type=F32)


def nt(left, right):
    return lax.dot_general(left, right, (((1,), (1,)), ((), ())), preferred_element_type=F32)


def tn(left, right):
    return lax.dot_general(left, right, (((0,), (0,)), ((), ())), preferred_element_type=F32)


def shape(dims, kind):
    return jax.ShapeDtypeStruct(dims, kind)


def whole(dims):
    return pl.BlockSpec(dims, lambda *_: (0,) * len(dims))


OFF, NEIGHBOUR, INDEX, AT, OTHER = 0, 4, 8, 12, 13


class Topo:
    def __init__(self):
        self.dp = lax.axis_size("dp")
        me = lax.axis_index("dp")
        core = lax.axis_index("tensor")
        line_at, square_at = me >> 2, me & 3

        def by_core(index):
            return jnp.where(core == 0, index, (index >> 1) | ((index & 1) << 1))

        self.core = core
        self.square_at = square_at
        self.line = ((LINE, 2 * LINE), (2 * LINE, LINE))
        self.square = ((1, 2), (2, 1))
        count = jnp.arange(LINE, dtype=jnp.int32)
        self.info = jnp.concatenate(
            [
                by_core(count),
                line_at ^ by_core(count),
                by_core(line_at ^ count),
                jnp.stack([square_at, 1 - core]),
            ]
        ).astype(jnp.int32)

    def swap(self, array, bits, phase):
        perm = []
        for place in range(self.dp):
            for core in range(2):
                perm.append((place * 2 + core, (place ^ bits[core][phase]) * 2 + core))
        return lax.ppermute(array, ("dp", "tensor"), perm)

    def other_core(self, array):
        return lax.ppermute(array, "tensor", [(0, 1), (1, 0)])

    def both_ways(self, array):
        return lax.all_to_all(array, "tensor", 0, 0, tiled=True)


CLOCK = [None]
TOKEN = jax.ShapeDtypeStruct((8, 128), F32)
IN_VMEM = pl.BlockSpec(memory_space=pltpu.VMEM)
IN_SMEM = pl.BlockSpec(memory_space=pltpu.SMEM)


def in_order(body, ins, outs):
    taken = 0 if CLOCK[0] is None else 1

    def full(*refs):
        body(*refs[:ins], *refs[ins + taken : ins + taken + outs], *refs[ins + taken + outs + 1 :])

    return full


def run(kernel, single, args):
    taken = [] if CLOCK[0] is None else [CLOCK[0]]
    *out, CLOCK[0] = kernel(*args, *taken)
    return out[0] if single else out


def as_list(value):
    return list(value) if isinstance(value, (list, tuple)) else [value]


def call(body, grid, in_specs, out_specs, out_shape, scratch, info, *args, mib=32):
    outs = as_list(out_shape)
    late = 0 if CLOCK[0] is None else 1
    kernel = pl.pallas_call(
        in_order(body, 1 + len(in_specs), len(outs)),
        grid_spec=pltpu.PrefetchScalarGridSpec(
            num_scalar_prefetch=1,
            grid=grid,
            in_specs=list(in_specs) + [IN_VMEM] * late,
            out_specs=as_list(out_specs) + [IN_VMEM],
            scratch_shapes=list(scratch),
        ),
        out_shape=outs + [TOKEN],
        compiler_params=pltpu.CompilerParams(vmem_limit_bytes=mib * 2**20),
        cost_estimate=pl.CostEstimate(flops=1000, bytes_accessed=1000, transcendentals=0),
        name=body.__qualname__.split(".")[0],
    )
    return run(kernel, not isinstance(out_shape, (list, tuple)), (info,) + args)


def small(body, out_shape, scratch, info, *args, mib=16):
    outs = as_list(out_shape)
    late = 0 if CLOCK[0] is None else 1
    kernel = pl.pallas_call(
        in_order(body, 1 + len(args), len(outs)),
        in_specs=[IN_SMEM] + [IN_VMEM] * (len(args) + late),
        out_specs=[IN_VMEM] * (len(outs) + 1),
        scratch_shapes=list(scratch),
        out_shape=outs + [TOKEN],
        compiler_params=pltpu.CompilerParams(vmem_limit_bytes=mib * 2**20),
        cost_estimate=pl.CostEstimate(flops=1000, bytes_accessed=1000, transcendentals=0),
        name=body.__qualname__.split(".")[0],
    )
    return run(kernel, not isinstance(out_shape, (list, tuple)), (info,) + args)


def tie(info, array):
    def body(info_ref, in_ref, out_ref):
        out_ref[...] = in_ref[...]

    return small(body, shape(array.shape, array.dtype), [], info, array)


def join(info, *args):
    def body(info_ref, *refs):
        start = 0
        for ref in refs[:-1]:
            refs[-1][start : start + ref.shape[0]] = ref[...]
            start += ref.shape[0]

    rows = sum(a.shape[0] for a in args)
    return small(body, shape((rows,) + args[0].shape[1:], args[0].dtype), [], info, *args)


def beside(info, *args):
    def body(info_ref, *refs):
        start = 0
        for ref in refs[:-1]:
            refs[-1][:, start : start + ref.shape[1]] = ref[...]
            start += ref.shape[1]

    cols = sum(a.shape[1] for a in args)
    return small(body, shape((args[0].shape[0], cols), args[0].dtype), [], info, *args)


def placed(info, rows, takes, *args):
    def body(info_ref, *refs):
        for index, (which, start) in enumerate(takes):
            target = pl.multiple_of(info_ref[NEIGHBOUR + index] * rows, 16)
            refs[-1][pl.ds(target, rows)] = refs[which][start : start + rows]

    return small(body, shape((LINE * rows, args[0].shape[1]), BF), [], info, *args)


def second_chunks(info, kept, got):
    rows = kept.shape[0] // 2

    def body(info_ref, kept_ref, got_ref, out_ref):
        out_ref[:rows] = kept_ref[rows:]
        out_ref[rows:] = got_ref[rows:]

    return small(body, shape(kept.shape, BF), [], info, kept, got)


def cut_columns(info, part, *weights):
    count = len(weights)
    rows, cols = weights[0].shape
    short = cols - (LINE - 1) * part

    def body(info_ref, *refs):
        ins, outs = refs[:count], refs[count:]
        for index in range(LINE):
            at = info_ref[NEIGHBOUR + index]
            out = outs[1 - index % 2]
            low = index // 2 * rows
            for which, ref in enumerate(ins):
                start = pl.multiple_of(at * part, LANES)
                first = which * part
                out[low : low + rows, first : first + short] = ref[:, pl.ds(start, short)]
                if short < part:
                    rest = pl.multiple_of(jnp.minimum(at, LINE - 2) * part + short, LANES)
                    tail = ref[:, pl.ds(rest, part - short)]
                    out[low : low + rows, first + short : first + part] = jnp.where(
                        at < LINE - 1, tail, jnp.zeros_like(tail)
                    )

    return small(body, [shape((2 * rows, count * part), BF)] * 2, [], info, *weights)


def piece_copies(info_ref, pieces, target, sems, cols=None, first_col=0):
    rows = target.shape[0] // LINE
    low, high = cols or (0, pieces[0].shape[1])
    index = 0
    for piece in pieces:
        for block in range(piece.shape[0] // rows):
            start = pl.multiple_of(info_ref[OFF + index] * rows, rows)
            yield pltpu.make_async_copy(
                piece.at[pl.ds(block * rows, rows), pl.ds(low, high - low)],
                target.at[pl.ds(start, rows), pl.ds(first_col + low, high - low)],
                sems.at[index],
            )
            index += 1


def square_blocks(info_ref, pieces, width):
    rows = width // LINE
    index = 0
    for piece in pieces:
        for block in range(piece.shape[0] // rows):
            start = pl.multiple_of(info_ref[OFF + index] * rows, LANES)
            yield pl.ds(start, rows), piece[block * rows : (block + 1) * rows]
            index += 1


def inward(values, at, store):
    width = values.shape[1]
    block = width // LINE
    rest = block // LINE
    for square in range(LINE):
        parts = [
            values[:, line * block + square * rest : line * block + (square + 1) * rest]
            for line in range(LINE)
        ]
        start = pl.multiple_of((square ^ at) * block, LANES)
        store(pl.ds(start, block), jnp.concatenate(parts, axis=1))


def outward(ref, at):
    width = ref.shape[1]
    block = width // LINE
    rest = block // LINE
    blocks = []
    for square in range(LINE):
        start = pl.multiple_of((square ^ at) * block, LANES)
        blocks.append(ref[:, pl.ds(start, block)])
    parts = []
    for line in range(LINE):
        for square in range(LINE):
            parts.append(blocks[square][:, line * rest : (line + 1) * rest])
    return jnp.concatenate(parts, axis=1)


def turn_rows(info, rows):
    def body(info_ref, rows_ref, out_ref, held):
        def store(cols, block):
            held[:, cols] = block

        inward(rows_ref[...].astype(F32), info_ref[AT], store)
        out_ref[...] = held[...].astype(BF)

    return small(body, shape(rows.shape, BF), [pltpu.VMEM(rows.shape, F32)], info, rows)


def open_rows(info, rows, gains):
    def body(info_ref, rows_ref, gains_ref, out_ref, in_ref, gain_ref, held):
        def store_gain(cols, block):
            gain_ref[:, cols] = block

        def store(cols, block):
            held[:, cols] = block

        inward(gains_ref[...], info_ref[AT], store_gain)
        inward(rows_ref[...].astype(F32), info_ref[AT], store)
        values = held[...]
        in_ref[...] = values.astype(BF)
        factor = lax.rsqrt(jnp.mean(values * values, axis=1, keepdims=True) + EPSILON)
        out_ref[...] = (values * factor * gain_ref[0:1, :]).astype(BF)

    return small(
        body,
        [shape(rows.shape, BF), shape(rows.shape, BF), shape(gains.shape, F32)],
        [pltpu.VMEM(rows.shape, F32)],
        info,
        rows,
        gains,
    )


def state_rows(info, rows, own, got, gain):
    def body(info_ref, rows_ref, own_ref, got_ref, gain_ref, out_ref, state_ref):
        start = pl.multiple_of(info_ref[OTHER] * dims[0], 16)
        got = got_ref[pl.ds(start, dims[0])] if got_ref.shape[0] > dims[0] else got_ref[...]
        values = rows_ref[...].astype(F32) + (own_ref[...] + got.astype(F32))
        state_ref[...] = values
        factor = lax.rsqrt(jnp.mean(values * values, axis=1, keepdims=True) + EPSILON)
        out_ref[...] = (values * factor * gain_ref[...]).astype(BF)

    dims = rows.shape
    return small(
        body,
        [shape(dims, BF), shape(dims, F32)],
        [],
        info,
        rows,
        own,
        got,
        gain,
    )


def close_rows(info, state, own, got):
    def body(info_ref, state_ref, own_ref, got_ref, out_ref, held):
        held[...] = state_ref[...] + (own_ref[...].astype(F32) + got_ref[...].astype(F32))
        out_ref[...] = outward(held, info_ref[AT]).astype(BF)

    dims = state.shape
    return small(
        body,
        shape(dims, BF),
        [pltpu.VMEM(dims, F32)],
        info,
        state,
        own,
        got,
    )


def norm_back(info, values, own, got, base, gain, turn):
    def body(info_ref, values_ref, own_ref, got_ref, base_ref, gain_ref, *refs):
        values = values_ref[...].astype(F32)
        factor = lax.rsqrt(jnp.mean(values * values, axis=1, keepdims=True) + EPSILON)
        normed = values * factor
        grad = own_ref[...].astype(F32) + got_ref[...].astype(F32)
        scaled = grad * gain_ref[...]
        row_inner = jnp.mean(scaled * normed, axis=1, keepdims=True)
        total = base_ref[...].astype(F32) + factor * (scaled - normed * row_inner)
        gain_grad = jnp.sum(grad * normed, axis=0, keepdims=True)
        if turn:
            out_ref, gain_out_ref, held, gain_held = refs
            held[...] = total
            out_ref[...] = outward(held, info_ref[AT]).astype(BF)
        else:
            low_ref, out_ref, gain_out_ref, gain_held = refs
            out_ref[...] = total
            low_ref[...] = total.astype(BF)
        gain_held[...] = gain_grad
        gain_out_ref[...] = outward(gain_held, info_ref[AT])

    dims = values.shape
    kinds = (BF,) if turn else (BF, F32)
    return small(
        body,
        [shape(dims, kind) for kind in kinds] + [shape(gain.shape, F32)],
        ([pltpu.VMEM(dims, F32)] if turn else []) + [pltpu.VMEM(gain.shape, F32)],
        info,
        values,
        own,
        got,
        base,
        gain,
    )


def turned(values, cosine, sine):
    return values * cosine + pltpu.roll(values, HEAD_DIM // 2, 1) * sine


def attend(info, rows, pieces, bias, cosine, sine, row_info, col_info, q_heads, kv_heads):
    count, cols = len(pieces), pieces[0].shape[1]
    group, width = rows.shape
    q_cols = q_heads * HEAD_DIM

    def body(info_ref, in_ref, *refs):
        pieces = refs[:count]
        bias_ref, cos_ref, sin_ref, row_ref, col_ref = refs[count : count + 5]
        mixed_ref, lin_ref, mass_ref = refs[count + 5 :]
        cosine, sine = cos_ref[...], sin_ref[...]
        scale = 1.0 / math.sqrt(HEAD_DIM)
        linear = bias_ref[...]
        for cols, piece in square_blocks(info_ref, pieces, width):
            linear = linear + nn(in_ref[:, cols], piece)
        for head in range(q_heads + 2 * kv_heads):
            cols = slice(head * HEAD_DIM, (head + 1) * HEAD_DIM)
            part = linear[:, cols]
            if head < q_heads + kv_heads:
                part = turned(part, cosine, sine)
            lin_ref[:, cols] = part.astype(BF)
        allowed = (row_ref[:, 0:1] <= col_ref[...]) & (col_ref[...] <= row_ref[:, 1:2])
        for head in range(q_heads):
            key = q_heads + head // (q_heads // kv_heads)
            value = key + kv_heads
            cols = slice(head * HEAD_DIM, (head + 1) * HEAD_DIM)
            raw = nt(lin_ref[:, cols], lin_ref[:, key * HEAD_DIM : (key + 1) * HEAD_DIM])
            scores = jnp.where(allowed, raw * scale, MASKED)
            peak = jnp.max(scores, axis=1, keepdims=True)
            exponent = jnp.exp(scores - peak)
            mass = jnp.sum(exponent, axis=1, keepdims=True)
            mass_ref[:, head : head + 1] = peak + jnp.log(mass)
            probs = (exponent * (1.0 / mass)).astype(BF)
            mixed_ref[:, cols] = nn(
                probs, lin_ref[:, value * HEAD_DIM : (value + 1) * HEAD_DIM]
            ).astype(BF)

    plain = (bias, cosine, sine, row_info, col_info)
    return small(
        body,
        [shape((group, q_cols), BF), shape((group, cols), BF), shape((group, LANES), F32)],
        [],
        info,
        rows,
        *pieces,
        *plain,
    )


def project(info, rows, pieces, width):
    count, cols = len(pieces), pieces[0].shape[1]
    half = rows.shape[0] // 2

    def body(info_ref, in_ref, *refs):
        pieces = refs[:count]
        other_ref, own_ref = refs[count:]
        for cols, piece in square_blocks(info_ref, pieces, width):
            both = nt(in_ref[...], piece)
            own_ref[:, cols] = both[:half]
            other_ref[:, cols] = both[half:].astype(BF)

    return small(
        body,
        [shape((half, width), BF), shape((half, width), F32)],
        [],
        info,
        rows,
        *pieces,
    )


def attend_back(
    info, state, o_pieces, pieces, linear, mass, cosine, sine, row_info, col_info, q_heads, kv_heads
):
    count, cols = len(pieces), pieces[0].shape[1]
    group, width = state.shape
    q_cols = q_heads * HEAD_DIM
    half = group // 2

    def body(info_ref, state_ref, *refs):
        o_refs, q_refs = refs[:count], refs[count : 2 * count]
        lin_ref, mass_ref, cos_ref, sin_ref, row_ref, col_ref = refs[2 * count : 2 * count + 6]
        grad_ref, bias_ref, own_ref, other_ref = refs[2 * count + 6 : 2 * count + 10]
        heads_ref = refs[-1]
        cosine, sine = cos_ref[...], -sin_ref[...]
        scale = 1.0 / math.sqrt(HEAD_DIM)
        heads = 0.0
        for cols, piece in square_blocks(info_ref, o_refs, width):
            heads = heads + nn(state_ref[:, cols], piece)
        heads_ref[...] = heads.astype(BF)
        allowed = (row_ref[:, 0:1] <= col_ref[...]) & (col_ref[...] <= row_ref[:, 1:2])
        per_group = q_heads // kv_heads
        for place in range(kv_heads):
            key_cols = slice((q_heads + place) * HEAD_DIM, (q_heads + place + 1) * HEAD_DIM)
            first = q_heads + kv_heads + place
            value_cols = slice(first * HEAD_DIM, (first + 1) * HEAD_DIM)
            keys, values = lin_ref[:, key_cols], lin_ref[:, value_cols]
            grad_keys, grad_values = 0.0, 0.0
            for head in range(place * per_group, (place + 1) * per_group):
                cols = slice(head * HEAD_DIM, (head + 1) * HEAD_DIM)
                queries, grads = lin_ref[:, cols], heads_ref[:, cols]
                scores = jnp.where(allowed, nt(queries, keys) * scale, MASKED)
                probs = jnp.exp(scores - mass_ref[:, head : head + 1])
                grad_probs = nt(grads, values)
                inner = jnp.sum(probs * grad_probs, axis=1, keepdims=True)
                grad_scores = (probs * (grad_probs - inner) * scale).astype(BF)
                grad_values += tn(probs.astype(BF), grads)
                grad_keys += tn(grad_scores, queries)
                grad_ref[:, cols] = turned(nn(grad_scores, keys), cosine, sine).astype(BF)
            grad_ref[:, key_cols] = turned(grad_keys, cosine, sine).astype(BF)
            grad_ref[:, value_cols] = grad_values.astype(BF)
        bias_ref[...] = jnp.sum(grad_ref[...].astype(F32), axis=0, keepdims=True)
        for cols, piece in square_blocks(info_ref, q_refs, width):
            both = nt(grad_ref[...], piece)
            own_ref[:, cols] = both[:half]
            other_ref[:, cols] = both[half:].astype(BF)

    plain = (linear, mass, cosine, sine, row_info, col_info)
    return small(
        body,
        [
            shape((group, cols), BF),
            shape((1, cols), F32),
            shape((half, width), F32),
            shape((half, width), BF),
        ],
        [pltpu.VMEM((group, q_cols), BF)],
        info,
        state,
        *o_pieces,
        *pieces,
        *plain,
    )


def forward(info, x, gate_up, tile, step=256):
    count, part = len(gate_up), gate_up[0].shape[1] // 2
    total, width = x.shape
    spans = [(low, min(low + step, part)) for low in range(0, part, step)]

    def body(info_ref, x_ref, *refs):
        pieces = refs[:count]
        hid_ref, gate_ref, up_ref, weight, sems = refs[count:]

        def span_copies(index):
            low, high = spans[index]
            yield from piece_copies(info_ref, pieces, weight, sems.at[2 * index], (low, high))
            yield from piece_copies(
                info_ref, pieces, weight, sems.at[2 * index + 1], (part + low, part + high)
            )

        opening = pl.program_id(0) == 0

        @pl.when(opening)
        def _():
            for index in range(len(spans)):
                for copy in span_copies(index):
                    copy.start()

        x = x_ref[...]
        for index, (low, high) in enumerate(spans):

            @pl.when(opening)
            def _(index=index):
                for copy in span_copies(index):
                    copy.wait()

            gate = nn(x, weight[:, low:high])
            up = nn(x, weight[:, part + low : part + high])
            share = 1.0 / (1.0 + jnp.exp(-gate))
            active = gate * share
            hid_ref[:, low:high] = (active * up).astype(BF)
            gate_ref[:, low:high] = (up * share * (1.0 + gate * (1.0 - share))).astype(BF)
            up_ref[:, low:high] = active.astype(BF)

    return call(
        body,
        (total // tile,),
        [pl.BlockSpec((tile, width), lambda i, _: (i, 0))] + [ANY] * count,
        [pl.BlockSpec((tile, part), lambda i, _: (i, 0))] * 3,
        [shape((total, part), BF)] * 3,
        [
            pltpu.VMEM((width, 2 * part), BF),
            pltpu.SemaphoreType.DMA((2 * len(spans), LINE)),
        ],
        info,
        x,
        *gate_up,
    )


def halves_spec(tile, width, steps, spread):
    half = steps // 2

    def later(i, info_ref):
        first = info_ref[OTHER] * half if spread else 0
        return (first + jnp.maximum(i - half, 0), 0)

    return [
        pl.BlockSpec((tile, width), lambda i, _: (jnp.minimum(i, half - 1), 0)),
        pl.BlockSpec((tile, width), later),
    ]


def store_half(value, steps, first_ref, second_ref):
    early = pl.program_id(0) < steps // 2

    @pl.when(early)
    def _():
        first_ref[...] = value

    @pl.when(jnp.logical_not(early))
    def _():
        second_ref[...] = value


def down_sum(info, hidden, down, tile, width):
    count = len(down)
    total, part = hidden.shape
    steps = total // tile

    def body(info_ref, hid_ref, *refs):
        pieces = refs[:count]
        own_ref, other_ref, weight, sems = refs[count:]

        @pl.when(pl.program_id(0) == 0)
        def _():
            copies = list(piece_copies(info_ref, pieces, weight, sems))
            for copy in copies:
                copy.start()
            for copy in copies:
                copy.wait()

        value = nt(hid_ref[...], weight[...]).astype(BF)
        store_half(value, steps, own_ref, other_ref)

    return call(
        body,
        (steps,),
        [pl.BlockSpec((tile, part), lambda i, _: (i, 0))] + [ANY] * count,
        halves_spec(tile, width, steps, False),
        [shape((total // 2, width), BF)] * 2,
        [pltpu.VMEM((width, part), BF), pltpu.SemaphoreType.DMA((LINE,))],
        info,
        hidden,
        *down,
    )


def backward(info, g, gate_factor, up_factor, gate_up, down, tile, step=256):
    count, part = len(down), down[0].shape[1]
    total, width = g.shape
    steps = total // tile
    spans = [(low, min(low + step, part)) for low in range(0, part, step)]

    def body(info_ref, g_ref, gate_ref, up_ref, *refs):
        gate_up, down = refs[:count], refs[count : 2 * count]
        grad_ref, own_ref, other_ref, weight, sems = refs[2 * count :]

        def span_copies(index):
            yield from piece_copies(info_ref, down, weight, sems.at[index], spans[index], 2 * part)

        def late_copies():
            yield from piece_copies(info_ref, gate_up, weight, sems.at[len(spans)])

        opening = pl.program_id(0) == 0

        @pl.when(opening)
        def _():
            for index in range(len(spans)):
                for copy in span_copies(index):
                    copy.start()
            for copy in late_copies():
                copy.start()

        g = g_ref[...]
        for index, (low, high) in enumerate(spans):

            @pl.when(opening)
            def _(index=index):
                for copy in span_copies(index):
                    copy.wait()

            grad = nn(g, weight[:, 2 * part + low : 2 * part + high])
            grad_ref[:, low:high] = (grad * gate_ref[:, low:high].astype(F32)).astype(BF)
            grad_ref[:, part + low : part + high] = (
                grad * up_ref[:, low:high].astype(F32)
            ).astype(BF)

        @pl.when(opening)
        def _():
            for copy in late_copies():
                copy.wait()

        value = nt(grad_ref[...], weight[:, : 2 * part]).astype(BF)
        store_half(value, steps, own_ref, other_ref)

    return call(
        body,
        (steps,),
        [pl.BlockSpec((tile, cols), lambda i, _: (i, 0)) for cols in (width, part, part)]
        + [ANY] * (2 * count),
        [pl.BlockSpec((tile, 2 * part), lambda i, _: (i, 0))] + halves_spec(tile, width, steps, False),
        [shape((total, 2 * part), BF)] + [shape((total // 2, width), BF)] * 2,
        [
            pltpu.VMEM((width, 3 * part), BF),
            pltpu.SemaphoreType.DMA((len(spans) + 1, LINE)),
        ],
        info,
        g,
        gate_factor,
        up_factor,
        *gate_up,
        *down,
    )


def grads_sent(info, left, right, block):
    total, cols = right.shape

    def body(info_ref, left_ref, right_ref, out_ref):
        out_ref[...] = tn(left_ref[...], right_ref[...]).astype(BF)

    return call(
        body,
        (2,),
        [
            pl.BlockSpec((total, block), lambda i, info_ref: (0, info_ref[OFF + 2 + i])),
            whole(right.shape),
        ],
        pl.BlockSpec((block, cols), lambda i, _: (i, 0)),
        shape((2 * block, cols), BF),
        [],
        info,
        left,
        right,
    )


def grads_kept(info, left, right, block, got):
    total, cols = right.shape

    def body(info_ref, left_ref, right_ref, got_ref, keep_ref, send_ref):
        value = (tn(left_ref[...], right_ref[...]) + got_ref[...].astype(F32)).astype(BF)
        store_half(value, 2, keep_ref, send_ref)

    return call(
        body,
        (2,),
        [
            pl.BlockSpec((total, block), lambda i, info_ref: (0, info_ref[OFF + i])),
            whole(right.shape),
            pl.BlockSpec((block, cols), lambda i, _: (i, 0)),
        ],
        [whole((block, cols))] * 2,
        [shape((block, cols), BF)] * 2,
        [],
        info,
        left,
        right,
        got,
    )


def sum_split(info, block, count, keep_at, send_at, left, right):
    cols = left.shape[1]

    def body(info_ref, left_ref, right_ref, *outs):
        for out, (first, stride, along) in zip(outs, (keep_at, send_at)):
            for step in range(count):
                index = first + stride * step
                if along:
                    rows = pl.ds(pl.multiple_of(info_ref[NEIGHBOUR + index] * block, 16), block)
                else:
                    rows = pl.ds(index * block, block)
                total = left_ref[rows].astype(F32) + right_ref[rows].astype(F32)
                out[step * block : (step + 1) * block] = total.astype(BF)

    return small(body, [shape((count * block, cols), BF)] * 2, [], info, left, right)


def sum_out(info, left, right, widths):
    rows = left.shape[0]

    def body(info_ref, left_ref, right_ref, *outs):
        total = left_ref[...].astype(F32) + right_ref[...].astype(F32)
        start = 0
        for out, cols in zip(outs, widths):
            out[...] = total[:, start : start + cols]
            start += cols

    return small(
        body,
        [shape((rows, cols), F32) for cols in widths],
        [],
        info,
        left,
        right,
    )


def columns_out(info, kept, got, last, part, cols):
    rows = kept.shape[0] // 2
    count = kept.shape[1] // part

    def body(info_ref, kept_ref, got_ref, last_ref, *outs):
        pieces = [kept_ref[:rows], got_ref[:rows], last_ref[:rows], last_ref[rows:]]
        for place in range(LINE):
            low = place * part
            span = min(part, cols - low)
            for index, piece in enumerate(pieces):

                @pl.when(info_ref[INDEX + place] == index)
                def _(piece=piece, low=low, span=span):
                    for which, out in enumerate(outs):
                        start = which * part
                        out[:, low : low + span] = piece[:, start : start + span].astype(F32)

    return small(
        body,
        [shape((rows, cols), F32)] * count,
        [],
        info,
        kept,
        got,
        last,
    )


def sequence_info(length_row, places):
    seq_ends = jnp.cumsum(length_row)
    starts = seq_ends - length_row
    inside = (places[:, None] >= starts[None, :]) & (places[:, None] < seq_ends[None, :])
    return jnp.sum(jnp.where(inside, starts[None, :], 0), axis=1)


def per_device(
    tokens,
    out_grad,
    lengths,
    attn_gain,
    q_weight,
    q_bias,
    k_weight,
    k_bias,
    v_weight,
    v_bias,
    o_weight,
    mlp_gain,
    gate_weight,
    up_weight,
    down_weight,
):
    CLOCK[0] = None
    topo = Topo()
    info = topo.info
    line, square = topo.line, topo.square
    local_rows, width = tokens.shape
    shard_rows = q_weight.shape[0]
    block = width // LINE
    q_cols = q_weight.shape[1]
    kv_cols = k_weight.shape[1]
    qkv_cols = q_cols + 2 * kv_cols
    ff_cols = gate_weight.shape[1]
    part = -(-ff_cols // (LINE * LANES)) * LANES
    q_heads, kv_heads = q_cols // HEAD_DIM, kv_cols // HEAD_DIM
    tile = local_rows * LINE // 2

    q_own = beside(info, q_weight, k_weight, v_weight)
    q_one = topo.swap(q_own, line, 0)
    gate_up_send, gate_up_keep = cut_columns(info, part, gate_weight, up_weight)

    q_joined = join(info, q_own, q_one)
    q_two = topo.swap(q_joined, line, 1)
    bias_all = jnp.concatenate([q_bias, k_bias, v_bias]).astype(F32)[None, :]
    gains = jnp.stack([attn_gain, mlp_gain]).astype(F32)
    attn_own, inputs, gains = open_rows(info, tokens, gains)
    gain_one, gain_two = gains[0:1], gains[1:2]
    attn_other = topo.other_core(attn_own)
    out_grad_in = turn_rows(info, out_grad)
    row_ids = jnp.arange(local_rows, dtype=jnp.int32)
    places = jnp.concatenate(
        [topo.core * local_rows + row_ids, (1 - topo.core) * local_rows + row_ids]
    )
    starts = sequence_info(lengths[0], places)
    frequency = jnp.power(ROPE_BASE, -2.0 * jnp.arange(HEAD_DIM // 2, dtype=F32) / HEAD_DIM)
    angles = (places - starts).astype(F32)[:, None] * frequency[None, :]
    cosine_half, sine_half = jnp.cos(angles), jnp.sin(angles)
    cosine = jnp.concatenate([cosine_half, cosine_half], axis=1)
    sine = jnp.concatenate([-sine_half, sine_half], axis=1)
    row_info = jnp.stack([starts, places], axis=1)
    col_info = places[None, :]
    from_line = [(0, 0), (0, shard_rows), (1, 0), (1, shard_rows)]
    from_exchange = [(0, 0), (1, 0), (2, 0), (2, shard_rows)]

    o_own = join(info, o_weight)
    o_one = topo.swap(o_own, line, 0)
    q_piece = placed(info, shard_rows, from_line, q_joined, q_two)
    q_near = topo.swap(q_piece, square, 0)
    gate_up_one = topo.swap(tie(info, gate_up_send), line, 0)
    attn_in = join(info, attn_own, attn_other)
    q_all = [join(info, q_piece, q_near)]
    q_all.append(topo.swap(q_all[0], square, 1))
    o_joined = join(info, o_own, o_one)
    o_two = topo.swap(o_joined, line, 1)
    o_piece = placed(info, shard_rows, from_line, o_joined, o_two)
    o_near = topo.swap(o_piece, square, 0)
    gate_up_two = topo.swap(second_chunks(info, gate_up_keep, gate_up_one), line, 1)
    o_all = [join(info, o_piece, o_near)]
    o_all.append(topo.swap(o_all[0], square, 1))
    down_send, down_keep = cut_columns(info, part, down_weight)
    down_one = topo.swap(down_send, line, 0)

    mixed, linear, mass = attend(
        info, attn_in, q_all, bias_all, cosine, sine, row_info, col_info, q_heads, kv_heads
    )
    gate_up_piece = placed(
        info, shard_rows, from_exchange, gate_up_keep, gate_up_one, gate_up_two
    )
    gate_up_near = topo.swap(gate_up_piece, square, 0)
    down_two = topo.swap(second_chunks(info, down_keep, down_one), line, 1)
    other_attn, own_attn = project(info, mixed, o_all, width)
    other_attn = topo.other_core(other_attn)
    mlp_own, state = state_rows(info, inputs, own_attn, other_attn, gain_two)
    mlp_one = topo.swap(mlp_own, line, 0)
    grad_out_one = topo.swap(tie(info, out_grad_in), line, 0)

    gate_up = [join(info, gate_up_piece, gate_up_near)]
    gate_up.append(topo.swap(gate_up[0], square, 1))
    down_piece = placed(info, shard_rows, from_exchange, down_keep, down_one, down_two)
    down_near = topo.swap(down_piece, square, 0)
    mlp_half = join(info, mlp_own, mlp_one)
    mlp_two = topo.swap(mlp_half, line, 1)
    mlp_early = topo.other_core(mlp_half)
    grad_out_half = join(info, out_grad_in, grad_out_one)
    grad_out_two = topo.swap(grad_out_half, line, 1)
    mlp_late = topo.other_core(mlp_two)
    mlp_in = join(info, mlp_half, mlp_two, mlp_early, mlp_late)
    down = [join(info, down_piece, down_near)]
    down.append(topo.swap(down[0], square, 1))
    grad_out_early = topo.other_core(grad_out_half)

    hidden, gate_factor, up_factor = forward(info, mlp_in, gate_up, tile)
    grad_out_late = topo.other_core(grad_out_two)
    out_own, out_other = down_sum(info, hidden, down, tile, width)
    out_other = topo.other_core(out_other)
    grad_out_all = join(info, grad_out_half, grad_out_two, grad_out_early, grad_out_late)
    pair = (0, 1, False), (2, 1, False)
    rows = local_rows
    out_keep, out_send = sum_split(info, rows, 2, *pair, out_own, out_other)
    out_one = topo.swap(out_send, line, 1)
    down_full = grads_sent(info, grad_out_all, hidden, block)
    down_got = topo.swap(down_full, square, 1)
    grads, back_own, back_other = backward(
        info, grad_out_all, gate_factor, up_factor, gate_up, down, tile
    )
    back_other = topo.other_core(back_other)
    down_kept, down_send = grads_kept(info, grad_out_all, hidden, block, down_got)
    down_last = topo.swap(down_send, square, 0)
    single = (0, 1, False), (1, 1, False)
    out_keep, out_send = sum_split(info, rows, 1, *single, out_keep, out_one)
    out_two = topo.swap(out_send, line, 0)
    back_keep, back_send = sum_split(info, rows, 2, *pair, back_own, back_other)
    back_one = topo.swap(back_send, line, 1)
    gate_up_full = grads_sent(info, mlp_in, grads, block)
    gate_up_got = topo.swap(gate_up_full, square, 1)
    chunks = (0, 2, True), (1, 2, True)
    down_keep, down_send = sum_split(info, shard_rows, 2, *chunks, down_kept, down_last)
    down_one = topo.swap(down_send, line, 0)
    block_out = close_rows(info, state, out_keep, out_two)
    back_keep, back_send = sum_split(info, rows, 1, *single, back_keep, back_one)
    back_two = topo.swap(back_send, line, 0)
    down_two = topo.swap(second_chunks(info, down_keep, down_one), line, 1)

    grad_state_low, grad_state, gain_two_grad = norm_back(
        info, state, back_keep, back_two, out_grad_in, gain_two, False
    )
    state_other = topo.other_core(grad_state_low)
    gate_up_kept, gate_up_send = grads_kept(info, mlp_in, grads, block, gate_up_got)
    gate_up_last = topo.swap(gate_up_send, square, 0)
    grad_state_all = join(info, grad_state_low, state_other)
    o_full = grads_sent(info, grad_state_all, mixed, block)
    o_got = topo.swap(o_full, square, 1)
    grad_linear, bias_grad, own_part, other_part = attend_back(
        info,
        grad_state_all,
        o_all,
        q_all,
        linear,
        mass,
        cosine,
        sine,
        row_info,
        col_info,
        q_heads,
        kv_heads,
    )
    part_other = topo.other_core(other_part)
    q_full = grads_sent(info, attn_in, grad_linear, block)
    q_got = topo.swap(q_full, square, 1)
    (down_grads,) = columns_out(info, down_keep, down_one, down_two, part, ff_cols)
    o_kept, o_send = grads_kept(info, grad_state_all, mixed, block, o_got)
    o_last = topo.swap(o_send, square, 0)
    gate_up_keep, gate_up_send = sum_split(
        info, shard_rows, 2, *chunks, gate_up_kept, gate_up_last
    )
    gate_up_one = topo.swap(gate_up_send, line, 0)
    tokens_grad, gain_one_grad = norm_back(
        info, inputs, own_part, part_other, grad_state, gain_one, True
    )
    gain_grads = jnp.concatenate([gain_one_grad, gain_two_grad], axis=0)
    gain_grads = gain_grads + topo.other_core(gain_grads)
    sums = jnp.concatenate([bias_grad.reshape(-1), gain_grads.reshape(-1)]).reshape(-1, LANES)
    sums = sums + topo.swap(sums, line, 0)

    q_kept, q_send = grads_kept(info, attn_in, grad_linear, block, q_got)
    q_last = topo.swap(q_send, square, 0)
    sums = sums + topo.swap(sums, line, 1)
    ordered = (0, 1, True), (2, 1, True)
    o_keep, o_send = sum_split(info, shard_rows, 2, *ordered, o_kept, o_last)
    o_one = topo.swap(o_send, line, 1)
    sums = sums + topo.swap(sums, square, 0)
    gate_up_two = topo.swap(second_chunks(info, gate_up_keep, gate_up_one), line, 1)
    sums = sums + topo.swap(sums, square, 1)
    sums = sums.reshape(-1)
    own_bias = sums[:qkv_cols]
    gain_sum = sums[qkv_cols:].reshape(2, width)
    q_keep, q_send = sum_split(info, shard_rows, 2, *ordered, q_kept, q_last)
    q_one = topo.swap(q_send, line, 1)
    o_keep, o_send = sum_split(info, shard_rows, 1, *single, o_keep, o_one)
    o_two = topo.swap(o_send, line, 0)
    q_keep, q_send = sum_split(info, shard_rows, 1, *single, q_keep, q_one)
    q_two = topo.swap(q_send, line, 0)
    (o_grads,) = sum_out(info, o_keep, o_two, (q_cols,))
    gate_grads, up_grads = columns_out(
        info, gate_up_keep, gate_up_one, gate_up_two, part, ff_cols
    )
    q_grads, k_grads, v_grads = sum_out(info, q_keep, q_two, (q_cols, kv_cols, kv_cols))
    CLOCK[0] = None
    return (
        block_out,
        tokens_grad,
        gain_sum[0],
        q_grads,
        own_bias[:q_cols],
        k_grads,
        own_bias[q_cols : q_cols + kv_cols],
        v_grads,
        own_bias[q_cols + kv_cols :],
        o_grads,
        gain_sum[1],
        gate_grads,
        up_grads,
        down_grads,
    )


def solution(mesh):
    rows = P(("dp", "tensor"), None)
    both = P("dp", "tensor")
    half = P("tensor")
    in_specs = (
        rows, rows, P("dp", None), P(), both, half, both, half, both, half, both, P(), both, both, both,
    )
    out_specs = (
        rows, rows, P(), both, half, both, half, both, half, both, P(), both, both, both,
    )
    fast = mesh.shape["dp"] == LINE * LINE and mesh.shape["tensor"] == 2
    return jax.shard_map(
        per_device if fast else plain_device,
        mesh=mesh,
        in_specs=in_specs,
        out_specs=out_specs,
        check_vma=False,
    )
```

```python
import functools
import math

import jax
import jax.numpy as jnp
from jax import lax
from jax.experimental import pallas as pl
from jax.experimental.pallas import tpu as pltpu
from jax.sharding import PartitionSpec as P

HEAD_DIM = 128
EPSILON = 1e-06
ROPE_BASE = 1000000.0
MASKED = -1e30
LINE = 4
LANES = 128
BF = jnp.bfloat16
F32 = jnp.float32
VMEM_BYTES = 56 * 2**20
ANY = pl.BlockSpec(memory_space=pl.ANY)


def normalize(values):
    factor = lax.rsqrt(jnp.mean(values * values, axis=1, keepdims=True) + EPSILON)
    return (values * factor, factor)


def plain_norm_back(grad_normed, normed, factor, gain_vec):
    scaled = grad_normed * gain_vec[None, :]
    row_inner = jnp.mean(scaled * normed, axis=1, keepdims=True)
    return (factor * (scaled - normed * row_inner), jnp.sum(grad_normed * normed, axis=0))


def rope_tables(positions, width):
    half_width = width // 2
    frequency = jnp.power(ROPE_BASE, -2.0 * jnp.arange(half_width, dtype=F32) / width)
    angles = positions.astype(F32)[:, None] * frequency[None, :]
    return (jnp.cos(angles), jnp.sin(angles))


def rotate(values, cosine_table, sine_table):
    half_width = values.shape[-1] // 2
    lower_half = values[..., :half_width]
    upper_half = values[..., half_width:]
    return jnp.concatenate(
        [
            lower_half * cosine_table - upper_half * sine_table,
            upper_half * cosine_table + lower_half * sine_table,
        ],
        axis=-1,
    )


def unrotate(values, cosine_table, sine_table):
    return rotate(values, cosine_table, -sine_table)


def segment_info(length_row, places):
    seq_ends = jnp.cumsum(length_row)
    starts = seq_ends - length_row
    segment = jnp.sum((places[:, None] >= seq_ends[None, :]).astype(jnp.int32), axis=1)
    slot_ids = jnp.arange(length_row.shape[0], dtype=jnp.int32)
    offset = jnp.sum(jnp.where(segment[:, None] == slot_ids[None, :], starts[None, :], 0), axis=1)
    return (segment, places - offset)


class PlainTopo:
    def __init__(self):
        self.dp = lax.axis_size("dp")
        self.square = self.dp // LINE
        self.me = lax.axis_index("dp")
        self.core = lax.axis_index("tensor")
        self.line_at = self.me // self.square
        self.square_at = self.me % self.square
        line_bits = [self.square << i for i in range(LINE.bit_length() - 1)]
        square_bits = [1 << i for i in range(self.square.bit_length() - 1)]
        self.line = (line_bits, line_bits[::-1])
        self.squares = (square_bits, square_bits[::-1])

    def swap(self, array, bits, phase):
        perm = []
        for place in range(self.dp):
            for core in range(2):
                perm.append((place * 2 + core, (place ^ bits[core][phase]) * 2 + core))
        return lax.ppermute(array, ("dp", "tensor"), perm)

    def other_core(self, array):
        return lax.ppermute(array, "tensor", [(0, 1), (1, 0)])

    def offset(self, bits, index, unit):
        totals = [0, 0]
        for core in range(2):
            for phase, bit in enumerate(bits[core]):
                if index >> phase & 1:
                    totals[core] ^= bit // unit
        return jnp.where(self.core == 0, totals[0], totals[1])

    def gather(self, own, bits):
        pieces = [own]
        for phase in range(len(bits[0])):
            pieces = pieces + [self.swap(piece, bits, phase) for piece in pieces]
        return pieces

    def gather_joined(self, own, bits):
        joined = own
        for phase in range(len(bits[0])):
            joined = jnp.concatenate([joined, self.swap(joined, bits, phase)], axis=0)
        return joined

    def scatter_sum(self, array, bits):
        for phase in reversed(range(len(bits[0]))):
            half = array.shape[0] // 2
            got = self.swap(array[half:], bits, phase)
            array = (array[:half].astype(F32) + got.astype(F32)).astype(BF)
        return array

    def total(self, array):
        for bits in (self.line, self.squares):
            for phase in range(len(bits[0])):
                array = array + self.swap(array, bits, phase)
        return array

    def exchange(self, chunks, bits):
        rows = chunks[0].shape[0]
        held = [chunk for chunk in chunks]
        for phase in range(len(bits[0])):
            step = 1 << phase
            keep = [i for i in range(len(chunks)) if not i & step]
            keep = [i for i in keep if held[i] is not None]
            sent = jnp.concatenate([held[i + step] for i in keep], axis=0)
            got = self.swap(sent, bits, phase)
            parts = jnp.split(got, len(keep), axis=0)
            for i, part in zip(keep, parts):
                held[i] = jnp.concatenate([held[i], part], axis=0)
                held[i + step] = None
        return jnp.split(held[0], len(chunks), axis=0)

    def ordered(self, pieces, bits, unit, at):
        count = len(pieces)
        tables = []
        for core in range(2):
            table = [0] * count
            for index in range(count):
                total = 0
                for phase, bit in enumerate(bits[core]):
                    if index >> phase & 1:
                        total ^= bit // unit
                table[total] = index
            tables.append(table)
        tables = jnp.asarray(tables, jnp.int32)[self.core]
        stacked = jnp.stack(pieces)
        return [
            lax.dynamic_index_in_dim(
                stacked, lax.dynamic_index_in_dim(tables, place ^ at, 0, False), 0, False
            )
            for place in range(count)
        ]


def to_inner(rows, topo):
    count, width = rows.shape
    rest = width // topo.dp
    cut = rows.reshape(count, LINE, topo.square, rest).transpose(2, 0, 1, 3)
    cut = cut.reshape(topo.square, count, LINE * rest)
    return jnp.concatenate(
        [
            lax.dynamic_index_in_dim(cut, topo.square_at ^ i, 0, False)
            for i in range(topo.square)
        ],
        axis=1,
    )


def to_outer(rows, topo):
    count, width = rows.shape
    rest = width // topo.dp
    cut = rows.reshape(count, topo.square, LINE * rest).transpose(1, 0, 2)
    cut = jnp.stack(
        [
            lax.dynamic_index_in_dim(cut, topo.square_at ^ i, 0, False)
            for i in range(topo.square)
        ]
    )
    cut = cut.reshape(topo.square, count, LINE, rest).transpose(1, 2, 0, 3)
    return cut.reshape(count, width)


def dot(left, right):
    return jnp.dot(left, right, preferred_element_type=F32)


def dot_t(left, right):
    return lax.dot_general(left, right, (((1,), (1,)), ((), ())), preferred_element_type=F32)


def t_dot(left, right):
    return lax.dot_general(left, right, (((0,), (0,)), ((), ())), preferred_element_type=F32)


def attention_scores(queries, key_rows, allowed):
    score_scale = 1.0 / math.sqrt(queries.shape[-1])
    raw_scores = jnp.einsum("qgpd,kgd->gpqk", queries, key_rows, preferred_element_type=F32)
    return jnp.where(allowed[None, None], raw_scores * score_scale, MASKED)


def plain_device(
    tokens,
    out_grad,
    lengths,
    attn_gain,
    q_weight,
    q_bias,
    k_weight,
    k_bias,
    v_weight,
    v_bias,
    o_weight,
    mlp_gain,
    gate_weight,
    up_weight,
    down_weight,
):
    topo = PlainTopo()
    local_rows, width = tokens.shape
    group_rows = 2 * local_rows
    q_cols = q_weight.shape[1]
    kv_cols = k_weight.shape[1]
    qkv_cols = q_cols + 2 * kv_cols
    ff_cols = gate_weight.shape[1]
    part = -(-ff_cols // (LINE * LANES)) * LANES
    kv_groups = kv_cols // HEAD_DIM
    per_group = q_cols // HEAD_DIM // kv_groups
    score_scale = 1.0 / math.sqrt(HEAD_DIM)

    def line_gather(shard):
        pieces = jnp.split(topo.gather_joined(shard, topo.line), LINE, axis=0)
        return jnp.concatenate(topo.ordered(pieces, topo.line, topo.square, topo.line_at), axis=0)

    def square_gather(shard):
        pieces = topo.gather(shard, topo.squares)
        return jnp.concatenate(topo.ordered(pieces, topo.squares, 1, 0), axis=0)

    def square_scatter(grads):
        pieces = jnp.split(grads.astype(BF), topo.square, axis=0)
        by_index = topo.ordered(pieces, tuple(b for b in topo.squares), 1, 0)
        return topo.scatter_sum(jnp.concatenate(by_index, axis=0), topo.squares)

    def line_offset(index):
        return topo.line_at ^ topo.offset(topo.line, index, topo.square)

    def columns_in(shards):
        padded = [jnp.pad(s, ((0, 0), (0, LINE * part - ff_cols))) for s in shards]
        chunks = []
        for index in range(LINE):
            start = line_offset(index) * part
            chunks.append(
                jnp.concatenate(
                    [lax.dynamic_slice_in_dim(s, start, part, axis=1) for s in padded], axis=1
                )
            )
        got = topo.exchange(chunks, topo.line)
        return jnp.concatenate(topo.ordered(got, topo.line, topo.square, topo.line_at), axis=0)

    def columns_out(piece, count):
        rows = piece.shape[0] // LINE
        chunks = [
            lax.dynamic_slice_in_dim(piece, line_offset(index) * rows, rows, axis=0)
            for index in range(LINE)
        ]
        got = topo.ordered(
            topo.exchange(chunks, topo.line), topo.line, topo.square, topo.line_at
        )
        return [
            jnp.concatenate([g[:, i * part : (i + 1) * part] for g in got], axis=1)[
                :, :ff_cols
            ].astype(F32)
            for i in range(count)
        ]

    def rows_out(piece):
        rows = piece.shape[0] // LINE
        chunks = [
            lax.dynamic_slice_in_dim(piece, line_offset(index) * rows, rows, axis=0)
            for index in range(LINE)
        ]
        return topo.scatter_sum(jnp.concatenate(chunks, axis=0), topo.line).astype(F32)

    def both_cores(rows):
        return jnp.concatenate([rows, topo.other_core(rows)], axis=0)

    def core_sum(rows):
        half = rows.shape[0] // 2
        return rows[:half] + topo.other_core(rows[half:].astype(BF)).astype(F32)

    def line_tokens(rows):
        return both_cores(topo.gather_joined(rows, topo.line))

    def line_sum(partial):
        return topo.scatter_sum(core_sum(partial).astype(BF), topo.line).astype(F32)

    row_ids = jnp.arange(local_rows, dtype=jnp.int32)
    places = jnp.concatenate(
        [topo.core * local_rows + row_ids, (1 - topo.core) * local_rows + row_ids]
    )
    segment, positions = segment_info(lengths[0], places)
    allowed = (segment[:, None] == segment[None, :]) & (places[None, :] <= places[:, None])
    cosine_table, sine_table = rope_tables(positions, HEAD_DIM)
    q_cosine = cosine_table[:, None, None, :]
    q_sine = sine_table[:, None, None, :]
    k_cosine = cosine_table[:, None, :]
    k_sine = sine_table[:, None, :]

    inputs_low = to_inner(tokens, topo)
    out_grad_low = to_inner(out_grad, topo)
    gains = to_inner(jnp.stack([attn_gain, mlp_gain]), topo).astype(F32)
    gain_one, gain_two = gains[0], gains[1]
    inputs = inputs_low.astype(F32)
    bias_all = jnp.concatenate([q_bias, k_bias, v_bias]).astype(F32)

    qkv_local = jnp.concatenate([q_weight, k_weight, v_weight], axis=1)
    qkv_all = square_gather(line_gather(qkv_local))
    o_all = square_gather(line_gather(o_weight))
    down_all = square_gather(columns_in([down_weight]))
    grad_out_all = line_tokens(out_grad_low)
    gate_up = square_gather(columns_in([gate_weight, up_weight]))

    normed_one, factor_one = normalize(inputs)
    attn_in = both_cores((normed_one * gain_one[None, :]).astype(BF))
    linear = dot(attn_in, qkv_all) + bias_all[None, :]
    queries = rotate(
        linear[:, :q_cols].reshape(group_rows, kv_groups, per_group, HEAD_DIM), q_cosine, q_sine
    ).astype(BF)
    key_rows = rotate(
        linear[:, q_cols : q_cols + kv_cols].reshape(group_rows, kv_groups, HEAD_DIM),
        k_cosine,
        k_sine,
    ).astype(BF)
    values = linear[:, q_cols + kv_cols :].reshape(group_rows, kv_groups, HEAD_DIM).astype(BF)
    scores = attention_scores(queries, key_rows, allowed)
    row_peak = jnp.max(scores, axis=-1, keepdims=True)
    exponent = jnp.exp(scores - row_peak)
    row_mass = jnp.sum(exponent, axis=-1, keepdims=True)
    log_mass = row_peak + jnp.log(row_mass)
    probs_low = (exponent / row_mass).astype(BF)
    mixed_heads = jnp.einsum("gpqk,kgd->qgpd", probs_low, values, preferred_element_type=F32)
    mixed_heads = mixed_heads.reshape(group_rows, q_cols).astype(BF)
    hidden_state = inputs + core_sum(dot_t(mixed_heads, o_all))
    normed_two, factor_two = normalize(hidden_state)

    mlp_in = line_tokens((normed_two * gain_two[None, :]).astype(BF))
    grad_hidden = dot(grad_out_all, down_all)
    gate_up_out = dot(mlp_in, gate_up)
    gate_val = gate_up_out[:, :part]
    up_val = gate_up_out[:, part:]
    sigmoid_gate = jax.nn.sigmoid(gate_val)
    activated = gate_val * sigmoid_gate
    hidden_units = (activated * up_val).astype(BF)
    grad_gate = (
        grad_hidden * up_val * sigmoid_gate * (1.0 + gate_val * (1.0 - sigmoid_gate))
    ).astype(BF)
    grad_up = (grad_hidden * activated).astype(BF)
    grad_gate_up = jnp.concatenate([grad_gate, grad_up], axis=1)
    grad_normed_two = line_sum(dot_t(grad_gate_up, gate_up))
    block_out = (hidden_state + line_sum(dot_t(hidden_units, down_all))).astype(BF)
    gate_grads, up_grads = columns_out(square_scatter(t_dot(mlp_in, grad_gate_up)), 2)
    (down_grads,) = columns_out(square_scatter(t_dot(grad_out_all, hidden_units)), 1)

    back_two, gain_two_grad = plain_norm_back(grad_normed_two, normed_two, factor_two, gain_two)
    grad_state = out_grad_low.astype(F32) + back_two
    grad_state_all = both_cores(grad_state.astype(BF))
    o_grads = rows_out(square_scatter(t_dot(grad_state_all, mixed_heads)))
    grad_mixed = dot(grad_state_all, o_all)
    grad_heads = grad_mixed.astype(BF).reshape(group_rows, kv_groups, per_group, HEAD_DIM)
    scores_again = attention_scores(queries, key_rows, allowed)
    prob_rows = jnp.exp(scores_again - log_mass)
    grad_probs = jnp.einsum("qgpd,kgd->gpqk", grad_heads, values, preferred_element_type=F32)
    row_inner = jnp.sum(prob_rows * grad_probs, axis=-1, keepdims=True)
    grad_scores = (prob_rows * (grad_probs - row_inner) * score_scale).astype(BF)
    grad_values = jnp.einsum(
        "gpqk,qgpd->kgd", prob_rows.astype(BF), grad_heads, preferred_element_type=F32
    )
    grad_queries = jnp.einsum("gpqk,kgd->qgpd", grad_scores, key_rows, preferred_element_type=F32)
    grad_keys = jnp.einsum("gpqk,qgpd->kgd", grad_scores, queries, preferred_element_type=F32)
    grad_linear = jnp.concatenate(
        [
            unrotate(grad_queries, q_cosine, q_sine).reshape(group_rows, q_cols),
            unrotate(grad_keys, k_cosine, k_sine).reshape(group_rows, kv_cols),
            grad_values.reshape(group_rows, kv_cols),
        ],
        axis=1,
    ).astype(BF)
    bias_grad = jnp.sum(grad_linear.astype(F32), axis=0)
    qkv_grads = rows_out(square_scatter(t_dot(attn_in, grad_linear)))
    grad_normed_one = core_sum(dot_t(grad_linear, qkv_all))
    back_one, gain_one_grad = plain_norm_back(grad_normed_one, normed_one, factor_one, gain_one)
    tokens_grad = (grad_state + back_one).astype(BF)
    gain_grads = to_outer(jnp.stack([gain_one_grad, gain_two_grad]), topo)
    gain_grads = gain_grads + topo.other_core(gain_grads)
    small = topo.total(jnp.concatenate([bias_grad, gain_grads.reshape(-1)]).reshape(-1, LANES))
    small = small.reshape(-1)
    own_bias = small[:qkv_cols]
    gain_sum = small[qkv_cols:].reshape(2, width)
    return (
        to_outer(block_out, topo),
        to_outer(tokens_grad, topo),
        gain_sum[0],
        qkv_grads[:, :q_cols],
        own_bias[:q_cols],
        qkv_grads[:, q_cols : q_cols + kv_cols],
        own_bias[q_cols : q_cols + kv_cols],
        qkv_grads[:, q_cols + kv_cols : qkv_cols],
        own_bias[q_cols + kv_cols :],
        o_grads,
        gain_sum[1],
        gate_grads,
        up_grads,
        down_grads,
    )


def nn(left, right):
    return jnp.dot(left, right, preferred_element_type=F32)


def nt(left, right):
    return lax.dot_general(left, right, (((1,), (1,)), ((), ())), preferred_element_type=F32)


def tn(left, right):
    return lax.dot_general(left, right, (((0,), (0,)), ((), ())), preferred_element_type=F32)


def shape(dims, kind):
    return jax.ShapeDtypeStruct(dims, kind)


def whole(dims):
    return pl.BlockSpec(dims, lambda *_: (0,) * len(dims))


OFF, NEIGHBOUR, INDEX, AT, OTHER = 0, 4, 8, 12, 13


class Topo:
    def __init__(self):
        self.dp = lax.axis_size("dp")
        me = lax.axis_index("dp")
        core = lax.axis_index("tensor")
        line_at, square_at = me >> 2, me & 3

        def by_core(index):
            return jnp.where(core == 0, index, (index >> 1) | ((index & 1) << 1))

        self.core = core
        self.square_at = square_at
        self.line = ((LINE, 2 * LINE), (2 * LINE, LINE))
        self.square = ((1, 2), (2, 1))
        count = jnp.arange(LINE, dtype=jnp.int32)
        self.info = jnp.concatenate(
            [
                by_core(count),
                line_at ^ by_core(count),
                by_core(line_at ^ count),
                jnp.stack([square_at, 1 - core]),
            ]
        ).astype(jnp.int32)

    def swap(self, array, bits, phase):
        perm = []
        for place in range(self.dp):
            for core in range(2):
                flip = bits[core][phase] if phase < 2 else bits[core][0] ^ bits[core][1]
                perm.append((place * 2 + core, (place ^ flip) * 2 + core))
        return lax.ppermute(array, ("dp", "tensor"), perm)

    def other_core(self, array):
        return lax.ppermute(array, "tensor", [(0, 1), (1, 0)])

    def both_ways(self, array):
        return lax.all_to_all(array, "tensor", 0, 0, tiled=True)


CLOCK = [None]
TOKEN = jax.ShapeDtypeStruct((8, 128), F32)
IN_VMEM = pl.BlockSpec(memory_space=pltpu.VMEM)
IN_SMEM = pl.BlockSpec(memory_space=pltpu.SMEM)


def in_order(body, ins, outs):
    taken = 0 if CLOCK[0] is None else 1

    def full(*refs):
        body(*refs[:ins], *refs[ins + taken : ins + taken + outs], *refs[ins + taken + outs + 1 :])

    return full


def run(kernel, single, args):
    taken = [] if CLOCK[0] is None else [CLOCK[0]]
    *out, CLOCK[0] = kernel(*args, *taken)
    return out[0] if single else out


def as_list(value):
    return list(value) if isinstance(value, (list, tuple)) else [value]


def call(body, grid, in_specs, out_specs, out_shape, scratch, info, *args, mib=32):
    outs = as_list(out_shape)
    late = 0 if CLOCK[0] is None else 1
    kernel = pl.pallas_call(
        in_order(body, 1 + len(in_specs), len(outs)),
        grid_spec=pltpu.PrefetchScalarGridSpec(
            num_scalar_prefetch=1,
            grid=grid,
            in_specs=list(in_specs) + [IN_VMEM] * late,
            out_specs=as_list(out_specs) + [IN_VMEM],
            scratch_shapes=list(scratch),
        ),
        out_shape=outs + [TOKEN],
        compiler_params=pltpu.CompilerParams(vmem_limit_bytes=mib * 2**20),
        cost_estimate=pl.CostEstimate(flops=1000, bytes_accessed=1000, transcendentals=0),
        name=body.__qualname__.split(".")[0],
    )
    return run(kernel, not isinstance(out_shape, (list, tuple)), (info,) + args)


def small(body, out_shape, scratch, info, *args, mib=10):
    outs = as_list(out_shape)
    late = 0 if CLOCK[0] is None else 1
    kernel = pl.pallas_call(
        in_order(body, 1 + len(args), len(outs)),
        in_specs=[IN_SMEM] + [IN_VMEM] * (len(args) + late),
        out_specs=[IN_VMEM] * (len(outs) + 1),
        scratch_shapes=list(scratch),
        out_shape=outs + [TOKEN],
        compiler_params=pltpu.CompilerParams(vmem_limit_bytes=mib * 2**20),
        cost_estimate=pl.CostEstimate(flops=1000, bytes_accessed=1000, transcendentals=0),
        name=body.__qualname__.split(".")[0],
    )
    return run(kernel, not isinstance(out_shape, (list, tuple)), (info,) + args)


def tie(info, array):
    def body(info_ref, in_ref, out_ref):
        out_ref[...] = in_ref[...]

    return small(body, shape(array.shape, array.dtype), [], info, array)


def spacer(topo):
    CLOCK[0] = topo.other_core(CLOCK[0])


def wait_for(info, *arrays):
    def body(*refs):
        del refs

    late = 0 if CLOCK[0] is None else 1
    kernel = pl.pallas_call(
        body,
        in_specs=[ANY] * len(arrays) + [IN_VMEM] * late,
        out_specs=[IN_VMEM],
        out_shape=[TOKEN],
        compiler_params=pltpu.CompilerParams(vmem_limit_bytes=16 * 2**20),
        cost_estimate=pl.CostEstimate(flops=1, bytes_accessed=1, transcendentals=0),
        name="wait_for",
    )
    (CLOCK[0],) = kernel(*arrays, *([CLOCK[0]] if late else []))


def join(info, *args):
    def body(info_ref, *refs):
        start = 0
        for ref in refs[:-1]:
            refs[-1][start : start + ref.shape[0]] = ref[...]
            start += ref.shape[0]

    rows = sum(a.shape[0] for a in args)
    return small(body, shape((rows,) + args[0].shape[1:], args[0].dtype), [], info, *args)


def join_split(info, widths, *args):
    rows = sum(a.shape[0] for a in args)

    def body(info_ref, *refs):
        ins, outs = refs[: len(args)], refs[len(args) :]
        low = 0
        for ref in ins:
            start = 0
            for out, cols in zip(outs, widths):
                out[low : low + ref.shape[0]] = ref[:, start : start + cols]
                start += cols
            low += ref.shape[0]

    return small(body, [shape((rows, cols), BF) for cols in widths], [], info, *args)


def beside(info, *args):
    def body(info_ref, *refs):
        start = 0
        for ref in refs[:-1]:
            refs[-1][:, start : start + ref.shape[1]] = ref[...]
            start += ref.shape[1]

    cols = sum(a.shape[1] for a in args)
    return small(body, shape((args[0].shape[0], cols), args[0].dtype), [], info, *args)


def placed(info, rows, takes, *args):
    def body(info_ref, *refs):
        for index, (which, start) in enumerate(takes):
            target = pl.multiple_of(info_ref[NEIGHBOUR + index] * rows, 16)
            refs[-1][pl.ds(target, rows)] = refs[which][start : start + rows]

    return small(body, shape((LINE * rows, args[0].shape[1]), BF), [], info, *args)


def second_chunks(info, kept, got):
    rows = kept.shape[0] // 2

    def body(info_ref, kept_ref, got_ref, out_ref):
        out_ref[:rows] = kept_ref[rows:]
        out_ref[rows:] = got_ref[rows:]

    return small(body, shape(kept.shape, BF), [], info, kept, got)


def cut_columns(info, part, *weights):
    count = len(weights)
    rows, cols = weights[0].shape
    short = cols - (LINE - 1) * part

    def body(info_ref, *refs):
        ins, outs = refs[:count], refs[count:]
        for index in range(LINE):
            at = info_ref[NEIGHBOUR + index]
            out = outs[1 - index % 2]
            low = index // 2 * rows
            for which, ref in enumerate(ins):
                start = pl.multiple_of(at * part, LANES)
                first = which * part
                out[low : low + rows, first : first + short] = ref[:, pl.ds(start, short)]
                if short < part:
                    rest = pl.multiple_of(jnp.minimum(at, LINE - 2) * part + short, LANES)
                    tail = ref[:, pl.ds(rest, part - short)]
                    out[low : low + rows, first + short : first + part] = jnp.where(
                        at < LINE - 1, tail, jnp.zeros_like(tail)
                    )

    return small(body, [shape((2 * rows, count * part), BF)] * 2, [], info, *weights)


def piece_copies(info_ref, pieces, target, sems, cols=None, first_col=0):
    rows = target.shape[0] // LINE
    low, high = cols or (0, pieces[0].shape[1])
    index = 0
    for piece in pieces:
        for block in range(piece.shape[0] // rows):
            start = pl.multiple_of(info_ref[OFF + index] * rows, rows)
            yield pltpu.make_async_copy(
                piece.at[pl.ds(block * rows, rows), pl.ds(low, high - low)],
                target.at[pl.ds(start, rows), pl.ds(first_col + low, high - low)],
                sems.at[index],
            )
            index += 1


def square_blocks(info_ref, pieces, width):
    rows = width // LINE
    index = 0
    for piece in pieces:
        for block in range(piece.shape[0] // rows):
            start = pl.multiple_of(info_ref[OFF + index] * rows, LANES)
            yield pl.ds(start, rows), piece[block * rows : (block + 1) * rows]
            index += 1


def inward(values, at, store):
    width = values.shape[1]
    block = width // LINE
    rest = block // LINE
    for square in range(LINE):
        parts = [
            values[:, line * block + square * rest : line * block + (square + 1) * rest]
            for line in range(LINE)
        ]
        start = pl.multiple_of((square ^ at) * block, LANES)
        store(pl.ds(start, block), jnp.concatenate(parts, axis=1))


def outward(ref, at):
    width = ref.shape[1]
    block = width // LINE
    rest = block // LINE
    blocks = []
    for square in range(LINE):
        start = pl.multiple_of((square ^ at) * block, LANES)
        blocks.append(ref[:, pl.ds(start, block)])
    parts = []
    for line in range(LINE):
        for square in range(LINE):
            parts.append(blocks[square][:, line * rest : (line + 1) * rest])
    return jnp.concatenate(parts, axis=1)


def turn_rows(info, rows):
    def body(info_ref, rows_ref, out_ref, held):
        def store(cols, block):
            held[:, cols] = block

        inward(rows_ref[...].astype(F32), info_ref[AT], store)
        out_ref[...] = held[...].astype(BF)

    return small(body, shape(rows.shape, BF), [pltpu.VMEM(rows.shape, F32)], info, rows)


def open_rows(info, rows, gains):
    def body(info_ref, rows_ref, gains_ref, out_ref, in_ref, gain_ref, held):
        def store_gain(cols, block):
            gain_ref[:, cols] = block

        def store(cols, block):
            held[:, cols] = block

        inward(gains_ref[...], info_ref[AT], store_gain)
        inward(rows_ref[...].astype(F32), info_ref[AT], store)
        values = held[...]
        in_ref[...] = values.astype(BF)
        factor = lax.rsqrt(jnp.mean(values * values, axis=1, keepdims=True) + EPSILON)
        out_ref[...] = (values * factor * gain_ref[0:1, :]).astype(BF)

    return small(
        body,
        [shape(rows.shape, BF), shape(rows.shape, BF), shape(gains.shape, F32)],
        [pltpu.VMEM(rows.shape, F32)],
        info,
        rows,
        gains,
    )


def state_rows(info, rows, own, got, gain):
    def body(info_ref, rows_ref, own_ref, early_ref, late_ref, gain_ref, out_ref, state_ref):
        half = dims[0] // 2
        for start, got_ref in ((0, early_ref), (half, late_ref)):
            span = pl.ds(start, half)
            values = rows_ref[span].astype(F32) + (own_ref[span] + got_ref[...].astype(F32))
            state_ref[span] = values
            factor = lax.rsqrt(jnp.mean(values * values, axis=1, keepdims=True) + EPSILON)
            out_ref[span] = (values * factor * gain_ref[...]).astype(BF)

    dims = rows.shape
    return small(
        body, [shape(dims, BF), shape(dims, F32)], [], info, rows, own, *got, gain
    )


def close_rows(info, state, own, got):
    def body(info_ref, state_ref, own_ref, got_ref, out_ref, held):
        held[...] = state_ref[...] + (own_ref[...].astype(F32) + got_ref[...].astype(F32))
        out_ref[...] = outward(held, info_ref[AT]).astype(BF)

    dims = state.shape
    return small(
        body,
        shape(dims, BF),
        [pltpu.VMEM(dims, F32)],
        info,
        state,
        own,
        got,
    )


def norm_back(info, values, own, got, base, gain, turn):
    def body(info_ref, values_ref, own_ref, got_ref, base_ref, gain_ref, *refs):
        values = values_ref[...].astype(F32)
        factor = lax.rsqrt(jnp.mean(values * values, axis=1, keepdims=True) + EPSILON)
        normed = values * factor
        grad = own_ref[...].astype(F32) + got_ref[...].astype(F32)
        scaled = grad * gain_ref[...]
        row_inner = jnp.mean(scaled * normed, axis=1, keepdims=True)
        total = base_ref[...].astype(F32) + factor * (scaled - normed * row_inner)
        gain_grad = jnp.sum(grad * normed, axis=0, keepdims=True)
        if turn:
            out_ref, gain_out_ref, held, gain_held = refs
            held[...] = total
            out_ref[...] = outward(held, info_ref[AT]).astype(BF)
        else:
            low_ref, out_ref, gain_out_ref, gain_held = refs
            out_ref[...] = total
            low_ref[...] = total.astype(BF)
        gain_held[...] = gain_grad
        gain_out_ref[...] = outward(gain_held, info_ref[AT])

    dims = values.shape
    kinds = (BF,) if turn else (BF, F32)
    return small(
        body,
        [shape(dims, kind) for kind in kinds] + [shape(gain.shape, F32)],
        ([pltpu.VMEM(dims, F32)] if turn else []) + [pltpu.VMEM(gain.shape, F32)],
        info,
        values,
        own,
        got,
        base,
        gain,
    )


def turned(values, cosine, sine):
    return values * cosine + pltpu.roll(values, HEAD_DIM // 2, 1) * sine


def attend(info, rows, pieces, bias, cosine, sine, row_info, col_info, q_heads, kv_heads):
    count, cols = len(pieces), pieces[0].shape[1]
    group, width = rows.shape
    q_cols = q_heads * HEAD_DIM

    def body(info_ref, in_ref, *refs):
        pieces = refs[:count]
        bias_ref, cos_ref, sin_ref, row_ref, col_ref = refs[count : count + 5]
        mixed_ref, lin_ref, mass_ref = refs[count + 5 :]
        cosine, sine = cos_ref[...], sin_ref[...]
        scale = 1.0 / math.sqrt(HEAD_DIM)
        linear = bias_ref[...]
        for cols, piece in square_blocks(info_ref, pieces, width):
            linear = linear + nn(in_ref[:, cols], piece)
        for head in range(q_heads + 2 * kv_heads):
            cols = slice(head * HEAD_DIM, (head + 1) * HEAD_DIM)
            part = linear[:, cols]
            if head < q_heads + kv_heads:
                part = turned(part, cosine, sine)
            lin_ref[:, cols] = part.astype(BF)
        allowed = (row_ref[:, 0:1] <= col_ref[...]) & (col_ref[...] <= row_ref[:, 1:2])
        for head in range(q_heads):
            key = q_heads + head // (q_heads // kv_heads)
            value = key + kv_heads
            cols = slice(head * HEAD_DIM, (head + 1) * HEAD_DIM)
            raw = nt(lin_ref[:, cols], lin_ref[:, key * HEAD_DIM : (key + 1) * HEAD_DIM])
            scores = jnp.where(allowed, raw * scale, MASKED)
            peak = jnp.max(scores, axis=1, keepdims=True)
            exponent = jnp.exp(scores - peak)
            mass = jnp.sum(exponent, axis=1, keepdims=True)
            mass_ref[:, head : head + 1] = peak + jnp.log(mass)
            probs = (exponent * (1.0 / mass)).astype(BF)
            mixed_ref[:, cols] = nn(
                probs, lin_ref[:, value * HEAD_DIM : (value + 1) * HEAD_DIM]
            ).astype(BF)

    plain = (bias, cosine, sine, row_info, col_info)
    return small(
        body,
        [shape((group, q_cols), BF), shape((group, cols), BF), shape((group, LANES), F32)],
        [],
        info,
        rows,
        *pieces,
        *plain,
        mib=20,
    )


def project(info, rows, pieces, width):
    count, cols = len(pieces), pieces[0].shape[1]
    half = rows.shape[0] // 2

    def body(info_ref, in_ref, *refs):
        pieces = refs[:count]
        early_ref, late_ref, own_ref = refs[count:]
        for cols, piece in square_blocks(info_ref, pieces, width):
            both = nt(in_ref[...], piece)
            own_ref[:, cols] = both[:half]
            early_ref[:, cols] = both[half : half + half // 2].astype(BF)
            late_ref[:, cols] = both[half + half // 2 :].astype(BF)

    return small(
        body,
        [shape((half // 2, width), BF)] * 2 + [shape((half, width), F32)],
        [],
        info,
        rows,
        *pieces,
    )


def attend_back(
    info, state, o_pieces, pieces, linear, mass, cosine, sine, row_info, col_info, q_heads, kv_heads
):
    count, cols = len(pieces), pieces[0].shape[1]
    group, width = state.shape
    q_cols = q_heads * HEAD_DIM
    half = group // 2

    def body(info_ref, state_ref, *refs):
        o_refs, q_refs = refs[:count], refs[count : 2 * count]
        lin_ref, mass_ref, cos_ref, sin_ref, row_ref, col_ref = refs[2 * count : 2 * count + 6]
        grad_ref, bias_ref, own_ref, other_ref = refs[2 * count + 6 : 2 * count + 10]
        heads_ref = refs[-1]
        cosine, sine = cos_ref[...], -sin_ref[...]
        scale = 1.0 / math.sqrt(HEAD_DIM)
        heads = 0.0
        for cols, piece in square_blocks(info_ref, o_refs, width):
            heads = heads + nn(state_ref[:, cols], piece)
        heads_ref[...] = heads.astype(BF)
        allowed = (row_ref[:, 0:1] <= col_ref[...]) & (col_ref[...] <= row_ref[:, 1:2])
        per_group = q_heads // kv_heads
        for place in range(kv_heads):
            key_cols = slice((q_heads + place) * HEAD_DIM, (q_heads + place + 1) * HEAD_DIM)
            first = q_heads + kv_heads + place
            value_cols = slice(first * HEAD_DIM, (first + 1) * HEAD_DIM)
            keys, values = lin_ref[:, key_cols], lin_ref[:, value_cols]
            grad_keys, grad_values = 0.0, 0.0
            for head in range(place * per_group, (place + 1) * per_group):
                cols = slice(head * HEAD_DIM, (head + 1) * HEAD_DIM)
                queries, grads = lin_ref[:, cols], heads_ref[:, cols]
                scores = jnp.where(allowed, nt(queries, keys) * scale, MASKED)
                probs = jnp.exp(scores - mass_ref[:, head : head + 1])
                grad_probs = nt(grads, values)
                inner = jnp.sum(probs * grad_probs, axis=1, keepdims=True)
                grad_scores = (probs * (grad_probs - inner) * scale).astype(BF)
                grad_values += tn(probs.astype(BF), grads)
                grad_keys += tn(grad_scores, queries)
                grad_ref[:, cols] = turned(nn(grad_scores, keys), cosine, sine).astype(BF)
            grad_ref[:, key_cols] = turned(grad_keys, cosine, sine).astype(BF)
            grad_ref[:, value_cols] = grad_values.astype(BF)
        bias_ref[...] = jnp.sum(grad_ref[...].astype(F32), axis=0, keepdims=True)
        for cols, piece in square_blocks(info_ref, q_refs, width):
            both = nt(grad_ref[...], piece)
            own_ref[:, cols] = both[:half]
            other_ref[:, cols] = both[half:].astype(BF)

    plain = (linear, mass, cosine, sine, row_info, col_info)
    return small(
        body,
        [
            shape((group, cols), BF),
            shape((1, cols), F32),
            shape((half, width), F32),
            shape((half, width), BF),
        ],
        [pltpu.VMEM((group, q_cols), BF)],
        info,
        state,
        *o_pieces,
        *pieces,
        *plain,
        mib=24,
    )


def forward(info, x, gate_up, tile, step=256):
    count, part = len(gate_up), gate_up[0].shape[1] // 2
    total, width = x.shape
    spans = [(low, min(low + step, part)) for low in range(0, part, step)]

    def body(info_ref, x_ref, *refs):
        pieces = refs[:count]
        hid_ref, gate_ref, up_ref, weight, sems = refs[count:]

        def span_copies(index):
            low, high = spans[index]
            yield from piece_copies(info_ref, pieces, weight, sems.at[2 * index], (low, high))
            yield from piece_copies(
                info_ref, pieces, weight, sems.at[2 * index + 1], (part + low, part + high)
            )

        opening = pl.program_id(0) == 0

        @pl.when(opening)
        def _():
            for index in range(len(spans)):
                for copy in span_copies(index):
                    copy.start()

        x = x_ref[...]
        for index, (low, high) in enumerate(spans):

            @pl.when(opening)
            def _(index=index):
                for copy in span_copies(index):
                    copy.wait()

            gate = nn(x, weight[:, low:high])
            up = nn(x, weight[:, part + low : part + high])
            share = 1.0 / (1.0 + jnp.exp(-gate))
            active = gate * share
            hid_ref[:, low:high] = (active * up).astype(BF)
            gate_ref[:, low:high] = (up * share * (1.0 + gate * (1.0 - share))).astype(BF)
            up_ref[:, low:high] = active.astype(BF)

    return call(
        body,
        (total // tile,),
        [pl.BlockSpec((tile, width), lambda i, _: (i, 0))] + [ANY] * count,
        [pl.BlockSpec((tile, part), lambda i, _: (i, 0))] * 3,
        [shape((total, part), BF)] * 3,
        [
            pltpu.VMEM((width, 2 * part), BF),
            pltpu.SemaphoreType.DMA((2 * len(spans), LINE)),
        ],
        info,
        x,
        *gate_up,
        mib=24,
    )


def halves_spec(tile, width, steps, spread):
    half = steps // 2

    def later(i, info_ref):
        first = info_ref[OTHER] * half if spread else 0
        return (first + jnp.maximum(i - half, 0), 0)

    return [
        pl.BlockSpec((tile, width), lambda i, _: (jnp.minimum(i, half - 1), 0)),
        pl.BlockSpec((tile, width), later),
    ]


def cut_rows(info, array, count):
    rows = array.shape[0] // count

    def body(info_ref, in_ref, *outs):
        for index, out in enumerate(outs):
            out[...] = in_ref[index * rows : (index + 1) * rows]

    return small(body, [shape((rows, array.shape[1]), array.dtype)] * count, [], info, array)


def store_half(value, steps, first_ref, second_ref):
    early = pl.program_id(0) < steps // 2

    @pl.when(early)
    def _():
        first_ref[...] = value

    @pl.when(jnp.logical_not(early))
    def _():
        second_ref[...] = value


def down_sum(info, hidden, down, tile, width):
    count = len(down)
    total, part = hidden.shape
    steps = total // tile

    def body(info_ref, hid_ref, *refs):
        pieces = refs[:count]
        own_ref, other_ref, weight, sems = refs[count:]

        @pl.when(pl.program_id(0) == 0)
        def _():
            copies = list(piece_copies(info_ref, pieces, weight, sems))
            for copy in copies:
                copy.start()
            for copy in copies:
                copy.wait()

        value = nt(hid_ref[...], weight[...]).astype(BF)
        store_half(value, steps, own_ref, other_ref)

    return call(
        body,
        (steps,),
        [pl.BlockSpec((tile, part), lambda i, _: (i, 0))] + [ANY] * count,
        halves_spec(tile, width, steps, False),
        [shape((total // 2, width), BF)] * 2,
        [pltpu.VMEM((width, part), BF), pltpu.SemaphoreType.DMA((LINE,))],
        info,
        hidden,
        *down,
        mib=18,
    )


def backward(info, half, g, gate_factor, up_factor, gate_up, down, tile, step=256):
    count, up_count, part = len(down), len(gate_up), down[0].shape[1]
    total, width = g.shape[0] // 2, g.shape[1]
    steps = total // tile
    spans = [(low, min(low + step, part)) for low in range(0, part, step)]

    def body(info_ref, g_ref, gate_ref, up_ref, *refs):
        gate_up, down = refs[:up_count], refs[up_count : up_count + count]
        back_ref, grad_ref, weight, sems = refs[up_count + count :]

        def span_copies(index):
            yield from piece_copies(info_ref, down, weight, sems.at[index], spans[index], 2 * part)

        def late_copies():
            yield from piece_copies(info_ref, gate_up, weight, sems.at[len(spans)])

        opening = pl.program_id(0) == 0

        @pl.when(opening)
        def _():
            for index in range(len(spans)):
                for copy in span_copies(index):
                    copy.start()
            for copy in late_copies():
                copy.start()

        g = g_ref[...]
        for index, (low, high) in enumerate(spans):

            @pl.when(opening)
            def _(index=index):
                for copy in span_copies(index):
                    copy.wait()

            grad = nn(g, weight[:, 2 * part + low : 2 * part + high])
            grad_ref[:, low:high] = (grad * gate_ref[:, low:high].astype(F32)).astype(BF)
            grad_ref[:, part + low : part + high] = (
                grad * up_ref[:, low:high].astype(F32)
            ).astype(BF)

        @pl.when(opening)
        def _():
            for copy in late_copies():
                copy.wait()

        back_ref[...] = nt(grad_ref[...], weight[:, : 2 * part]).astype(BF)

    return call(
        body,
        (steps,),
        [pl.BlockSpec((tile, cols), lambda i, _: (half * steps + i, 0)) for cols in (width, part, part)]
        + [ANY] * (up_count + count),
        [pl.BlockSpec((tile, cols), lambda i, _: (i, 0)) for cols in (width, 2 * part)],
        [shape((total, cols), BF) for cols in (width, 2 * part)],
        [
            pltpu.VMEM((width, 3 * part), BF),
            pltpu.SemaphoreType.DMA((len(spans) + 1, LINE)),
        ],
        info,
        g,
        gate_factor,
        up_factor,
        *gate_up,
        *down,
    )


def rows_spec(block, rights, where):
    rows = rights[0].shape[0]
    return [
        pl.BlockSpec((rows, block), lambda i, info_ref, r=r: (r, info_ref[OFF + where(i)]))
        for r in range(len(rights))
    ]


def grads_of(info, left, rights, block, index, got=None):
    rows, cols = rights[0].shape
    parts = len(rights)
    tile = next(t for t in (768, 512, 384, 256, 128) if cols % t == 0)

    def body(info_ref, *refs):
        value = 0.0
        for r in range(parts):
            value = value + tn(refs[r][...], refs[parts + r][...])
        if got is not None:
            value = value + refs[2 * parts][...].astype(F32)
        refs[-1][...] = value.astype(BF)

    out = pl.BlockSpec((block, tile), lambda i, _: (0, i))
    return call(
        body,
        (cols // tile,),
        rows_spec(block, rights, lambda i: index)
        + [pl.BlockSpec((rows, tile), lambda i, _: (0, i))] * parts
        + ([] if got is None else [out]),
        out,
        shape((block, cols), BF),
        [],
        info,
        *([left] * parts),
        *rights,
        *([] if got is None else [got]),
        mib=20,
    )


def grads_sent(info, left, right, block):
    total, cols = right.shape

    def body(info_ref, left_ref, right_ref, out_ref):
        out_ref[...] = tn(left_ref[...], right_ref[...]).astype(BF)

    return call(
        body,
        (2,),
        rows_spec(block, [right], lambda i: 2 + i) + [whole(right.shape)],
        pl.BlockSpec((block, cols), lambda i, _: (i, 0)),
        shape((2 * block, cols), BF),
        [],
        info,
        left,
        right,
        mib=20,
    )


def grads_kept(info, left, right, block, got):
    total, cols = right.shape

    def body(info_ref, left_ref, right_ref, got_ref, keep_ref, send_ref):
        value = (tn(left_ref[...], right_ref[...]) + got_ref[...].astype(F32)).astype(BF)
        store_half(value, 2, keep_ref, send_ref)

    return call(
        body,
        (2,),
        rows_spec(block, [right], lambda i: i)
        + [whole(right.shape), pl.BlockSpec((block, cols), lambda i, _: (i, 0))],
        [whole((block, cols))] * 2,
        [shape((block, cols), BF)] * 2,
        [],
        info,
        left,
        right,
        got,
        mib=20,
    )


def sum_split(info, block, count, keep_at, send_at, left, *rights):
    cols = left.shape[1]
    pieces = len(rights)
    rows_each = rights[0].shape[0]

    def body(info_ref, left_ref, *refs):
        right_refs, outs = refs[:pieces], refs[pieces:]
        for out, (first, stride, along) in zip(outs, (keep_at, send_at)):
            for step in range(count):
                index = first + stride * step
                if along:
                    rows = pl.ds(pl.multiple_of(info_ref[NEIGHBOUR + index] * block, 16), block)
                    total = left_ref[rows].astype(F32) + right_refs[0][rows].astype(F32)
                    out[step * block : (step + 1) * block] = total.astype(BF)
                    continue
                low, high = index * block, (index + 1) * block
                while low < high:
                    which = low // rows_each
                    end = min(high, (which + 1) * rows_each)
                    base = which * rows_each
                    total = left_ref[low:end].astype(F32)
                    total = total + right_refs[which][low - base : end - base].astype(F32)
                    start = step * block + low - index * block
                    out[start : start + end - low] = total.astype(BF)
                    low = end

    return small(body, [shape((count * block, cols), BF)] * 2, [], info, left, *rights)


def sum_out(info, left, right, widths):
    rows = left.shape[0]

    def body(info_ref, left_ref, right_ref, *outs):
        total = left_ref[...].astype(F32) + right_ref[...].astype(F32)
        start = 0
        for out, cols in zip(outs, widths):
            out[...] = total[:, start : start + cols]
            start += cols

    return small(
        body,
        [shape((rows, cols), F32) for cols in widths],
        [],
        info,
        left,
        right,
    )


def sum_rows(info, own, got, first):
    def body(info_ref, own_ref, got_ref, out_ref):
        if first:
            out_ref[:first] = own_ref[:first]
        out_ref[first:] = own_ref[first:] + got_ref[first:]

    return small(body, shape(own.shape, F32), [], info, own, got)


def columns_out(info, kept, got, last, part, cols):
    rows = kept.shape[0] // 2
    count = kept.shape[1] // part

    def body(info_ref, kept_ref, got_ref, last_ref, *outs):
        pieces = [kept_ref[:rows], got_ref[:rows], last_ref[:rows], last_ref[rows:]]
        for place in range(LINE):
            low = place * part
            span = min(part, cols - low)
            for index, piece in enumerate(pieces):

                @pl.when(info_ref[INDEX + place] == index)
                def _(piece=piece, low=low, span=span):
                    for which, out in enumerate(outs):
                        start = which * part
                        out[:, low : low + span] = piece[:, start : start + span].astype(F32)

    return small(
        body,
        [shape((rows, cols), F32)] * count,
        [],
        info,
        kept,
        got,
        last,
    )


def sequence_info(length_row, places):
    seq_ends = jnp.cumsum(length_row)
    starts = seq_ends - length_row
    inside = (places[:, None] >= starts[None, :]) & (places[:, None] < seq_ends[None, :])
    return jnp.sum(jnp.where(inside, starts[None, :], 0), axis=1)


def per_device(
    tokens,
    out_grad,
    lengths,
    attn_gain,
    q_weight,
    q_bias,
    k_weight,
    k_bias,
    v_weight,
    v_bias,
    o_weight,
    mlp_gain,
    gate_weight,
    up_weight,
    down_weight,
):
    CLOCK[0] = None
    topo = Topo()
    info = topo.info
    line, square = topo.line, topo.square
    local_rows, width = tokens.shape
    shard_rows = q_weight.shape[0]
    block = width // LINE
    q_cols = q_weight.shape[1]
    kv_cols = k_weight.shape[1]
    qkv_cols = q_cols + 2 * kv_cols
    ff_cols = gate_weight.shape[1]
    part = -(-ff_cols // (LINE * LANES)) * LANES
    q_heads, kv_heads = q_cols // HEAD_DIM, kv_cols // HEAD_DIM
    tile = local_rows * LINE // 2

    attn_own_weight = beside(info, q_weight, k_weight, v_weight, o_weight)
    attn_one = topo.swap(attn_own_weight, line, 0)
    gate_up_send, gate_up_keep = cut_columns(info, part, gate_weight, up_weight)

    attn_joined = join(info, attn_own_weight, attn_one)
    attn_two = topo.swap(attn_joined, line, 1)
    bias_all = jnp.concatenate([q_bias, k_bias, v_bias]).astype(F32)[None, :]
    gains = jnp.stack([attn_gain, mlp_gain]).astype(F32)
    attn_own, inputs, gains = open_rows(info, tokens, gains)
    gain_one, gain_two = gains[0:1], gains[1:2]
    attn_other = topo.other_core(attn_own)
    out_grad_in = turn_rows(info, out_grad)
    row_ids = jnp.arange(local_rows, dtype=jnp.int32)
    places = jnp.concatenate(
        [topo.core * local_rows + row_ids, (1 - topo.core) * local_rows + row_ids]
    )
    starts = sequence_info(lengths[0], places)
    frequency = jnp.power(ROPE_BASE, -2.0 * jnp.arange(HEAD_DIM // 2, dtype=F32) / HEAD_DIM)
    angles = (places - starts).astype(F32)[:, None] * frequency[None, :]
    cosine_half, sine_half = jnp.cos(angles), jnp.sin(angles)
    cosine = jnp.concatenate([cosine_half, cosine_half], axis=1)
    sine = jnp.concatenate([-sine_half, sine_half], axis=1)
    row_info = jnp.stack([starts, places], axis=1)
    col_info = places[None, :]
    from_line = [(0, 0), (0, shard_rows), (1, 0), (1, shard_rows)]
    from_exchange = [(0, 0), (1, 0), (2, 0), (2, shard_rows)]

    attn_piece = placed(info, shard_rows, from_line, attn_joined, attn_two)
    attn_near = topo.swap(attn_piece, square, 0)
    gate_up_one = topo.swap(tie(info, gate_up_send), line, 0)
    attn_in = join(info, attn_own, attn_other)
    q_joined, o_joined = join_split(info, (qkv_cols, q_cols), attn_piece, attn_near)
    q_all = [q_joined, topo.swap(q_joined, square, 1)]
    o_all = [o_joined, topo.swap(o_joined, square, 1)]
    gate_up_two = topo.swap(second_chunks(info, gate_up_keep, gate_up_one), line, 1)

    mixed, linear, mass = attend(
        info, attn_in, q_all, bias_all, cosine, sine, row_info, col_info, q_heads, kv_heads
    )
    down_send, down_keep = cut_columns(info, part, down_weight)
    down_one = topo.swap(down_send, line, 0)
    gate_up_piece = placed(
        info, shard_rows, from_exchange, gate_up_keep, gate_up_one, gate_up_two
    )
    gate_up_near = topo.swap(gate_up_piece, square, 0)
    *other_attn, own_attn = project(info, mixed, o_all, width)
    gate_up_far = topo.swap(gate_up_piece, square, 1)
    other_attn = [topo.other_core(half_rows) for half_rows in other_attn]
    mlp_own, state = state_rows(info, inputs, own_attn, other_attn, gain_two)
    mlp_one = topo.swap(mlp_own, line, 0)

    down_two = topo.swap(second_chunks(info, down_keep, down_one), line, 1)
    mlp_half = join(info, mlp_own, mlp_one)
    mlp_two = topo.swap(mlp_half, line, 1)
    mlp_early = topo.other_core(mlp_half)
    down_piece = placed(info, shard_rows, from_exchange, down_keep, down_one, down_two)
    wait_for(info, gate_up_near, gate_up_far)
    gate_up_last = topo.swap(tie(info, gate_up_near), square, 1)
    down_near = topo.swap(down_piece, square, 0)
    wait_for(info, mlp_two)
    mlp_late = topo.other_core(tie(info, mlp_two))
    grad_out_one = topo.swap(tie(info, out_grad_in), line, 0)
    wait_for(info, gate_up_last)
    gate_up = [gate_up_piece, gate_up_near, gate_up_far, gate_up_last]
    down = [join(info, down_piece, down_near)]
    down.append(topo.swap(down[0], square, 1))
    mlp_in = join(info, mlp_half, mlp_two, mlp_early, mlp_late)
    grad_out_two = topo.swap(tie(info, out_grad_in), line, 1)

    hidden, gate_factor, up_factor = forward(info, mlp_in, gate_up, tile)
    wait_for(info, grad_out_one, grad_out_two)
    grad_out_last = topo.swap(tie(info, grad_out_one), line, 1)
    out_own, out_other = down_sum(info, hidden, down, tile, width)
    out_other = topo.other_core(out_other)
    pair = (0, 1, False), (2, 1, False)
    single = (0, 1, False), (1, 1, False)
    chunks = (0, 2, True), (1, 2, True)
    rows = local_rows
    grad_out_half = join(info, out_grad_in, grad_out_one, grad_out_two, grad_out_last)
    grad_out_all = join(info, grad_out_half, topo.other_core(grad_out_half))
    out_keep, out_send = sum_split(info, rows, 2, *pair, out_own, out_other)
    out_one = topo.swap(out_send, line, 1)
    factors = (grad_out_all, gate_factor, up_factor, gate_up, down)
    back_other, grads_other = backward(info, 1, *factors, tile)
    back_other = [topo.other_core(part_rows) for part_rows in cut_rows(info, back_other, 2)]
    down_grad = functools.partial(grads_of, info, grad_out_all, [hidden], block)
    down_first = topo.swap(down_grad(3), square, 1)
    down_next = topo.swap(down_grad(2), square, 1)
    out_keep, out_send = sum_split(info, rows, 1, *single, out_keep, out_one)
    out_two = topo.swap(out_send, line, 0)
    back_own, grads_own = backward(info, 0, *factors, tile)
    wait_for(info, out_two, down_first, down_next)
    back_keep, back_send = sum_split(info, rows, 2, *pair, back_own, *back_other)
    back_one = topo.swap(back_send, line, 1)
    gate_up_grad = functools.partial(grads_of, info, mlp_in, [grads_own, grads_other], block)
    down_last = topo.swap(down_grad(1, down_first), square, 0)
    gate_up_first = topo.swap(gate_up_grad(3), square, 1)
    gate_up_send = gate_up_grad(2)
    down_kept = down_grad(0, down_next)
    back_keep, back_send = sum_split(info, rows, 1, *single, back_keep, back_one)
    back_two = topo.swap(back_send, line, 0)
    down_keep, down_send = sum_split(info, shard_rows, 2, *chunks, down_kept, down_last)
    gate_up_next = topo.swap(tie(info, gate_up_send), square, 1)
    gate_up_send = gate_up_grad(1, gate_up_first)
    gate_up_last = topo.swap(gate_up_send, square, 0)
    block_out = close_rows(info, state, out_keep, out_two)

    grad_state_low, grad_state, gain_two_grad = norm_back(
        info, state, back_keep, back_two, out_grad_in, gain_two, False
    )
    state_other = topo.other_core(grad_state_low)
    down_one = topo.swap(tie(info, down_send), line, 0)
    grad_state_all = join(info, grad_state_low, state_other)
    grad_linear, bias_grad, own_part, other_part = attend_back(
        info,
        grad_state_all,
        o_all,
        q_all,
        linear,
        mass,
        cosine,
        sine,
        row_info,
        col_info,
        q_heads,
        kv_heads,
    )
    part_other = topo.other_core(other_part)
    down_two = topo.swap(second_chunks(info, down_keep, down_one), line, 1)
    gate_up_kept = gate_up_grad(0, gate_up_next)
    gate_up_keep, gate_up_send = sum_split(
        info, shard_rows, 2, *chunks, gate_up_kept, gate_up_last
    )
    gate_up_one = topo.swap(gate_up_send, line, 0)
    q_full = grads_sent(info, attn_in, grad_linear, block)
    q_got = topo.swap(q_full, square, 1)
    o_full = grads_sent(info, grad_state_all, mixed, block)
    o_got = topo.swap(o_full, square, 1)
    tokens_grad, gain_one_grad = norm_back(
        info, inputs, own_part, part_other, grad_state, gain_one, True
    )
    sums = jnp.concatenate([bias_grad, gain_one_grad, gain_two_grad], axis=1)
    sums = sums.reshape(-1, LANES)
    shared = qkv_cols // LANES
    sums_got = topo.other_core(sums)
    (down_grads,) = columns_out(info, down_keep, down_one, down_two, part, ff_cols)
    sums = sum_rows(info, sums, sums_got, shared)
    sums_got = topo.swap(sums, square, 0)

    gate_up_two = topo.swap(second_chunks(info, gate_up_keep, gate_up_one), line, 1)
    q_kept, q_send = grads_kept(info, attn_in, grad_linear, block, q_got)
    q_last = topo.swap(q_send, square, 0)
    o_kept, o_send = grads_kept(info, grad_state_all, mixed, block, o_got)
    o_last = topo.swap(o_send, square, 0)
    sums = sum_rows(info, sums, sums_got, 0)
    sums_got = topo.swap(sums, square, 1)
    ordered = (0, 1, True), (2, 1, True)
    q_keep, q_send = sum_split(info, shard_rows, 2, *ordered, q_kept, q_last)
    q_one = topo.swap(q_send, line, 1)
    o_keep, o_send = sum_split(info, shard_rows, 2, *ordered, o_kept, o_last)
    o_one = topo.swap(o_send, line, 1)
    sums = sum_rows(info, sums, sums_got, 0)
    sums_got = topo.swap(sums, line, 0)
    q_keep, q_send = sum_split(info, shard_rows, 1, *single, q_keep, q_one)
    q_two = topo.swap(q_send, line, 0)
    sums = sum_rows(info, sums, sums_got, 0)
    sums_got = topo.swap(sums, line, 1)
    o_keep, o_send = sum_split(info, shard_rows, 1, *single, o_keep, o_one)
    o_two = topo.swap(o_send, line, 0)
    gate_grads, up_grads = columns_out(
        info, gate_up_keep, gate_up_one, gate_up_two, part, ff_cols
    )
    q_grads, k_grads, v_grads = sum_out(info, q_keep, q_two, (q_cols, kv_cols, kv_cols))
    (o_grads,) = sum_out(info, o_keep, o_two, (q_cols,))
    sums = sum_rows(info, sums, sums_got, 0).reshape(-1)
    own_bias = sums[:qkv_cols]
    gain_sum = sums[qkv_cols:].reshape(2, width)
    CLOCK[0] = None
    return (
        block_out,
        tokens_grad,
        gain_sum[0],
        q_grads,
        own_bias[:q_cols],
        k_grads,
        own_bias[q_cols : q_cols + kv_cols],
        v_grads,
        own_bias[q_cols + kv_cols :],
        o_grads,
        gain_sum[1],
        gate_grads,
        up_grads,
        down_grads,
    )


def solution(mesh):
    rows = P(("dp", "tensor"), None)
    both = P("dp", "tensor")
    half = P("tensor")
    in_specs = (
        rows, rows, P("dp", None), P(), both, half, both, half, both, half, both, P(), both, both, both,
    )
    out_specs = (
        rows, rows, P(), both, half, both, half, both, half, both, P(), both, both, both,
    )
    fast = mesh.shape["dp"] == LINE * LINE and mesh.shape["tensor"] == 2
    return jax.shard_map(
        per_device if fast else plain_device,
        mesh=mesh,
        in_specs=in_specs,
        out_specs=out_specs,
        check_vma=False,
    )
```

```python
import functools
import math

import jax
import jax.numpy as jnp
from jax import lax
from jax.experimental import pallas as pl
from jax.experimental.pallas import tpu as pltpu
from jax.sharding import PartitionSpec as P

HEAD_DIM = 128
EPSILON = 1e-06
ROPE_BASE = 1000000.0
MASKED = -1e30
LINE = 4
LANES = 128
BF = jnp.bfloat16
F32 = jnp.float32
VMEM_BYTES = 56 * 2**20
ANY = pl.BlockSpec(memory_space=pl.ANY)


def normalize(values):
    factor = lax.rsqrt(jnp.mean(values * values, axis=1, keepdims=True) + EPSILON)
    return (values * factor, factor)


def plain_norm_back(grad_normed, normed, factor, gain_vec):
    scaled = grad_normed * gain_vec[None, :]
    row_inner = jnp.mean(scaled * normed, axis=1, keepdims=True)
    return (factor * (scaled - normed * row_inner), jnp.sum(grad_normed * normed, axis=0))


def rope_tables(positions, width):
    half_width = width // 2
    frequency = jnp.power(ROPE_BASE, -2.0 * jnp.arange(half_width, dtype=F32) / width)
    angles = positions.astype(F32)[:, None] * frequency[None, :]
    return (jnp.cos(angles), jnp.sin(angles))


def rotate(values, cosine_table, sine_table):
    half_width = values.shape[-1] // 2
    lower_half = values[..., :half_width]
    upper_half = values[..., half_width:]
    return jnp.concatenate(
        [
            lower_half * cosine_table - upper_half * sine_table,
            upper_half * cosine_table + lower_half * sine_table,
        ],
        axis=-1,
    )


def unrotate(values, cosine_table, sine_table):
    return rotate(values, cosine_table, -sine_table)


def segment_info(length_row, places):
    seq_ends = jnp.cumsum(length_row)
    starts = seq_ends - length_row
    segment = jnp.sum((places[:, None] >= seq_ends[None, :]).astype(jnp.int32), axis=1)
    slot_ids = jnp.arange(length_row.shape[0], dtype=jnp.int32)
    offset = jnp.sum(jnp.where(segment[:, None] == slot_ids[None, :], starts[None, :], 0), axis=1)
    return (segment, places - offset)


class PlainTopo:
    def __init__(self):
        self.dp = lax.axis_size("dp")
        self.square = self.dp // LINE
        self.me = lax.axis_index("dp")
        self.core = lax.axis_index("tensor")
        self.line_at = self.me // self.square
        self.square_at = self.me % self.square
        line_bits = [self.square << i for i in range(LINE.bit_length() - 1)]
        square_bits = [1 << i for i in range(self.square.bit_length() - 1)]
        self.line = (line_bits, line_bits[::-1])
        self.squares = (square_bits, square_bits[::-1])

    def swap(self, array, bits, phase):
        perm = []
        for place in range(self.dp):
            for core in range(2):
                perm.append((place * 2 + core, (place ^ bits[core][phase]) * 2 + core))
        return lax.ppermute(array, ("dp", "tensor"), perm)

    def other_core(self, array):
        return lax.ppermute(array, "tensor", [(0, 1), (1, 0)])

    def offset(self, bits, index, unit):
        totals = [0, 0]
        for core in range(2):
            for phase, bit in enumerate(bits[core]):
                if index >> phase & 1:
                    totals[core] ^= bit // unit
        return jnp.where(self.core == 0, totals[0], totals[1])

    def gather(self, own, bits):
        pieces = [own]
        for phase in range(len(bits[0])):
            pieces = pieces + [self.swap(piece, bits, phase) for piece in pieces]
        return pieces

    def gather_joined(self, own, bits):
        joined = own
        for phase in range(len(bits[0])):
            joined = jnp.concatenate([joined, self.swap(joined, bits, phase)], axis=0)
        return joined

    def scatter_sum(self, array, bits):
        for phase in reversed(range(len(bits[0]))):
            half = array.shape[0] // 2
            got = self.swap(array[half:], bits, phase)
            array = (array[:half].astype(F32) + got.astype(F32)).astype(BF)
        return array

    def total(self, array):
        for bits in (self.line, self.squares):
            for phase in range(len(bits[0])):
                array = array + self.swap(array, bits, phase)
        return array

    def exchange(self, chunks, bits):
        rows = chunks[0].shape[0]
        held = [chunk for chunk in chunks]
        for phase in range(len(bits[0])):
            step = 1 << phase
            keep = [i for i in range(len(chunks)) if not i & step]
            keep = [i for i in keep if held[i] is not None]
            sent = jnp.concatenate([held[i + step] for i in keep], axis=0)
            got = self.swap(sent, bits, phase)
            parts = jnp.split(got, len(keep), axis=0)
            for i, part in zip(keep, parts):
                held[i] = jnp.concatenate([held[i], part], axis=0)
                held[i + step] = None
        return jnp.split(held[0], len(chunks), axis=0)

    def ordered(self, pieces, bits, unit, at):
        count = len(pieces)
        tables = []
        for core in range(2):
            table = [0] * count
            for index in range(count):
                total = 0
                for phase, bit in enumerate(bits[core]):
                    if index >> phase & 1:
                        total ^= bit // unit
                table[total] = index
            tables.append(table)
        tables = jnp.asarray(tables, jnp.int32)[self.core]
        stacked = jnp.stack(pieces)
        return [
            lax.dynamic_index_in_dim(
                stacked, lax.dynamic_index_in_dim(tables, place ^ at, 0, False), 0, False
            )
            for place in range(count)
        ]


def to_inner(rows, topo):
    count, width = rows.shape
    rest = width // topo.dp
    cut = rows.reshape(count, LINE, topo.square, rest).transpose(2, 0, 1, 3)
    cut = cut.reshape(topo.square, count, LINE * rest)
    return jnp.concatenate(
        [
            lax.dynamic_index_in_dim(cut, topo.square_at ^ i, 0, False)
            for i in range(topo.square)
        ],
        axis=1,
    )


def to_outer(rows, topo):
    count, width = rows.shape
    rest = width // topo.dp
    cut = rows.reshape(count, topo.square, LINE * rest).transpose(1, 0, 2)
    cut = jnp.stack(
        [
            lax.dynamic_index_in_dim(cut, topo.square_at ^ i, 0, False)
            for i in range(topo.square)
        ]
    )
    cut = cut.reshape(topo.square, count, LINE, rest).transpose(1, 2, 0, 3)
    return cut.reshape(count, width)


def dot(left, right):
    return jnp.dot(left, right, preferred_element_type=F32)


def dot_t(left, right):
    return lax.dot_general(left, right, (((1,), (1,)), ((), ())), preferred_element_type=F32)


def t_dot(left, right):
    return lax.dot_general(left, right, (((0,), (0,)), ((), ())), preferred_element_type=F32)


def attention_scores(queries, key_rows, allowed):
    score_scale = 1.0 / math.sqrt(queries.shape[-1])
    raw_scores = jnp.einsum("qgpd,kgd->gpqk", queries, key_rows, preferred_element_type=F32)
    return jnp.where(allowed[None, None], raw_scores * score_scale, MASKED)


def plain_device(
    tokens,
    out_grad,
    lengths,
    attn_gain,
    q_weight,
    q_bias,
    k_weight,
    k_bias,
    v_weight,
    v_bias,
    o_weight,
    mlp_gain,
    gate_weight,
    up_weight,
    down_weight,
):
    topo = PlainTopo()
    local_rows, width = tokens.shape
    group_rows = 2 * local_rows
    q_cols = q_weight.shape[1]
    kv_cols = k_weight.shape[1]
    qkv_cols = q_cols + 2 * kv_cols
    ff_cols = gate_weight.shape[1]
    part = -(-ff_cols // (LINE * LANES)) * LANES
    kv_groups = kv_cols // HEAD_DIM
    per_group = q_cols // HEAD_DIM // kv_groups
    score_scale = 1.0 / math.sqrt(HEAD_DIM)

    def line_gather(shard):
        pieces = jnp.split(topo.gather_joined(shard, topo.line), LINE, axis=0)
        return jnp.concatenate(topo.ordered(pieces, topo.line, topo.square, topo.line_at), axis=0)

    def square_gather(shard):
        pieces = topo.gather(shard, topo.squares)
        return jnp.concatenate(topo.ordered(pieces, topo.squares, 1, 0), axis=0)

    def square_scatter(grads):
        pieces = jnp.split(grads.astype(BF), topo.square, axis=0)
        by_index = topo.ordered(pieces, tuple(b for b in topo.squares), 1, 0)
        return topo.scatter_sum(jnp.concatenate(by_index, axis=0), topo.squares)

    def line_offset(index):
        return topo.line_at ^ topo.offset(topo.line, index, topo.square)

    def columns_in(shards):
        padded = [jnp.pad(s, ((0, 0), (0, LINE * part - ff_cols))) for s in shards]
        chunks = []
        for index in range(LINE):
            start = line_offset(index) * part
            chunks.append(
                jnp.concatenate(
                    [lax.dynamic_slice_in_dim(s, start, part, axis=1) for s in padded], axis=1
                )
            )
        got = topo.exchange(chunks, topo.line)
        return jnp.concatenate(topo.ordered(got, topo.line, topo.square, topo.line_at), axis=0)

    def columns_out(piece, count):
        rows = piece.shape[0] // LINE
        chunks = [
            lax.dynamic_slice_in_dim(piece, line_offset(index) * rows, rows, axis=0)
            for index in range(LINE)
        ]
        got = topo.ordered(
            topo.exchange(chunks, topo.line), topo.line, topo.square, topo.line_at
        )
        return [
            jnp.concatenate([g[:, i * part : (i + 1) * part] for g in got], axis=1)[
                :, :ff_cols
            ].astype(F32)
            for i in range(count)
        ]

    def rows_out(piece):
        rows = piece.shape[0] // LINE
        chunks = [
            lax.dynamic_slice_in_dim(piece, line_offset(index) * rows, rows, axis=0)
            for index in range(LINE)
        ]
        return topo.scatter_sum(jnp.concatenate(chunks, axis=0), topo.line).astype(F32)

    def both_cores(rows):
        return jnp.concatenate([rows, topo.other_core(rows)], axis=0)

    def core_sum(rows):
        half = rows.shape[0] // 2
        return rows[:half] + topo.other_core(rows[half:].astype(BF)).astype(F32)

    def line_tokens(rows):
        return both_cores(topo.gather_joined(rows, topo.line))

    def line_sum(partial):
        return topo.scatter_sum(core_sum(partial).astype(BF), topo.line).astype(F32)

    row_ids = jnp.arange(local_rows, dtype=jnp.int32)
    places = jnp.concatenate(
        [topo.core * local_rows + row_ids, (1 - topo.core) * local_rows + row_ids]
    )
    segment, positions = segment_info(lengths[0], places)
    allowed = (segment[:, None] == segment[None, :]) & (places[None, :] <= places[:, None])
    cosine_table, sine_table = rope_tables(positions, HEAD_DIM)
    q_cosine = cosine_table[:, None, None, :]
    q_sine = sine_table[:, None, None, :]
    k_cosine = cosine_table[:, None, :]
    k_sine = sine_table[:, None, :]

    inputs_low = to_inner(tokens, topo)
    out_grad_low = to_inner(out_grad, topo)
    gains = to_inner(jnp.stack([attn_gain, mlp_gain]), topo).astype(F32)
    gain_one, gain_two = gains[0], gains[1]
    inputs = inputs_low.astype(F32)
    bias_all = jnp.concatenate([q_bias, k_bias, v_bias]).astype(F32)

    qkv_local = jnp.concatenate([q_weight, k_weight, v_weight], axis=1)
    qkv_all = square_gather(line_gather(qkv_local))
    o_all = square_gather(line_gather(o_weight))
    down_all = square_gather(columns_in([down_weight]))
    grad_out_all = line_tokens(out_grad_low)
    gate_up = square_gather(columns_in([gate_weight, up_weight]))

    normed_one, factor_one = normalize(inputs)
    attn_in = both_cores((normed_one * gain_one[None, :]).astype(BF))
    linear = dot(attn_in, qkv_all) + bias_all[None, :]
    queries = rotate(
        linear[:, :q_cols].reshape(group_rows, kv_groups, per_group, HEAD_DIM), q_cosine, q_sine
    ).astype(BF)
    key_rows = rotate(
        linear[:, q_cols : q_cols + kv_cols].reshape(group_rows, kv_groups, HEAD_DIM),
        k_cosine,
        k_sine,
    ).astype(BF)
    values = linear[:, q_cols + kv_cols :].reshape(group_rows, kv_groups, HEAD_DIM).astype(BF)
    scores = attention_scores(queries, key_rows, allowed)
    row_peak = jnp.max(scores, axis=-1, keepdims=True)
    exponent = jnp.exp(scores - row_peak)
    row_mass = jnp.sum(exponent, axis=-1, keepdims=True)
    log_mass = row_peak + jnp.log(row_mass)
    probs_low = (exponent / row_mass).astype(BF)
    mixed_heads = jnp.einsum("gpqk,kgd->qgpd", probs_low, values, preferred_element_type=F32)
    mixed_heads = mixed_heads.reshape(group_rows, q_cols).astype(BF)
    hidden_state = inputs + core_sum(dot_t(mixed_heads, o_all))
    normed_two, factor_two = normalize(hidden_state)

    mlp_in = line_tokens((normed_two * gain_two[None, :]).astype(BF))
    grad_hidden = dot(grad_out_all, down_all)
    gate_up_out = dot(mlp_in, gate_up)
    gate_val = gate_up_out[:, :part]
    up_val = gate_up_out[:, part:]
    sigmoid_gate = jax.nn.sigmoid(gate_val)
    activated = gate_val * sigmoid_gate
    hidden_units = (activated * up_val).astype(BF)
    grad_gate = (
        grad_hidden * up_val * sigmoid_gate * (1.0 + gate_val * (1.0 - sigmoid_gate))
    ).astype(BF)
    grad_up = (grad_hidden * activated).astype(BF)
    grad_gate_up = jnp.concatenate([grad_gate, grad_up], axis=1)
    grad_normed_two = line_sum(dot_t(grad_gate_up, gate_up))
    block_out = (hidden_state + line_sum(dot_t(hidden_units, down_all))).astype(BF)
    gate_grads, up_grads = columns_out(square_scatter(t_dot(mlp_in, grad_gate_up)), 2)
    (down_grads,) = columns_out(square_scatter(t_dot(grad_out_all, hidden_units)), 1)

    back_two, gain_two_grad = plain_norm_back(grad_normed_two, normed_two, factor_two, gain_two)
    grad_state = out_grad_low.astype(F32) + back_two
    grad_state_all = both_cores(grad_state.astype(BF))
    o_grads = rows_out(square_scatter(t_dot(grad_state_all, mixed_heads)))
    grad_mixed = dot(grad_state_all, o_all)
    grad_heads = grad_mixed.astype(BF).reshape(group_rows, kv_groups, per_group, HEAD_DIM)
    scores_again = attention_scores(queries, key_rows, allowed)
    prob_rows = jnp.exp(scores_again - log_mass)
    grad_probs = jnp.einsum("qgpd,kgd->gpqk", grad_heads, values, preferred_element_type=F32)
    row_inner = jnp.sum(prob_rows * grad_probs, axis=-1, keepdims=True)
    grad_scores = (prob_rows * (grad_probs - row_inner) * score_scale).astype(BF)
    grad_values = jnp.einsum(
        "gpqk,qgpd->kgd", prob_rows.astype(BF), grad_heads, preferred_element_type=F32
    )
    grad_queries = jnp.einsum("gpqk,kgd->qgpd", grad_scores, key_rows, preferred_element_type=F32)
    grad_keys = jnp.einsum("gpqk,qgpd->kgd", grad_scores, queries, preferred_element_type=F32)
    grad_linear = jnp.concatenate(
        [
            unrotate(grad_queries, q_cosine, q_sine).reshape(group_rows, q_cols),
            unrotate(grad_keys, k_cosine, k_sine).reshape(group_rows, kv_cols),
            grad_values.reshape(group_rows, kv_cols),
        ],
        axis=1,
    ).astype(BF)
    bias_grad = jnp.sum(grad_linear.astype(F32), axis=0)
    qkv_grads = rows_out(square_scatter(t_dot(attn_in, grad_linear)))
    grad_normed_one = core_sum(dot_t(grad_linear, qkv_all))
    back_one, gain_one_grad = plain_norm_back(grad_normed_one, normed_one, factor_one, gain_one)
    tokens_grad = (grad_state + back_one).astype(BF)
    gain_grads = to_outer(jnp.stack([gain_one_grad, gain_two_grad]), topo)
    gain_grads = gain_grads + topo.other_core(gain_grads)
    small = topo.total(jnp.concatenate([bias_grad, gain_grads.reshape(-1)]).reshape(-1, LANES))
    small = small.reshape(-1)
    own_bias = small[:qkv_cols]
    gain_sum = small[qkv_cols:].reshape(2, width)
    return (
        to_outer(block_out, topo),
        to_outer(tokens_grad, topo),
        gain_sum[0],
        qkv_grads[:, :q_cols],
        own_bias[:q_cols],
        qkv_grads[:, q_cols : q_cols + kv_cols],
        own_bias[q_cols : q_cols + kv_cols],
        qkv_grads[:, q_cols + kv_cols : qkv_cols],
        own_bias[q_cols + kv_cols :],
        o_grads,
        gain_sum[1],
        gate_grads,
        up_grads,
        down_grads,
    )


def nn(left, right):
    return jnp.dot(left, right, preferred_element_type=F32)


def nt(left, right):
    return lax.dot_general(left, right, (((1,), (1,)), ((), ())), preferred_element_type=F32)


def tn(left, right):
    return lax.dot_general(left, right, (((0,), (0,)), ((), ())), preferred_element_type=F32)


def shape(dims, kind):
    return jax.ShapeDtypeStruct(dims, kind)


def whole(dims):
    return pl.BlockSpec(dims, lambda *_: (0,) * len(dims))


OFF, NEIGHBOUR, INDEX, AT, OTHER = 0, 4, 8, 12, 13


class Topo:
    def __init__(self):
        self.dp = lax.axis_size("dp")
        me = lax.axis_index("dp")
        core = lax.axis_index("tensor")
        line_at, square_at = me >> 2, me & 3

        def by_core(index):
            return jnp.where(core == 0, index, (index >> 1) | ((index & 1) << 1))

        self.core = core
        self.square_at = square_at
        self.line = ((LINE, 2 * LINE), (2 * LINE, LINE))
        self.square = ((1, 2), (2, 1))
        count = jnp.arange(LINE, dtype=jnp.int32)
        self.info = jnp.concatenate(
            [
                by_core(count),
                line_at ^ by_core(count),
                by_core(line_at ^ count),
                jnp.stack([square_at, 1 - core]),
            ]
        ).astype(jnp.int32)

    def swap(self, array, bits, phase):
        perm = []
        for place in range(self.dp):
            for core in range(2):
                flip = bits[core][phase] if phase < 2 else bits[core][0] ^ bits[core][1]
                perm.append((place * 2 + core, (place ^ flip) * 2 + core))
        return lax.ppermute(array, ("dp", "tensor"), perm)

    def other_core(self, array):
        return lax.ppermute(array, "tensor", [(0, 1), (1, 0)])

    def both_ways(self, array):
        return lax.all_to_all(array, "tensor", 0, 0, tiled=True)


CLOCK = [None]
TOKEN = jax.ShapeDtypeStruct((8, 128), F32)
IN_VMEM = pl.BlockSpec(memory_space=pltpu.VMEM)
IN_SMEM = pl.BlockSpec(memory_space=pltpu.SMEM)


def in_order(body, ins, outs):
    taken = 0 if CLOCK[0] is None else 1

    def full(*refs):
        body(*refs[:ins], *refs[ins + taken : ins + taken + outs], *refs[ins + taken + outs + 1 :])

    return full


def run(kernel, single, args):
    taken = [] if CLOCK[0] is None else [CLOCK[0]]
    *out, CLOCK[0] = kernel(*args, *taken)
    return out[0] if single else out


def as_list(value):
    return list(value) if isinstance(value, (list, tuple)) else [value]


def call(body, grid, in_specs, out_specs, out_shape, scratch, info, *args, mib=32):
    outs = as_list(out_shape)
    late = 0 if CLOCK[0] is None else 1
    kernel = pl.pallas_call(
        in_order(body, 1 + len(in_specs), len(outs)),
        grid_spec=pltpu.PrefetchScalarGridSpec(
            num_scalar_prefetch=1,
            grid=grid,
            in_specs=list(in_specs) + [IN_VMEM] * late,
            out_specs=as_list(out_specs) + [IN_VMEM],
            scratch_shapes=list(scratch),
        ),
        out_shape=outs + [TOKEN],
        compiler_params=pltpu.CompilerParams(vmem_limit_bytes=mib * 2**20),
        cost_estimate=pl.CostEstimate(flops=1000, bytes_accessed=1000, transcendentals=0),
        name=body.__qualname__.split(".")[0],
    )
    return run(kernel, not isinstance(out_shape, (list, tuple)), (info,) + args)


def small(body, out_shape, scratch, info, *args, mib=10, out_spec=IN_VMEM):
    outs = as_list(out_shape)
    late = 0 if CLOCK[0] is None else 1
    kernel = pl.pallas_call(
        in_order(body, 1 + len(args), len(outs)),
        in_specs=[IN_SMEM] + [IN_VMEM] * (len(args) + late),
        out_specs=[out_spec] * len(outs) + [IN_VMEM],
        scratch_shapes=list(scratch),
        out_shape=outs + [TOKEN],
        compiler_params=pltpu.CompilerParams(vmem_limit_bytes=mib * 2**20),
        cost_estimate=pl.CostEstimate(flops=1000, bytes_accessed=1000, transcendentals=0),
        name=body.__qualname__.split(".")[0],
    )
    return run(kernel, not isinstance(out_shape, (list, tuple)), (info,) + args)


def tie(info, array):
    def body(info_ref, in_ref, out_ref):
        out_ref[...] = in_ref[...]

    return small(body, shape(array.shape, array.dtype), [], info, array)


def spacer(info, topo, array):
    wait_for(info, topo.other_core(tie(info, array)))


def wait_for(info, *arrays):
    def body(*refs):
        del refs

    late = 0 if CLOCK[0] is None else 1
    kernel = pl.pallas_call(
        body,
        in_specs=[ANY] * len(arrays) + [IN_VMEM] * late,
        out_specs=[IN_VMEM],
        out_shape=[TOKEN],
        compiler_params=pltpu.CompilerParams(vmem_limit_bytes=16 * 2**20),
        cost_estimate=pl.CostEstimate(flops=1, bytes_accessed=1, transcendentals=0),
        name="wait_for",
    )
    (CLOCK[0],) = kernel(*arrays, *([CLOCK[0]] if late else []))


def join(info, *args):
    def body(info_ref, *refs):
        start = 0
        for ref in refs[:-1]:
            refs[-1][start : start + ref.shape[0]] = ref[...]
            start += ref.shape[0]

    rows = sum(a.shape[0] for a in args)
    return small(body, shape((rows,) + args[0].shape[1:], args[0].dtype), [], info, *args)


def join_far(info, *args):
    def body(info_ref, *refs):
        ins, out, sems = refs[: len(args)], refs[len(args)], refs[-1]
        start = 0
        copies = []
        for index, ref in enumerate(ins):
            rows = ref.shape[0]
            copies.append(
                pltpu.make_async_copy(ref, out.at[pl.ds(start, rows)], sems.at[index])
            )
            start += rows
        for copy in copies:
            copy.start()
        for copy in copies:
            copy.wait()

    rows = sum(a.shape[0] for a in args)
    return small(
        body,
        shape((rows,) + args[0].shape[1:], args[0].dtype),
        [pltpu.SemaphoreType.DMA((len(args),))],
        info,
        *args,
        out_spec=ANY,
    )


def join_split(info, widths, *args):
    rows = sum(a.shape[0] for a in args)

    def body(info_ref, *refs):
        ins, outs = refs[: len(args)], refs[len(args) :]
        low = 0
        for ref in ins:
            start = 0
            for out, cols in zip(outs, widths):
                out[low : low + ref.shape[0]] = ref[:, start : start + cols]
                start += cols
            low += ref.shape[0]

    return small(body, [shape((rows, cols), BF) for cols in widths], [], info, *args)


def beside(info, *args):
    def body(info_ref, *refs):
        start = 0
        for ref in refs[:-1]:
            refs[-1][:, start : start + ref.shape[1]] = ref[...]
            start += ref.shape[1]

    cols = sum(a.shape[1] for a in args)
    return small(body, shape((args[0].shape[0], cols), args[0].dtype), [], info, *args)


def placed(info, rows, takes, *args):
    def body(info_ref, *refs):
        for index, (which, start) in enumerate(takes):
            target = pl.multiple_of(info_ref[NEIGHBOUR + index] * rows, 16)
            refs[-1][pl.ds(target, rows)] = refs[which][start : start + rows]

    return small(body, shape((LINE * rows, args[0].shape[1]), BF), [], info, *args)


def second_chunks(info, kept, got):
    rows = kept.shape[0] // 2

    def body(info_ref, kept_ref, got_ref, out_ref):
        out_ref[:rows] = kept_ref[rows:]
        out_ref[rows:] = got_ref[rows:]

    return small(body, shape(kept.shape, BF), [], info, kept, got)


def cut_columns(info, part, *weights):
    count = len(weights)
    rows, cols = weights[0].shape
    short = cols - (LINE - 1) * part

    def body(info_ref, *refs):
        ins, outs = refs[:count], refs[count:]
        for index in range(LINE):
            at = info_ref[NEIGHBOUR + index]
            out = outs[1 - index % 2]
            low = index // 2 * rows
            for which, ref in enumerate(ins):
                start = pl.multiple_of(at * part, LANES)
                first = which * part
                out[low : low + rows, first : first + short] = ref[:, pl.ds(start, short)]
                if short < part:
                    rest = pl.multiple_of(jnp.minimum(at, LINE - 2) * part + short, LANES)
                    tail = ref[:, pl.ds(rest, part - short)]
                    out[low : low + rows, first + short : first + part] = jnp.where(
                        at < LINE - 1, tail, jnp.zeros_like(tail)
                    )

    return small(body, [shape((2 * rows, count * part), BF)] * 2, [], info, *weights)


def square_blocks(info_ref, pieces, width):
    rows = width // LINE
    index = 0
    for piece in pieces:
        for block in range(piece.shape[0] // rows):
            start = pl.multiple_of(info_ref[OFF + index] * rows, LANES)
            yield pl.ds(start, rows), piece[block * rows : (block + 1) * rows]
            index += 1


def inward(values, at, store):
    width = values.shape[1]
    block = width // LINE
    rest = block // LINE
    for square in range(LINE):
        parts = [
            values[:, line * block + square * rest : line * block + (square + 1) * rest]
            for line in range(LINE)
        ]
        start = pl.multiple_of((square ^ at) * block, LANES)
        store(pl.ds(start, block), jnp.concatenate(parts, axis=1))


def outward(ref, at):
    width = ref.shape[1]
    block = width // LINE
    rest = block // LINE
    blocks = []
    for square in range(LINE):
        start = pl.multiple_of((square ^ at) * block, LANES)
        blocks.append(ref[:, pl.ds(start, block)])
    parts = []
    for line in range(LINE):
        for square in range(LINE):
            parts.append(blocks[square][:, line * rest : (line + 1) * rest])
    return jnp.concatenate(parts, axis=1)


def turn_rows(info, rows):
    def body(info_ref, rows_ref, out_ref, held):
        def store(cols, block):
            held[:, cols] = block

        inward(rows_ref[...].astype(F32), info_ref[AT], store)
        out_ref[...] = held[...].astype(BF)

    return small(body, shape(rows.shape, BF), [pltpu.VMEM(rows.shape, F32)], info, rows)


def open_rows(info, rows, gains):
    def body(info_ref, rows_ref, gains_ref, out_ref, in_ref, gain_ref, held):
        def store_gain(cols, block):
            gain_ref[:, cols] = block

        def store(cols, block):
            held[:, cols] = block

        inward(gains_ref[...], info_ref[AT], store_gain)
        inward(rows_ref[...].astype(F32), info_ref[AT], store)
        values = held[...]
        in_ref[...] = values.astype(BF)
        factor = lax.rsqrt(jnp.mean(values * values, axis=1, keepdims=True) + EPSILON)
        out_ref[...] = (values * factor * gain_ref[0:1, :]).astype(BF)

    return small(
        body,
        [shape(rows.shape, BF), shape(rows.shape, BF), shape(gains.shape, F32)],
        [pltpu.VMEM(rows.shape, F32)],
        info,
        rows,
        gains,
    )


def state_rows(info, rows, own, got, gain):
    def body(info_ref, rows_ref, own_ref, early_ref, late_ref, gain_ref, out_ref, state_ref):
        half = dims[0] // 2
        for start, got_ref in ((0, early_ref), (half, late_ref)):
            span = pl.ds(start, half)
            values = rows_ref[span].astype(F32) + (own_ref[span] + got_ref[...].astype(F32))
            state_ref[span] = values
            factor = lax.rsqrt(jnp.mean(values * values, axis=1, keepdims=True) + EPSILON)
            out_ref[span] = (values * factor * gain_ref[...]).astype(BF)

    dims = rows.shape
    return small(
        body, [shape(dims, BF), shape(dims, F32)], [], info, rows, own, *got, gain
    )


def close_rows(info, state, own, got):
    def body(info_ref, state_ref, own_ref, got_ref, out_ref, held):
        held[...] = state_ref[...] + (own_ref[...].astype(F32) + got_ref[...].astype(F32))
        out_ref[...] = outward(held, info_ref[AT]).astype(BF)

    dims = state.shape
    return small(
        body,
        shape(dims, BF),
        [pltpu.VMEM(dims, F32)],
        info,
        state,
        own,
        got,
    )


def norm_back(info, values, own, got, base, gain, turn):
    def body(info_ref, values_ref, own_ref, got_ref, base_ref, gain_ref, *refs):
        values = values_ref[...].astype(F32)
        factor = lax.rsqrt(jnp.mean(values * values, axis=1, keepdims=True) + EPSILON)
        normed = values * factor
        grad = own_ref[...].astype(F32) + got_ref[...].astype(F32)
        scaled = grad * gain_ref[...]
        row_inner = jnp.mean(scaled * normed, axis=1, keepdims=True)
        total = base_ref[...].astype(F32) + factor * (scaled - normed * row_inner)
        gain_grad = jnp.sum(grad * normed, axis=0, keepdims=True)
        if turn:
            out_ref, gain_out_ref, held, gain_held = refs
            held[...] = total
            out_ref[...] = outward(held, info_ref[AT]).astype(BF)
        else:
            low_ref, out_ref, gain_out_ref, gain_held = refs
            out_ref[...] = total
            low_ref[...] = total.astype(BF)
        gain_held[...] = gain_grad
        gain_out_ref[...] = outward(gain_held, info_ref[AT])

    dims = values.shape
    kinds = (BF,) if turn else (BF, F32)
    return small(
        body,
        [shape(dims, kind) for kind in kinds] + [shape(gain.shape, F32)],
        ([pltpu.VMEM(dims, F32)] if turn else []) + [pltpu.VMEM(gain.shape, F32)],
        info,
        values,
        own,
        got,
        base,
        gain,
    )


def turned(values, cosine, sine):
    return values * cosine + pltpu.roll(values, HEAD_DIM // 2, 1) * sine


def attend(info, rows, pieces, bias, cosine, sine, row_info, col_info, q_heads, kv_heads):
    count, cols = len(pieces), pieces[0].shape[1]
    group, width = rows.shape
    q_cols = q_heads * HEAD_DIM

    def body(info_ref, in_ref, *refs):
        pieces = refs[:count]
        bias_ref, cos_ref, sin_ref, row_ref, col_ref = refs[count : count + 5]
        mixed_ref, lin_ref, mass_ref = refs[count + 5 :]
        cosine, sine = cos_ref[...], sin_ref[...]
        scale = 1.0 / math.sqrt(HEAD_DIM)
        linear = bias_ref[...]
        for cols, piece in square_blocks(info_ref, pieces, width):
            linear = linear + nn(in_ref[:, cols], piece)
        for head in range(q_heads + 2 * kv_heads):
            cols = slice(head * HEAD_DIM, (head + 1) * HEAD_DIM)
            part = linear[:, cols]
            if head < q_heads + kv_heads:
                part = turned(part, cosine, sine)
            lin_ref[:, cols] = part.astype(BF)
        allowed = (row_ref[:, 0:1] <= col_ref[...]) & (col_ref[...] <= row_ref[:, 1:2])
        for head in range(q_heads):
            key = q_heads + head // (q_heads // kv_heads)
            value = key + kv_heads
            cols = slice(head * HEAD_DIM, (head + 1) * HEAD_DIM)
            raw = nt(lin_ref[:, cols], lin_ref[:, key * HEAD_DIM : (key + 1) * HEAD_DIM])
            scores = jnp.where(allowed, raw * scale, MASKED)
            peak = jnp.max(scores, axis=1, keepdims=True)
            exponent = jnp.exp(scores - peak)
            mass = jnp.sum(exponent, axis=1, keepdims=True)
            mass_ref[:, head : head + 1] = peak + jnp.log(mass)
            probs = (exponent * (1.0 / mass)).astype(BF)
            mixed_ref[:, cols] = nn(
                probs, lin_ref[:, value * HEAD_DIM : (value + 1) * HEAD_DIM]
            ).astype(BF)

    plain = (bias, cosine, sine, row_info, col_info)
    return small(
        body,
        [shape((group, q_cols), BF), shape((group, cols), BF), shape((group, LANES), F32)],
        [],
        info,
        rows,
        *pieces,
        *plain,
        mib=20,
    )


def project(info, rows, pieces, width):
    count, cols = len(pieces), pieces[0].shape[1]
    half = rows.shape[0] // 2

    def body(info_ref, in_ref, *refs):
        pieces = refs[:count]
        early_ref, late_ref, own_ref = refs[count:]
        for cols, piece in square_blocks(info_ref, pieces, width):
            both = nt(in_ref[...], piece)
            own_ref[:, cols] = both[:half]
            early_ref[:, cols] = both[half : half + half // 2].astype(BF)
            late_ref[:, cols] = both[half + half // 2 :].astype(BF)

    return small(
        body,
        [shape((half // 2, width), BF)] * 2 + [shape((half, width), F32)],
        [],
        info,
        rows,
        *pieces,
    )


def attend_back(
    info, state, o_pieces, pieces, linear, mass, cosine, sine, row_info, col_info, q_heads, kv_heads
):
    count, cols = len(pieces), pieces[0].shape[1]
    group, width = state.shape
    q_cols = q_heads * HEAD_DIM
    half = group // 2

    def body(info_ref, state_ref, *refs):
        o_refs, q_refs = refs[:count], refs[count : 2 * count]
        lin_ref, mass_ref, cos_ref, sin_ref, row_ref, col_ref = refs[2 * count : 2 * count + 6]
        grad_ref, bias_ref, own_ref, other_ref = refs[2 * count + 6 : 2 * count + 10]
        heads_ref = refs[-1]
        cosine, sine = cos_ref[...], -sin_ref[...]
        scale = 1.0 / math.sqrt(HEAD_DIM)
        heads = 0.0
        for cols, piece in square_blocks(info_ref, o_refs, width):
            heads = heads + nn(state_ref[:, cols], piece)
        heads_ref[...] = heads.astype(BF)
        allowed = (row_ref[:, 0:1] <= col_ref[...]) & (col_ref[...] <= row_ref[:, 1:2])
        per_group = q_heads // kv_heads
        for place in range(kv_heads):
            key_cols = slice((q_heads + place) * HEAD_DIM, (q_heads + place + 1) * HEAD_DIM)
            first = q_heads + kv_heads + place
            value_cols = slice(first * HEAD_DIM, (first + 1) * HEAD_DIM)
            keys, values = lin_ref[:, key_cols], lin_ref[:, value_cols]
            grad_keys, grad_values = 0.0, 0.0
            for head in range(place * per_group, (place + 1) * per_group):
                cols = slice(head * HEAD_DIM, (head + 1) * HEAD_DIM)
                queries, grads = lin_ref[:, cols], heads_ref[:, cols]
                scores = jnp.where(allowed, nt(queries, keys) * scale, MASKED)
                probs = jnp.exp(scores - mass_ref[:, head : head + 1])
                grad_probs = nt(grads, values)
                inner = jnp.sum(probs * grad_probs, axis=1, keepdims=True)
                grad_scores = (probs * (grad_probs - inner) * scale).astype(BF)
                grad_values += tn(probs.astype(BF), grads)
                grad_keys += tn(grad_scores, queries)
                grad_ref[:, cols] = turned(nn(grad_scores, keys), cosine, sine).astype(BF)
            grad_ref[:, key_cols] = turned(grad_keys, cosine, sine).astype(BF)
            grad_ref[:, value_cols] = grad_values.astype(BF)
        bias_ref[...] = jnp.sum(grad_ref[...].astype(F32), axis=0, keepdims=True)
        for cols, piece in square_blocks(info_ref, q_refs, width):
            both = nt(grad_ref[...], piece)
            own_ref[:, cols] = both[:half]
            other_ref[:, cols] = both[half:].astype(BF)

    plain = (linear, mass, cosine, sine, row_info, col_info)
    return small(
        body,
        [
            shape((group, cols), BF),
            shape((1, cols), F32),
            shape((half, width), F32),
            shape((half, width), BF),
        ],
        [pltpu.VMEM((group, q_cols), BF)],
        info,
        state,
        *o_pieces,
        *pieces,
        *plain,
        mib=24,
    )


def in_square(info, pieces, width):
    def body(info_ref, *refs):
        for rows, block in square_blocks(info_ref, refs[:-1], width):
            refs[-1][rows] = block

    return small(body, shape((width, pieces[0].shape[1]), BF), [], info, *pieces)


def forward(info, x, gate_up, tile, step=256):
    part = gate_up.shape[1] // 2
    total, width = x.shape
    spans = [(low, min(low + step, part)) for low in range(0, part, step)]

    def body(info_ref, x_ref, weight, hid_ref, gate_ref, up_ref):
        x = x_ref[...]
        for low, high in spans:
            gate = nn(x, weight[:, low:high])
            up = nn(x, weight[:, part + low : part + high])
            share = 1.0 / (1.0 + jnp.exp(-gate))
            active = gate * share
            hid_ref[:, low:high] = (active * up).astype(BF)
            gate_ref[:, low:high] = (up * share * (1.0 + gate * (1.0 - share))).astype(BF)
            up_ref[:, low:high] = active.astype(BF)

    return call(
        body,
        (total // tile,),
        [pl.BlockSpec((tile, width), lambda i, _: (i, 0)), IN_VMEM],
        [pl.BlockSpec((tile, part), lambda i, _: (i, 0))] * 3,
        [shape((total, part), BF)] * 3,
        [],
        info,
        x,
        gate_up,
        mib=16,
    )


def halves_spec(tile, width, steps, spread):
    half = steps // 2

    def later(i, info_ref):
        first = info_ref[OTHER] * half if spread else 0
        return (first + jnp.maximum(i - half, 0), 0)

    return [
        pl.BlockSpec((tile, width), lambda i, _: (jnp.minimum(i, half - 1), 0)),
        pl.BlockSpec((tile, width), later),
    ]


def cut_rows(info, array, count):
    rows = array.shape[0] // count

    def body(info_ref, in_ref, *outs):
        for index, out in enumerate(outs):
            out[...] = in_ref[index * rows : (index + 1) * rows]

    return small(body, [shape((rows, array.shape[1]), array.dtype)] * count, [], info, array)


def store_half(value, steps, first_ref, second_ref):
    early = pl.program_id(0) < steps // 2

    @pl.when(early)
    def _():
        first_ref[...] = value

    @pl.when(jnp.logical_not(early))
    def _():
        second_ref[...] = value


def down_sum(info, hidden, down, tile):
    width = down.shape[0]
    total, part = hidden.shape
    steps = total // tile

    def body(info_ref, hid_ref, weight, own_ref, other_ref):
        value = nt(hid_ref[...], weight[...]).astype(BF)
        store_half(value, steps, own_ref, other_ref)

    return call(
        body,
        (steps,),
        [pl.BlockSpec((tile, part), lambda i, _: (i, 0)), IN_VMEM],
        halves_spec(tile, width, steps, False),
        [shape((total // 2, width), BF)] * 2,
        [],
        info,
        hidden,
        down,
        mib=14,
    )


def backward(info, half, g, gate_factor, up_factor, gate_up, down, tile, step=256):
    part = down.shape[1]
    total, width = g.shape[0] // 2, g.shape[1]
    steps = total // tile
    spans = [(low, min(low + step, part)) for low in range(0, part, step)]

    def body(info_ref, g_ref, gate_ref, up_ref, gate_up_ref, down_ref, grad_ref, *back_refs):
        g = g_ref[...]
        for low, high in spans:
            grad = nn(g, down_ref[:, low:high])
            grad_ref[:, low:high] = (grad * gate_ref[:, low:high].astype(F32)).astype(BF)
            grad_ref[:, part + low : part + high] = (
                grad * up_ref[:, low:high].astype(F32)
            ).astype(BF)
        value = nt(grad_ref[...], gate_up_ref[...]).astype(BF)
        for number, back_ref in enumerate(back_refs):

            @pl.when(pl.program_id(0) == number)
            def _(back_ref=back_ref):
                back_ref[...] = value

    return call(
        body,
        (steps,),
        [pl.BlockSpec((tile, cols), lambda i, _: (half * steps + i, 0)) for cols in (width, part, part)]
        + [IN_VMEM] * 2,
        [pl.BlockSpec((tile, 2 * part), lambda i, _: (i, 0))] + [whole((tile, width))] * steps,
        [shape((total, 2 * part), BF)] + [shape((tile, width), BF)] * steps,
        [],
        info,
        g,
        gate_factor,
        up_factor,
        gate_up,
        down,
        mib=22,
    )


def rows_spec(block, rights, where):
    rows = rights[0].shape[0]
    return [
        pl.BlockSpec((rows, block), lambda i, info_ref, r=r: (r, info_ref[OFF + where(i)]))
        for r in range(len(rights))
    ]


def grads_of(info, left, rights, block, index, got=None, share=None):
    rows, cols = rights[0].shape
    parts = len(rights)
    cols = cols if share is None else cols // 2
    tile = next(t for t in (768, 512, 384, 256, 128) if cols % t == 0)
    first = 0 if share is None else share * (cols // tile)

    def body(info_ref, *refs):
        value = 0.0
        for r in range(parts):
            value = value + tn(refs[r][...], refs[parts + r][...])
        if got is not None:
            value = value + refs[2 * parts][...].astype(F32)
        refs[-1][...] = value.astype(BF)

    out = pl.BlockSpec((block, tile), lambda i, _: (0, i))
    taken = pl.BlockSpec((block, tile), lambda i, _: (0, first + i))
    return call(
        body,
        (cols // tile,),
        rows_spec(block, rights, lambda i: index)
        + [pl.BlockSpec((rows, tile), lambda i, _: (0, first + i))] * parts
        + ([] if got is None else [taken]),
        out,
        shape((block, cols), BF),
        [],
        info,
        *([left] * parts),
        *rights,
        *([] if got is None else [got]),
        mib=16,
    )


def grads_sent(info, left, right, block):
    total, cols = right.shape

    def body(info_ref, left_ref, right_ref, out_ref):
        out_ref[...] = tn(left_ref[...], right_ref[...]).astype(BF)

    return call(
        body,
        (2,),
        rows_spec(block, [right], lambda i: 2 + i) + [whole(right.shape)],
        pl.BlockSpec((block, cols), lambda i, _: (i, 0)),
        shape((2 * block, cols), BF),
        [],
        info,
        left,
        right,
        mib=16,
    )


def grads_kept(info, left, right, block, got):
    total, cols = right.shape

    def body(info_ref, left_ref, right_ref, got_ref, keep_ref, send_ref):
        value = (tn(left_ref[...], right_ref[...]) + got_ref[...].astype(F32)).astype(BF)
        store_half(value, 2, keep_ref, send_ref)

    return call(
        body,
        (2,),
        rows_spec(block, [right], lambda i: i)
        + [whole(right.shape), pl.BlockSpec((block, cols), lambda i, _: (i, 0))],
        [whole((block, cols))] * 2,
        [shape((block, cols), BF)] * 2,
        [],
        info,
        left,
        right,
        got,
        mib=16,
    )


def sum_split(info, block, count, keep_at, send_at, lefts, rights):
    cols = lefts[0].shape[1]
    pieces = len(lefts)
    wide = rights[0].shape[1]
    sizes = (lefts[0].shape[0], rights[0].shape[0])

    def rows_of(refs, size, low, high):
        which = low // size
        return refs[which][low - which * size : high - which * size].astype(F32)

    def body(info_ref, *refs):
        ins, outs = refs[:-2], refs[-2:]
        left_refs, right_refs = ins[:pieces], ins[pieces:]
        for out, (first, stride, along) in zip(outs, (keep_at, send_at)):
            for step in range(count):
                index = first + stride * step
                if along:
                    rows = pl.ds(pl.multiple_of(info_ref[NEIGHBOUR + index] * block, 16), block)
                    for number, right in enumerate(right_refs):
                        span = slice(number * wide, (number + 1) * wide)
                        total = left_refs[0][rows, span].astype(F32) + right[rows].astype(F32)
                        out[step * block : (step + 1) * block, span] = total.astype(BF)
                    continue
                low, high = index * block, (index + 1) * block
                while low < high:
                    end = min([high] + [(low // size + 1) * size for size in sizes])
                    total = rows_of(left_refs, sizes[0], low, end)
                    total = total + rows_of(right_refs, sizes[1], low, end)
                    start = step * block + low - index * block
                    out[start : start + end - low] = total.astype(BF)
                    low = end

    return small(
        body, [shape((count * block, cols), BF)] * 2, [], info, *lefts, *rights
    )


def sum_out(info, left, right, widths):
    rows = left.shape[0]

    def body(info_ref, left_ref, right_ref, *outs):
        total = left_ref[...].astype(F32) + right_ref[...].astype(F32)
        start = 0
        for out, cols in zip(outs, widths):
            out[...] = total[:, start : start + cols]
            start += cols

    return small(
        body,
        [shape((rows, cols), F32) for cols in widths],
        [],
        info,
        left,
        right,
    )


def sum_rows(info, own, got, first):
    def body(info_ref, own_ref, got_ref, out_ref):
        if first:
            out_ref[:first] = own_ref[:first]
        out_ref[first:] = own_ref[first:] + got_ref[first:]

    return small(body, shape(own.shape, F32), [], info, own, got)


def columns_out(info, kept, got, last, part, cols):
    rows = kept.shape[0] // 2
    count = kept.shape[1] // part

    def body(info_ref, kept_ref, got_ref, last_ref, *outs):
        pieces = [kept_ref[:rows], got_ref[:rows], last_ref[:rows], last_ref[rows:]]
        for place in range(LINE):
            low = place * part
            span = min(part, cols - low)
            for index, piece in enumerate(pieces):

                @pl.when(info_ref[INDEX + place] == index)
                def _(piece=piece, low=low, span=span):
                    for which, out in enumerate(outs):
                        start = which * part
                        out[:, low : low + span] = piece[:, start : start + span].astype(F32)

    return small(
        body,
        [shape((rows, cols), F32)] * count,
        [],
        info,
        kept,
        got,
        last,
    )


def sequence_info(length_row, places):
    seq_ends = jnp.cumsum(length_row)
    starts = seq_ends - length_row
    inside = (places[:, None] >= starts[None, :]) & (places[:, None] < seq_ends[None, :])
    return jnp.sum(jnp.where(inside, starts[None, :], 0), axis=1)


def per_device(
    tokens,
    out_grad,
    lengths,
    attn_gain,
    q_weight,
    q_bias,
    k_weight,
    k_bias,
    v_weight,
    v_bias,
    o_weight,
    mlp_gain,
    gate_weight,
    up_weight,
    down_weight,
):
    CLOCK[0] = None
    topo = Topo()
    info = topo.info
    line, square = topo.line, topo.square
    local_rows, width = tokens.shape
    shard_rows = q_weight.shape[0]
    block = width // LINE
    q_cols = q_weight.shape[1]
    kv_cols = k_weight.shape[1]
    qkv_cols = q_cols + 2 * kv_cols
    ff_cols = gate_weight.shape[1]
    part = -(-ff_cols // (LINE * LANES)) * LANES
    q_heads, kv_heads = q_cols // HEAD_DIM, kv_cols // HEAD_DIM
    tile = local_rows * LINE // 2

    attn_own_weight = beside(info, q_weight, k_weight, v_weight, o_weight)
    attn_one = topo.swap(attn_own_weight, line, 0)
    gate_up_send, gate_up_keep = cut_columns(info, part, gate_weight, up_weight)

    attn_joined = join(info, attn_own_weight, attn_one)
    attn_two = topo.swap(attn_joined, line, 1)
    bias_all = jnp.concatenate([q_bias, k_bias, v_bias]).astype(F32)[None, :]
    gains = jnp.stack([attn_gain, mlp_gain]).astype(F32)
    attn_own, inputs, gains = open_rows(info, tokens, gains)
    gain_one, gain_two = gains[0:1], gains[1:2]
    attn_other = topo.other_core(attn_own)
    out_grad_in = turn_rows(info, out_grad)
    row_ids = jnp.arange(local_rows, dtype=jnp.int32)
    places = jnp.concatenate(
        [topo.core * local_rows + row_ids, (1 - topo.core) * local_rows + row_ids]
    )
    starts = sequence_info(lengths[0], places)
    frequency = jnp.power(ROPE_BASE, -2.0 * jnp.arange(HEAD_DIM // 2, dtype=F32) / HEAD_DIM)
    angles = (places - starts).astype(F32)[:, None] * frequency[None, :]
    cosine_half, sine_half = jnp.cos(angles), jnp.sin(angles)
    cosine = jnp.concatenate([cosine_half, cosine_half], axis=1)
    sine = jnp.concatenate([-sine_half, sine_half], axis=1)
    row_info = jnp.stack([starts, places], axis=1)
    col_info = places[None, :]
    from_line = [(0, 0), (0, shard_rows), (1, 0), (1, shard_rows)]
    from_exchange = [(0, 0), (1, 0), (2, 0), (2, shard_rows)]

    attn_piece = placed(info, shard_rows, from_line, attn_joined, attn_two)
    attn_near = topo.swap(attn_piece, square, 0)
    gate_up_one = topo.swap(tie(info, gate_up_send), line, 0)
    attn_in = join(info, attn_own, attn_other)
    q_joined, o_joined = join_split(info, (qkv_cols, q_cols), attn_piece, attn_near)
    q_all = [q_joined, topo.swap(q_joined, square, 1)]
    o_all = [o_joined, topo.swap(o_joined, square, 1)]
    gate_up_two = topo.swap(second_chunks(info, gate_up_keep, gate_up_one), line, 1)

    mixed, linear, mass = attend(
        info, attn_in, q_all, bias_all, cosine, sine, row_info, col_info, q_heads, kv_heads
    )
    down_send, down_keep = cut_columns(info, part, down_weight)
    down_one = topo.swap(down_send, line, 0)
    gate_up_piece = placed(
        info, shard_rows, from_exchange, gate_up_keep, gate_up_one, gate_up_two
    )
    gate_up_near = topo.swap(gate_up_piece, square, 0)
    *other_attn, own_attn = project(info, mixed, o_all, width)
    gate_up_far = topo.swap(gate_up_piece, square, 1)
    other_attn = [topo.other_core(half_rows) for half_rows in other_attn]
    mlp_own, state = state_rows(info, inputs, own_attn, other_attn, gain_two)
    mlp_one = topo.swap(mlp_own, line, 0)

    down_two = topo.swap(second_chunks(info, down_keep, down_one), line, 1)
    mlp_half = join(info, mlp_own, mlp_one)
    mlp_two = topo.swap(mlp_half, line, 1)
    mlp_early = topo.other_core(mlp_half)
    down_piece = placed(info, shard_rows, from_exchange, down_keep, down_one, down_two)
    wait_for(info, gate_up_near, gate_up_far)
    gate_up_last = topo.swap(tie(info, gate_up_near), square, 1)
    down_near = topo.swap(down_piece, square, 0)
    wait_for(info, mlp_two)
    mlp_late = topo.other_core(tie(info, mlp_two))
    grad_out_one = topo.swap(tie(info, out_grad_in), line, 0)
    wait_for(info, gate_up_last)
    gate_up = in_square(
        info, [gate_up_piece, gate_up_near, gate_up_far, gate_up_last], width
    )
    down = [join(info, down_piece, down_near)]
    down.append(topo.swap(down[0], square, 1))
    mlp_in = join(info, mlp_half, mlp_two, mlp_early, mlp_late)
    grad_out_two = topo.swap(tie(info, out_grad_in), line, 1)

    hidden, gate_factor, up_factor = forward(info, mlp_in, gate_up, tile)
    wait_for(info, grad_out_one, grad_out_two)
    grad_out_last = topo.swap(tie(info, grad_out_one), line, 1)
    down = in_square(info, down, width)
    out_own, out_other = down_sum(info, hidden, down, tile)
    out_other = [topo.other_core(part_rows) for part_rows in cut_rows(info, out_other, 2)]
    pair = (0, 1, False), (2, 1, False)
    single = (0, 1, False), (1, 1, False)
    chunks = (0, 2, True), (1, 2, True)
    rows = local_rows
    grad_out_halves = [join(info, out_grad_in, grad_out_one), join(info, grad_out_two, grad_out_last)]
    grad_out_others = [topo.other_core(half_rows) for half_rows in grad_out_halves]
    out_keep, out_send = sum_split(info, rows, 2, *pair, [out_own], out_other)
    out_one = topo.swap(out_send, line, 1)
    grad_out_all = join(info, *grad_out_halves, *grad_out_others)
    factors = (grad_out_all, gate_factor, up_factor, gate_up, down)
    grads_other, *back_other = backward(info, 1, *factors, tile)
    back_other = [topo.other_core(part_rows) for part_rows in back_other]
    down_grad = functools.partial(grads_of, info, grad_out_all, [hidden], block)
    down_first = topo.swap(down_grad(3), square, 1)
    down_next = topo.swap(down_grad(2), square, 1)
    wait_for(info, out_one)
    grads_own, *back_own = backward(info, 0, *factors, tile)
    wait_for(info, down_first, down_next)
    back_keep, back_send = sum_split(info, rows, 2, *pair, back_own, back_other)
    back_one = topo.swap(back_send, line, 1)
    gate_up_grad = functools.partial(grads_of, info, mlp_in, [grads_own, grads_other], block)
    gate_up_first = topo.swap(gate_up_grad(3), square, 1)
    gate_up_send = gate_up_grad(2)
    down_last = topo.swap(down_grad(1, down_first), square, 0)
    down_kept = down_grad(0, down_next)
    back_keep, back_send = sum_split(info, rows, 1, *single, [back_keep], [back_one])
    back_two = topo.swap(back_send, line, 0)
    down_keep, down_send = sum_split(info, shard_rows, 2, *chunks, [down_kept], [down_last])
    gate_up_next = topo.swap(tie(info, gate_up_send), square, 1)
    gate_up_last = [
        topo.swap(gate_up_grad(1, gate_up_first, share), square, 0) for share in range(2)
    ]

    grad_state_low, grad_state, gain_two_grad = norm_back(
        info, state, back_keep, back_two, out_grad_in, gain_two, False
    )
    state_other = topo.other_core(grad_state_low)
    out_keep, out_send = sum_split(info, rows, 1, *single, [out_keep], [out_one])
    out_two = topo.swap(out_send, line, 0)
    down_one = topo.swap(tie(info, down_send), line, 0)
    grad_state_all = join(info, grad_state_low, state_other)
    grad_linear, bias_grad, own_part, other_part = attend_back(
        info,
        grad_state_all,
        o_all,
        q_all,
        linear,
        mass,
        cosine,
        sine,
        row_info,
        col_info,
        q_heads,
        kv_heads,
    )
    part_other = topo.other_core(other_part)
    down_two = topo.swap(second_chunks(info, down_keep, down_one), line, 1)
    q_full = grads_sent(info, attn_in, grad_linear, block)
    q_got = topo.swap(q_full, square, 1)
    o_full = grads_sent(info, grad_state_all, mixed, block)
    o_got = topo.swap(o_full, square, 1)
    block_out = close_rows(info, state, out_keep, out_two)
    gate_up_kept = gate_up_grad(0, gate_up_next)
    gate_up_keep, gate_up_send = sum_split(
        info, shard_rows, 2, *chunks, [gate_up_kept], gate_up_last
    )
    gate_up_one = topo.swap(gate_up_send, line, 0)
    (down_grads,) = columns_out(info, down_keep, down_one, down_two, part, ff_cols)
    tokens_grad, gain_one_grad = norm_back(
        info, inputs, own_part, part_other, grad_state, gain_one, True
    )
    sums = jnp.concatenate([bias_grad, gain_one_grad, gain_two_grad], axis=1)
    sums = sums.reshape(-1, LANES)
    shared = qkv_cols // LANES
    sums_got = topo.other_core(sums)
    sums = sum_rows(info, sums, sums_got, shared)
    sums_got = topo.swap(sums, square, 0)

    gate_up_two = topo.swap(second_chunks(info, gate_up_keep, gate_up_one), line, 1)
    q_kept, q_send = grads_kept(info, attn_in, grad_linear, block, q_got)
    q_last = topo.swap(q_send, square, 0)
    o_kept, o_send = grads_kept(info, grad_state_all, mixed, block, o_got)
    o_last = topo.swap(o_send, square, 0)
    sums = sum_rows(info, sums, sums_got, 0)
    sums_got = topo.swap(sums, square, 1)
    ordered = (0, 1, True), (2, 1, True)
    q_keep, q_send = sum_split(info, shard_rows, 2, *ordered, [q_kept], [q_last])
    q_one = topo.swap(q_send, line, 1)
    o_keep, o_send = sum_split(info, shard_rows, 2, *ordered, [o_kept], [o_last])
    o_one = topo.swap(o_send, line, 1)
    gate_grads, up_grads = columns_out(
        info, gate_up_keep, gate_up_one, gate_up_two, part, ff_cols
    )
    sums = sum_rows(info, sums, sums_got, 0)
    sums_got = topo.swap(sums, line, 0)
    q_keep, q_send = sum_split(info, shard_rows, 1, *single, [q_keep], [q_one])
    q_two = topo.swap(q_send, line, 0)
    sums = sum_rows(info, sums, sums_got, 0)
    sums_got = topo.swap(sums, line, 1)
    o_keep, o_send = sum_split(info, shard_rows, 1, *single, [o_keep], [o_one])
    o_two = topo.swap(o_send, line, 0)
    q_grads, k_grads, v_grads = sum_out(info, q_keep, q_two, (q_cols, kv_cols, kv_cols))
    (o_grads,) = sum_out(info, o_keep, o_two, (q_cols,))
    sums = sum_rows(info, sums, sums_got, 0).reshape(-1)
    own_bias = sums[:qkv_cols]
    gain_sum = sums[qkv_cols:].reshape(2, width)
    CLOCK[0] = None
    return (
        block_out,
        tokens_grad,
        gain_sum[0],
        q_grads,
        own_bias[:q_cols],
        k_grads,
        own_bias[q_cols : q_cols + kv_cols],
        v_grads,
        own_bias[q_cols + kv_cols :],
        o_grads,
        gain_sum[1],
        gate_grads,
        up_grads,
        down_grads,
    )


def solution(mesh):
    rows = P(("dp", "tensor"), None)
    both = P("dp", "tensor")
    half = P("tensor")
    in_specs = (
        rows, rows, P("dp", None), P(), both, half, both, half, both, half, both, P(), both, both, both,
    )
    out_specs = (
        rows, rows, P(), both, half, both, half, both, half, both, P(), both, both, both,
    )
    fast = mesh.shape["dp"] == LINE * LINE and mesh.shape["tensor"] == 2
    return jax.shard_map(
        per_device if fast else plain_device,
        mesh=mesh,
        in_specs=in_specs,
        out_specs=out_specs,
        check_vma=False,
    )
```

```python
import functools
import math

import jax
import jax.numpy as jnp
from jax import lax
from jax.experimental import pallas as pl
from jax.experimental.pallas import tpu as pltpu
from jax.sharding import PartitionSpec as P

HEAD_DIM = 128
EPSILON = 1e-06
ROPE_BASE = 1000000.0
MASKED = -1e30
LINE = 4
LANES = 128
BF = jnp.bfloat16
F32 = jnp.float32
VMEM_BYTES = 56 * 2**20
ANY = pl.BlockSpec(memory_space=pl.ANY)


def normalize(values):
    factor = lax.rsqrt(jnp.mean(values * values, axis=1, keepdims=True) + EPSILON)
    return (values * factor, factor)


def plain_norm_back(grad_normed, normed, factor, gain_vec):
    scaled = grad_normed * gain_vec[None, :]
    row_inner = jnp.mean(scaled * normed, axis=1, keepdims=True)
    return (factor * (scaled - normed * row_inner), jnp.sum(grad_normed * normed, axis=0))


def rope_tables(positions, width):
    half_width = width // 2
    frequency = jnp.power(ROPE_BASE, -2.0 * jnp.arange(half_width, dtype=F32) / width)
    angles = positions.astype(F32)[:, None] * frequency[None, :]
    return (jnp.cos(angles), jnp.sin(angles))


def rotate(values, cosine_table, sine_table):
    half_width = values.shape[-1] // 2
    lower_half = values[..., :half_width]
    upper_half = values[..., half_width:]
    return jnp.concatenate(
        [
            lower_half * cosine_table - upper_half * sine_table,
            upper_half * cosine_table + lower_half * sine_table,
        ],
        axis=-1,
    )


def unrotate(values, cosine_table, sine_table):
    return rotate(values, cosine_table, -sine_table)


def segment_info(length_row, places):
    seq_ends = jnp.cumsum(length_row)
    starts = seq_ends - length_row
    segment = jnp.sum((places[:, None] >= seq_ends[None, :]).astype(jnp.int32), axis=1)
    slot_ids = jnp.arange(length_row.shape[0], dtype=jnp.int32)
    offset = jnp.sum(jnp.where(segment[:, None] == slot_ids[None, :], starts[None, :], 0), axis=1)
    return (segment, places - offset)


class PlainTopo:
    def __init__(self):
        self.dp = lax.axis_size("dp")
        self.square = self.dp // LINE
        self.me = lax.axis_index("dp")
        self.core = lax.axis_index("tensor")
        self.line_at = self.me // self.square
        self.square_at = self.me % self.square
        line_bits = [self.square << i for i in range(LINE.bit_length() - 1)]
        square_bits = [1 << i for i in range(self.square.bit_length() - 1)]
        self.line = (line_bits, line_bits[::-1])
        self.squares = (square_bits, square_bits[::-1])

    def swap(self, array, bits, phase):
        perm = []
        for place in range(self.dp):
            for core in range(2):
                perm.append((place * 2 + core, (place ^ bits[core][phase]) * 2 + core))
        return lax.ppermute(array, ("dp", "tensor"), perm)

    def other_core(self, array):
        return lax.ppermute(array, "tensor", [(0, 1), (1, 0)])

    def offset(self, bits, index, unit):
        totals = [0, 0]
        for core in range(2):
            for phase, bit in enumerate(bits[core]):
                if index >> phase & 1:
                    totals[core] ^= bit // unit
        return jnp.where(self.core == 0, totals[0], totals[1])

    def gather(self, own, bits):
        pieces = [own]
        for phase in range(len(bits[0])):
            pieces = pieces + [self.swap(piece, bits, phase) for piece in pieces]
        return pieces

    def gather_joined(self, own, bits):
        joined = own
        for phase in range(len(bits[0])):
            joined = jnp.concatenate([joined, self.swap(joined, bits, phase)], axis=0)
        return joined

    def scatter_sum(self, array, bits):
        for phase in reversed(range(len(bits[0]))):
            half = array.shape[0] // 2
            got = self.swap(array[half:], bits, phase)
            array = (array[:half].astype(F32) + got.astype(F32)).astype(BF)
        return array

    def total(self, array):
        for bits in (self.line, self.squares):
            for phase in range(len(bits[0])):
                array = array + self.swap(array, bits, phase)
        return array

    def exchange(self, chunks, bits):
        rows = chunks[0].shape[0]
        held = [chunk for chunk in chunks]
        for phase in range(len(bits[0])):
            step = 1 << phase
            keep = [i for i in range(len(chunks)) if not i & step]
            keep = [i for i in keep if held[i] is not None]
            sent = jnp.concatenate([held[i + step] for i in keep], axis=0)
            got = self.swap(sent, bits, phase)
            parts = jnp.split(got, len(keep), axis=0)
            for i, part in zip(keep, parts):
                held[i] = jnp.concatenate([held[i], part], axis=0)
                held[i + step] = None
        return jnp.split(held[0], len(chunks), axis=0)

    def ordered(self, pieces, bits, unit, at):
        count = len(pieces)
        tables = []
        for core in range(2):
            table = [0] * count
            for index in range(count):
                total = 0
                for phase, bit in enumerate(bits[core]):
                    if index >> phase & 1:
                        total ^= bit // unit
                table[total] = index
            tables.append(table)
        tables = jnp.asarray(tables, jnp.int32)[self.core]
        stacked = jnp.stack(pieces)
        return [
            lax.dynamic_index_in_dim(
                stacked, lax.dynamic_index_in_dim(tables, place ^ at, 0, False), 0, False
            )
            for place in range(count)
        ]


def to_inner(rows, topo):
    count, width = rows.shape
    rest = width // topo.dp
    cut = rows.reshape(count, LINE, topo.square, rest).transpose(2, 0, 1, 3)
    cut = cut.reshape(topo.square, count, LINE * rest)
    return jnp.concatenate(
        [
            lax.dynamic_index_in_dim(cut, topo.square_at ^ i, 0, False)
            for i in range(topo.square)
        ],
        axis=1,
    )


def to_outer(rows, topo):
    count, width = rows.shape
    rest = width // topo.dp
    cut = rows.reshape(count, topo.square, LINE * rest).transpose(1, 0, 2)
    cut = jnp.stack(
        [
            lax.dynamic_index_in_dim(cut, topo.square_at ^ i, 0, False)
            for i in range(topo.square)
        ]
    )
    cut = cut.reshape(topo.square, count, LINE, rest).transpose(1, 2, 0, 3)
    return cut.reshape(count, width)


def dot(left, right):
    return jnp.dot(left, right, preferred_element_type=F32)


def dot_t(left, right):
    return lax.dot_general(left, right, (((1,), (1,)), ((), ())), preferred_element_type=F32)


def t_dot(left, right):
    return lax.dot_general(left, right, (((0,), (0,)), ((), ())), preferred_element_type=F32)


def attention_scores(queries, key_rows, allowed):
    score_scale = 1.0 / math.sqrt(queries.shape[-1])
    raw_scores = jnp.einsum("qgpd,kgd->gpqk", queries, key_rows, preferred_element_type=F32)
    return jnp.where(allowed[None, None], raw_scores * score_scale, MASKED)


def plain_device(
    tokens,
    out_grad,
    lengths,
    attn_gain,
    q_weight,
    q_bias,
    k_weight,
    k_bias,
    v_weight,
    v_bias,
    o_weight,
    mlp_gain,
    gate_weight,
    up_weight,
    down_weight,
):
    topo = PlainTopo()
    local_rows, width = tokens.shape
    group_rows = 2 * local_rows
    q_cols = q_weight.shape[1]
    kv_cols = k_weight.shape[1]
    qkv_cols = q_cols + 2 * kv_cols
    ff_cols = gate_weight.shape[1]
    part = -(-ff_cols // (LINE * LANES)) * LANES
    kv_groups = kv_cols // HEAD_DIM
    per_group = q_cols // HEAD_DIM // kv_groups
    score_scale = 1.0 / math.sqrt(HEAD_DIM)

    def line_gather(shard):
        pieces = jnp.split(topo.gather_joined(shard, topo.line), LINE, axis=0)
        return jnp.concatenate(topo.ordered(pieces, topo.line, topo.square, topo.line_at), axis=0)

    def square_gather(shard):
        pieces = topo.gather(shard, topo.squares)
        return jnp.concatenate(topo.ordered(pieces, topo.squares, 1, 0), axis=0)

    def square_scatter(grads):
        pieces = jnp.split(grads.astype(BF), topo.square, axis=0)
        by_index = topo.ordered(pieces, tuple(b for b in topo.squares), 1, 0)
        return topo.scatter_sum(jnp.concatenate(by_index, axis=0), topo.squares)

    def line_offset(index):
        return topo.line_at ^ topo.offset(topo.line, index, topo.square)

    def columns_in(shards):
        padded = [jnp.pad(s, ((0, 0), (0, LINE * part - ff_cols))) for s in shards]
        chunks = []
        for index in range(LINE):
            start = line_offset(index) * part
            chunks.append(
                jnp.concatenate(
                    [lax.dynamic_slice_in_dim(s, start, part, axis=1) for s in padded], axis=1
                )
            )
        got = topo.exchange(chunks, topo.line)
        return jnp.concatenate(topo.ordered(got, topo.line, topo.square, topo.line_at), axis=0)

    def columns_out(piece, count):
        rows = piece.shape[0] // LINE
        chunks = [
            lax.dynamic_slice_in_dim(piece, line_offset(index) * rows, rows, axis=0)
            for index in range(LINE)
        ]
        got = topo.ordered(
            topo.exchange(chunks, topo.line), topo.line, topo.square, topo.line_at
        )
        return [
            jnp.concatenate([g[:, i * part : (i + 1) * part] for g in got], axis=1)[
                :, :ff_cols
            ].astype(F32)
            for i in range(count)
        ]

    def rows_out(piece):
        rows = piece.shape[0] // LINE
        chunks = [
            lax.dynamic_slice_in_dim(piece, line_offset(index) * rows, rows, axis=0)
            for index in range(LINE)
        ]
        return topo.scatter_sum(jnp.concatenate(chunks, axis=0), topo.line).astype(F32)

    def both_cores(rows):
        return jnp.concatenate([rows, topo.other_core(rows)], axis=0)

    def core_sum(rows):
        half = rows.shape[0] // 2
        return rows[:half] + topo.other_core(rows[half:].astype(BF)).astype(F32)

    def line_tokens(rows):
        return both_cores(topo.gather_joined(rows, topo.line))

    def line_sum(partial):
        return topo.scatter_sum(core_sum(partial).astype(BF), topo.line).astype(F32)

    row_ids = jnp.arange(local_rows, dtype=jnp.int32)
    places = jnp.concatenate(
        [topo.core * local_rows + row_ids, (1 - topo.core) * local_rows + row_ids]
    )
    segment, positions = segment_info(lengths[0], places)
    allowed = (segment[:, None] == segment[None, :]) & (places[None, :] <= places[:, None])
    cosine_table, sine_table = rope_tables(positions, HEAD_DIM)
    q_cosine = cosine_table[:, None, None, :]
    q_sine = sine_table[:, None, None, :]
    k_cosine = cosine_table[:, None, :]
    k_sine = sine_table[:, None, :]

    inputs_low = to_inner(tokens, topo)
    out_grad_low = to_inner(out_grad, topo)
    gains = to_inner(jnp.stack([attn_gain, mlp_gain]), topo).astype(F32)
    gain_one, gain_two = gains[0], gains[1]
    inputs = inputs_low.astype(F32)
    bias_all = jnp.concatenate([q_bias, k_bias, v_bias]).astype(F32)

    qkv_local = jnp.concatenate([q_weight, k_weight, v_weight], axis=1)
    qkv_all = square_gather(line_gather(qkv_local))
    o_all = square_gather(line_gather(o_weight))
    down_all = square_gather(columns_in([down_weight]))
    grad_out_all = line_tokens(out_grad_low)
    gate_up = square_gather(columns_in([gate_weight, up_weight]))

    normed_one, factor_one = normalize(inputs)
    attn_in = both_cores((normed_one * gain_one[None, :]).astype(BF))
    linear = dot(attn_in, qkv_all) + bias_all[None, :]
    queries = rotate(
        linear[:, :q_cols].reshape(group_rows, kv_groups, per_group, HEAD_DIM), q_cosine, q_sine
    ).astype(BF)
    key_rows = rotate(
        linear[:, q_cols : q_cols + kv_cols].reshape(group_rows, kv_groups, HEAD_DIM),
        k_cosine,
        k_sine,
    ).astype(BF)
    values = linear[:, q_cols + kv_cols :].reshape(group_rows, kv_groups, HEAD_DIM).astype(BF)
    scores = attention_scores(queries, key_rows, allowed)
    row_peak = jnp.max(scores, axis=-1, keepdims=True)
    exponent = jnp.exp(scores - row_peak)
    row_mass = jnp.sum(exponent, axis=-1, keepdims=True)
    log_mass = row_peak + jnp.log(row_mass)
    probs_low = (exponent / row_mass).astype(BF)
    mixed_heads = jnp.einsum("gpqk,kgd->qgpd", probs_low, values, preferred_element_type=F32)
    mixed_heads = mixed_heads.reshape(group_rows, q_cols).astype(BF)
    hidden_state = inputs + core_sum(dot_t(mixed_heads, o_all))
    normed_two, factor_two = normalize(hidden_state)

    mlp_in = line_tokens((normed_two * gain_two[None, :]).astype(BF))
    grad_hidden = dot(grad_out_all, down_all)
    gate_up_out = dot(mlp_in, gate_up)
    gate_val = gate_up_out[:, :part]
    up_val = gate_up_out[:, part:]
    sigmoid_gate = jax.nn.sigmoid(gate_val)
    activated = gate_val * sigmoid_gate
    hidden_units = (activated * up_val).astype(BF)
    grad_gate = (
        grad_hidden * up_val * sigmoid_gate * (1.0 + gate_val * (1.0 - sigmoid_gate))
    ).astype(BF)
    grad_up = (grad_hidden * activated).astype(BF)
    grad_gate_up = jnp.concatenate([grad_gate, grad_up], axis=1)
    grad_normed_two = line_sum(dot_t(grad_gate_up, gate_up))
    block_out = (hidden_state + line_sum(dot_t(hidden_units, down_all))).astype(BF)
    gate_grads, up_grads = columns_out(square_scatter(t_dot(mlp_in, grad_gate_up)), 2)
    (down_grads,) = columns_out(square_scatter(t_dot(grad_out_all, hidden_units)), 1)

    back_two, gain_two_grad = plain_norm_back(grad_normed_two, normed_two, factor_two, gain_two)
    grad_state = out_grad_low.astype(F32) + back_two
    grad_state_all = both_cores(grad_state.astype(BF))
    o_grads = rows_out(square_scatter(t_dot(grad_state_all, mixed_heads)))
    grad_mixed = dot(grad_state_all, o_all)
    grad_heads = grad_mixed.astype(BF).reshape(group_rows, kv_groups, per_group, HEAD_DIM)
    scores_again = attention_scores(queries, key_rows, allowed)
    prob_rows = jnp.exp(scores_again - log_mass)
    grad_probs = jnp.einsum("qgpd,kgd->gpqk", grad_heads, values, preferred_element_type=F32)
    row_inner = jnp.sum(prob_rows * grad_probs, axis=-1, keepdims=True)
    grad_scores = (prob_rows * (grad_probs - row_inner) * score_scale).astype(BF)
    grad_values = jnp.einsum(
        "gpqk,qgpd->kgd", prob_rows.astype(BF), grad_heads, preferred_element_type=F32
    )
    grad_queries = jnp.einsum("gpqk,kgd->qgpd", grad_scores, key_rows, preferred_element_type=F32)
    grad_keys = jnp.einsum("gpqk,qgpd->kgd", grad_scores, queries, preferred_element_type=F32)
    grad_linear = jnp.concatenate(
        [
            unrotate(grad_queries, q_cosine, q_sine).reshape(group_rows, q_cols),
            unrotate(grad_keys, k_cosine, k_sine).reshape(group_rows, kv_cols),
            grad_values.reshape(group_rows, kv_cols),
        ],
        axis=1,
    ).astype(BF)
    bias_grad = jnp.sum(grad_linear.astype(F32), axis=0)
    qkv_grads = rows_out(square_scatter(t_dot(attn_in, grad_linear)))
    grad_normed_one = core_sum(dot_t(grad_linear, qkv_all))
    back_one, gain_one_grad = plain_norm_back(grad_normed_one, normed_one, factor_one, gain_one)
    tokens_grad = (grad_state + back_one).astype(BF)
    gain_grads = to_outer(jnp.stack([gain_one_grad, gain_two_grad]), topo)
    gain_grads = gain_grads + topo.other_core(gain_grads)
    small = topo.total(jnp.concatenate([bias_grad, gain_grads.reshape(-1)]).reshape(-1, LANES))
    small = small.reshape(-1)
    own_bias = small[:qkv_cols]
    gain_sum = small[qkv_cols:].reshape(2, width)
    return (
        to_outer(block_out, topo),
        to_outer(tokens_grad, topo),
        gain_sum[0],
        qkv_grads[:, :q_cols],
        own_bias[:q_cols],
        qkv_grads[:, q_cols : q_cols + kv_cols],
        own_bias[q_cols : q_cols + kv_cols],
        qkv_grads[:, q_cols + kv_cols : qkv_cols],
        own_bias[q_cols + kv_cols :],
        o_grads,
        gain_sum[1],
        gate_grads,
        up_grads,
        down_grads,
    )


def nn(left, right):
    return jnp.dot(left, right, preferred_element_type=F32)


def nt(left, right):
    return lax.dot_general(left, right, (((1,), (1,)), ((), ())), preferred_element_type=F32)


def tn(left, right):
    return lax.dot_general(left, right, (((0,), (0,)), ((), ())), preferred_element_type=F32)


def shape(dims, kind):
    return jax.ShapeDtypeStruct(dims, kind)


def whole(dims):
    return pl.BlockSpec(dims, lambda *_: (0,) * len(dims))


OFF, NEIGHBOUR, INDEX, AT, OTHER = 0, 4, 8, 12, 13


class Topo:
    def __init__(self):
        self.dp = lax.axis_size("dp")
        me = lax.axis_index("dp")
        core = lax.axis_index("tensor")
        line_at, square_at = me >> 2, me & 3

        def by_core(index):
            return jnp.where(core == 0, index, (index >> 1) | ((index & 1) << 1))

        self.core = core
        self.square_at = square_at
        self.line = ((LINE, 2 * LINE), (2 * LINE, LINE))
        self.square = ((1, 2), (2, 1))
        count = jnp.arange(LINE, dtype=jnp.int32)
        self.info = jnp.concatenate(
            [
                by_core(count),
                line_at ^ by_core(count),
                by_core(line_at ^ count),
                jnp.stack([square_at, 1 - core]),
            ]
        ).astype(jnp.int32)

    def swap(self, array, bits, phase):
        perm = []
        for place in range(self.dp):
            for core in range(2):
                flip = bits[core][phase] if phase < 2 else bits[core][0] ^ bits[core][1]
                perm.append((place * 2 + core, (place ^ flip) * 2 + core))
        return lax.ppermute(array, ("dp", "tensor"), perm)

    def other_core(self, array):
        return lax.ppermute(array, "tensor", [(0, 1), (1, 0)])

    def both_ways(self, array):
        return lax.all_to_all(array, "tensor", 0, 0, tiled=True)


CLOCK = [None]
TOKEN = jax.ShapeDtypeStruct((8, 128), F32)
IN_VMEM = pl.BlockSpec(memory_space=pltpu.VMEM)
IN_SMEM = pl.BlockSpec(memory_space=pltpu.SMEM)


def in_order(body, ins, outs):
    taken = 0 if CLOCK[0] is None else 1

    def full(*refs):
        body(*refs[:ins], *refs[ins + taken : ins + taken + outs], *refs[ins + taken + outs + 1 :])

    return full


def run(kernel, single, args):
    taken = [] if CLOCK[0] is None else [CLOCK[0]]
    *out, CLOCK[0] = kernel(*args, *taken)
    return out[0] if single else out


def as_list(value):
    return list(value) if isinstance(value, (list, tuple)) else [value]


def call(body, grid, in_specs, out_specs, out_shape, scratch, info, *args, mib=32):
    outs = as_list(out_shape)
    late = 0 if CLOCK[0] is None else 1
    kernel = pl.pallas_call(
        in_order(body, 1 + len(in_specs), len(outs)),
        grid_spec=pltpu.PrefetchScalarGridSpec(
            num_scalar_prefetch=1,
            grid=grid,
            in_specs=list(in_specs) + [IN_VMEM] * late,
            out_specs=as_list(out_specs) + [IN_VMEM],
            scratch_shapes=list(scratch),
        ),
        out_shape=outs + [TOKEN],
        compiler_params=pltpu.CompilerParams(vmem_limit_bytes=mib * 2**20),
        cost_estimate=pl.CostEstimate(flops=1000, bytes_accessed=1000, transcendentals=0),
        name=body.__qualname__.split(".")[0],
    )
    return run(kernel, not isinstance(out_shape, (list, tuple)), (info,) + args)


def small(body, out_shape, scratch, info, *args, mib=10, out_spec=IN_VMEM):
    outs = as_list(out_shape)
    late = 0 if CLOCK[0] is None else 1
    kernel = pl.pallas_call(
        in_order(body, 1 + len(args), len(outs)),
        in_specs=[IN_SMEM] + [IN_VMEM] * (len(args) + late),
        out_specs=[out_spec] * len(outs) + [IN_VMEM],
        scratch_shapes=list(scratch),
        out_shape=outs + [TOKEN],
        compiler_params=pltpu.CompilerParams(vmem_limit_bytes=mib * 2**20),
        cost_estimate=pl.CostEstimate(flops=1000, bytes_accessed=1000, transcendentals=0),
        name=body.__qualname__.split(".")[0],
    )
    return run(kernel, not isinstance(out_shape, (list, tuple)), (info,) + args)


def tie(info, array):
    def body(info_ref, in_ref, out_ref):
        out_ref[...] = in_ref[...]

    return small(body, shape(array.shape, array.dtype), [], info, array)


def spacer(info, topo, array):
    wait_for(info, topo.other_core(tie(info, array)))


def wait_for(info, *arrays):
    def body(*refs):
        del refs

    late = 0 if CLOCK[0] is None else 1
    kernel = pl.pallas_call(
        body,
        in_specs=[ANY] * len(arrays) + [IN_VMEM] * late,
        out_specs=[IN_VMEM],
        out_shape=[TOKEN],
        compiler_params=pltpu.CompilerParams(vmem_limit_bytes=16 * 2**20),
        cost_estimate=pl.CostEstimate(flops=1, bytes_accessed=1, transcendentals=0),
        name="wait_for",
    )
    (CLOCK[0],) = kernel(*arrays, *([CLOCK[0]] if late else []))


def join(info, *args):
    def body(info_ref, *refs):
        start = 0
        for ref in refs[:-1]:
            refs[-1][start : start + ref.shape[0]] = ref[...]
            start += ref.shape[0]

    rows = sum(a.shape[0] for a in args)
    return small(body, shape((rows,) + args[0].shape[1:], args[0].dtype), [], info, *args)


def join_far(info, *args):
    def body(info_ref, *refs):
        ins, out, sems = refs[: len(args)], refs[len(args)], refs[-1]
        start = 0
        copies = []
        for index, ref in enumerate(ins):
            rows = ref.shape[0]
            copies.append(
                pltpu.make_async_copy(ref, out.at[pl.ds(start, rows)], sems.at[index])
            )
            start += rows
        for copy in copies:
            copy.start()
        for copy in copies:
            copy.wait()

    rows = sum(a.shape[0] for a in args)
    return small(
        body,
        shape((rows,) + args[0].shape[1:], args[0].dtype),
        [pltpu.SemaphoreType.DMA((len(args),))],
        info,
        *args,
        out_spec=ANY,
    )


def join_split(info, widths, *args):
    rows = sum(a.shape[0] for a in args)

    def body(info_ref, *refs):
        ins, outs = refs[: len(args)], refs[len(args) :]
        low = 0
        for ref in ins:
            start = 0
            for out, cols in zip(outs, widths):
                out[low : low + ref.shape[0]] = ref[:, start : start + cols]
                start += cols
            low += ref.shape[0]

    return small(body, [shape((rows, cols), BF) for cols in widths], [], info, *args)


def beside(info, *args):
    def body(info_ref, *refs):
        start = 0
        for ref in refs[:-1]:
            refs[-1][:, start : start + ref.shape[1]] = ref[...]
            start += ref.shape[1]

    cols = sum(a.shape[1] for a in args)
    return small(body, shape((args[0].shape[0], cols), args[0].dtype), [], info, *args)


def placed(info, rows, takes, *args):
    def body(info_ref, *refs):
        for index, (which, start) in enumerate(takes):
            target = pl.multiple_of(info_ref[NEIGHBOUR + index] * rows, 16)
            refs[-1][pl.ds(target, rows)] = refs[which][start : start + rows]

    return small(body, shape((LINE * rows, args[0].shape[1]), BF), [], info, *args)


def second_chunks(info, kept, got):
    rows = kept.shape[0] // 2

    def body(info_ref, kept_ref, got_ref, out_ref):
        out_ref[:rows] = kept_ref[rows:]
        out_ref[rows:] = got_ref[rows:]

    return small(body, shape(kept.shape, BF), [], info, kept, got)


def cut_columns(info, part, *weights):
    count = len(weights)
    rows, cols = weights[0].shape
    short = cols - (LINE - 1) * part

    def body(info_ref, *refs):
        ins, outs = refs[:count], refs[count:]
        for index in range(LINE):
            at = info_ref[NEIGHBOUR + index]
            out = outs[1 - index % 2]
            low = index // 2 * rows
            for which, ref in enumerate(ins):
                start = pl.multiple_of(at * part, LANES)
                first = which * part
                out[low : low + rows, first : first + short] = ref[:, pl.ds(start, short)]
                if short < part:
                    rest = pl.multiple_of(jnp.minimum(at, LINE - 2) * part + short, LANES)
                    tail = ref[:, pl.ds(rest, part - short)]
                    out[low : low + rows, first + short : first + part] = jnp.where(
                        at < LINE - 1, tail, jnp.zeros_like(tail)
                    )

    return small(body, [shape((2 * rows, count * part), BF)] * 2, [], info, *weights)


def square_blocks(info_ref, pieces, width):
    rows = width // LINE
    index = 0
    for piece in pieces:
        for block in range(piece.shape[0] // rows):
            start = pl.multiple_of(info_ref[OFF + index] * rows, LANES)
            yield pl.ds(start, rows), piece[block * rows : (block + 1) * rows]
            index += 1


def inward(values, at, store):
    width = values.shape[1]
    block = width // LINE
    rest = block // LINE
    for square in range(LINE):
        parts = [
            values[:, line * block + square * rest : line * block + (square + 1) * rest]
            for line in range(LINE)
        ]
        start = pl.multiple_of((square ^ at) * block, LANES)
        store(pl.ds(start, block), jnp.concatenate(parts, axis=1))


def outward(ref, at):
    width = ref.shape[1]
    block = width // LINE
    rest = block // LINE
    blocks = []
    for square in range(LINE):
        start = pl.multiple_of((square ^ at) * block, LANES)
        blocks.append(ref[:, pl.ds(start, block)])
    parts = []
    for line in range(LINE):
        for square in range(LINE):
            parts.append(blocks[square][:, line * rest : (line + 1) * rest])
    return jnp.concatenate(parts, axis=1)


def turn_rows(info, rows):
    def body(info_ref, rows_ref, out_ref, held):
        def store(cols, block):
            held[:, cols] = block

        inward(rows_ref[...].astype(F32), info_ref[AT], store)
        out_ref[...] = held[...].astype(BF)

    return small(body, shape(rows.shape, BF), [pltpu.VMEM(rows.shape, F32)], info, rows)


def open_rows(info, rows, gains):
    def body(info_ref, rows_ref, gains_ref, out_ref, in_ref, gain_ref, held):
        def store_gain(cols, block):
            gain_ref[:, cols] = block

        def store(cols, block):
            held[:, cols] = block

        inward(gains_ref[...], info_ref[AT], store_gain)
        inward(rows_ref[...].astype(F32), info_ref[AT], store)
        values = held[...]
        in_ref[...] = values.astype(BF)
        factor = lax.rsqrt(jnp.mean(values * values, axis=1, keepdims=True) + EPSILON)
        out_ref[...] = (values * factor * gain_ref[0:1, :]).astype(BF)

    return small(
        body,
        [shape(rows.shape, BF), shape(rows.shape, BF), shape(gains.shape, F32)],
        [pltpu.VMEM(rows.shape, F32)],
        info,
        rows,
        gains,
    )


def state_rows(info, rows, own, got, gain):
    def body(info_ref, rows_ref, own_ref, early_ref, late_ref, gain_ref, out_ref, state_ref):
        half = dims[0] // 2
        for start, got_ref in ((0, early_ref), (half, late_ref)):
            span = pl.ds(start, half)
            values = rows_ref[span].astype(F32) + (own_ref[span] + got_ref[...].astype(F32))
            state_ref[span] = values
            factor = lax.rsqrt(jnp.mean(values * values, axis=1, keepdims=True) + EPSILON)
            out_ref[span] = (values * factor * gain_ref[...]).astype(BF)

    dims = rows.shape
    return small(
        body, [shape(dims, BF), shape(dims, F32)], [], info, rows, own, *got, gain
    )


def close_rows(info, state, own, got):
    def body(info_ref, state_ref, own_ref, got_ref, out_ref, held):
        held[...] = state_ref[...] + (own_ref[...].astype(F32) + got_ref[...].astype(F32))
        out_ref[...] = outward(held, info_ref[AT]).astype(BF)

    dims = state.shape
    return small(
        body,
        shape(dims, BF),
        [pltpu.VMEM(dims, F32)],
        info,
        state,
        own,
        got,
    )


def norm_back(info, values, own, got, base, gain, turn):
    def body(info_ref, values_ref, own_ref, got_ref, base_ref, gain_ref, *refs):
        values = values_ref[...].astype(F32)
        factor = lax.rsqrt(jnp.mean(values * values, axis=1, keepdims=True) + EPSILON)
        normed = values * factor
        grad = own_ref[...].astype(F32) + got_ref[...].astype(F32)
        scaled = grad * gain_ref[...]
        row_inner = jnp.mean(scaled * normed, axis=1, keepdims=True)
        total = base_ref[...].astype(F32) + factor * (scaled - normed * row_inner)
        gain_grad = jnp.sum(grad * normed, axis=0, keepdims=True)
        if turn:
            out_ref, gain_out_ref, held, gain_held = refs
            held[...] = total
            out_ref[...] = outward(held, info_ref[AT]).astype(BF)
        else:
            low_ref, out_ref, gain_out_ref, gain_held = refs
            out_ref[...] = total
            low_ref[...] = total.astype(BF)
        gain_held[...] = gain_grad
        gain_out_ref[...] = outward(gain_held, info_ref[AT])

    dims = values.shape
    kinds = (BF,) if turn else (BF, F32)
    return small(
        body,
        [shape(dims, kind) for kind in kinds] + [shape(gain.shape, F32)],
        ([pltpu.VMEM(dims, F32)] if turn else []) + [pltpu.VMEM(gain.shape, F32)],
        info,
        values,
        own,
        got,
        base,
        gain,
    )


def turned(values, cosine, sine):
    return values * cosine + pltpu.roll(values, HEAD_DIM // 2, 1) * sine


def attend(info, rows, pieces, bias, cosine, sine, row_info, col_info, q_heads, kv_heads):
    count, cols = len(pieces), pieces[0].shape[1]
    group, width = rows.shape
    q_cols = q_heads * HEAD_DIM

    def body(info_ref, in_ref, *refs):
        pieces = refs[:count]
        bias_ref, cos_ref, sin_ref, row_ref, col_ref = refs[count : count + 5]
        mixed_ref, lin_ref, mass_ref = refs[count + 5 :]
        cosine, sine = cos_ref[...], sin_ref[...]
        scale = 1.0 / math.sqrt(HEAD_DIM)
        linear = bias_ref[...]
        for cols, piece in square_blocks(info_ref, pieces, width):
            linear = linear + nn(in_ref[:, cols], piece)
        for head in range(q_heads + 2 * kv_heads):
            cols = slice(head * HEAD_DIM, (head + 1) * HEAD_DIM)
            part = linear[:, cols]
            if head < q_heads + kv_heads:
                part = turned(part, cosine, sine)
            lin_ref[:, cols] = part.astype(BF)
        allowed = (row_ref[:, 0:1] <= col_ref[...]) & (col_ref[...] <= row_ref[:, 1:2])
        for head in range(q_heads):
            key = q_heads + head // (q_heads // kv_heads)
            value = key + kv_heads
            cols = slice(head * HEAD_DIM, (head + 1) * HEAD_DIM)
            raw = nt(lin_ref[:, cols], lin_ref[:, key * HEAD_DIM : (key + 1) * HEAD_DIM])
            scores = jnp.where(allowed, raw * scale, MASKED)
            peak = jnp.max(scores, axis=1, keepdims=True)
            exponent = jnp.exp(scores - peak)
            mass = jnp.sum(exponent, axis=1, keepdims=True)
            mass_ref[:, head : head + 1] = peak + jnp.log(mass)
            probs = (exponent * (1.0 / mass)).astype(BF)
            mixed_ref[:, cols] = nn(
                probs, lin_ref[:, value * HEAD_DIM : (value + 1) * HEAD_DIM]
            ).astype(BF)

    plain = (bias, cosine, sine, row_info, col_info)
    return small(
        body,
        [shape((group, q_cols), BF), shape((group, cols), BF), shape((group, LANES), F32)],
        [],
        info,
        rows,
        *pieces,
        *plain,
        mib=12,
    )


def project(info, rows, pieces, width):
    count, cols = len(pieces), pieces[0].shape[1]
    half = rows.shape[0] // 2

    def body(info_ref, in_ref, *refs):
        pieces = refs[:count]
        early_ref, late_ref, own_ref = refs[count:]
        for cols, piece in square_blocks(info_ref, pieces, width):
            both = nt(in_ref[...], piece)
            own_ref[:, cols] = both[:half]
            early_ref[:, cols] = both[half : half + half // 2].astype(BF)
            late_ref[:, cols] = both[half + half // 2 :].astype(BF)

    return small(
        body,
        [shape((half // 2, width), BF)] * 2 + [shape((half, width), F32)],
        [],
        info,
        rows,
        *pieces,
    )


def attend_back(
    info, state, o_pieces, pieces, linear, mass, cosine, sine, row_info, col_info, q_heads, kv_heads
):
    count, cols = len(pieces), pieces[0].shape[1]
    group, width = state.shape
    q_cols = q_heads * HEAD_DIM
    half = group // 2

    def body(info_ref, state_ref, *refs):
        o_refs, q_refs = refs[:count], refs[count : 2 * count]
        lin_ref, mass_ref, cos_ref, sin_ref, row_ref, col_ref = refs[2 * count : 2 * count + 6]
        grad_ref, bias_ref, own_ref, other_ref = refs[2 * count + 6 : 2 * count + 10]
        heads_ref = refs[-1]
        cosine, sine = cos_ref[...], -sin_ref[...]
        scale = 1.0 / math.sqrt(HEAD_DIM)
        heads = 0.0
        for cols, piece in square_blocks(info_ref, o_refs, width):
            heads = heads + nn(state_ref[:, cols], piece)
        heads_ref[...] = heads.astype(BF)
        allowed = (row_ref[:, 0:1] <= col_ref[...]) & (col_ref[...] <= row_ref[:, 1:2])
        per_group = q_heads // kv_heads
        for place in range(kv_heads):
            key_cols = slice((q_heads + place) * HEAD_DIM, (q_heads + place + 1) * HEAD_DIM)
            first = q_heads + kv_heads + place
            value_cols = slice(first * HEAD_DIM, (first + 1) * HEAD_DIM)
            keys, values = lin_ref[:, key_cols], lin_ref[:, value_cols]
            grad_keys, grad_values = 0.0, 0.0
            for head in range(place * per_group, (place + 1) * per_group):
                cols = slice(head * HEAD_DIM, (head + 1) * HEAD_DIM)
                queries, grads = lin_ref[:, cols], heads_ref[:, cols]
                scores = jnp.where(allowed, nt(queries, keys) * scale, MASKED)
                probs = jnp.exp(scores - mass_ref[:, head : head + 1])
                grad_probs = nt(grads, values)
                inner = jnp.sum(probs * grad_probs, axis=1, keepdims=True)
                grad_scores = (probs * (grad_probs - inner) * scale).astype(BF)
                grad_values += tn(probs.astype(BF), grads)
                grad_keys += tn(grad_scores, queries)
                grad_ref[:, cols] = turned(nn(grad_scores, keys), cosine, sine).astype(BF)
            grad_ref[:, key_cols] = turned(grad_keys, cosine, sine).astype(BF)
            grad_ref[:, value_cols] = grad_values.astype(BF)
        bias_ref[...] = jnp.sum(grad_ref[...].astype(F32), axis=0, keepdims=True)
        for cols, piece in square_blocks(info_ref, q_refs, width):
            both = nt(grad_ref[...], piece)
            own_ref[:, cols] = both[:half]
            other_ref[:, cols] = both[half:].astype(BF)

    plain = (linear, mass, cosine, sine, row_info, col_info)
    return small(
        body,
        [
            shape((group, cols), BF),
            shape((1, cols), F32),
            shape((half, width), F32),
            shape((half, width), BF),
        ],
        [pltpu.VMEM((group, q_cols), BF)],
        info,
        state,
        *o_pieces,
        *pieces,
        *plain,
        mib=14,
    )


def in_square(info, pieces, width):
    def body(info_ref, *refs):
        for rows, block in square_blocks(info_ref, refs[:-1], width):
            refs[-1][rows] = block

    return small(body, shape((width, pieces[0].shape[1]), BF), [], info, *pieces)


def forward(info, x, gate_up, tile, step=256):
    part = gate_up.shape[1] // 2
    total, width = x.shape
    spans = [(low, min(low + step, part)) for low in range(0, part, step)]

    def body(info_ref, x_ref, weight, hid_ref, gate_ref, up_ref):
        x = x_ref[...]
        for low, high in spans:
            gate = nn(x, weight[:, low:high])
            up = nn(x, weight[:, part + low : part + high])
            share = 1.0 / (1.0 + jnp.exp(-gate))
            active = gate * share
            hid_ref[:, low:high] = (active * up).astype(BF)
            gate_ref[:, low:high] = (up * share * (1.0 + gate * (1.0 - share))).astype(BF)
            up_ref[:, low:high] = active.astype(BF)

    return call(
        body,
        (total // tile,),
        [pl.BlockSpec((tile, width), lambda i, _: (i, 0)), IN_VMEM],
        [pl.BlockSpec((tile, part), lambda i, _: (i, 0))] * 3,
        [shape((total, part), BF)] * 3,
        [],
        info,
        x,
        gate_up,
        mib=12,
    )


def halves_spec(tile, width, steps, spread):
    half = steps // 2

    def later(i, info_ref):
        first = info_ref[OTHER] * half if spread else 0
        return (first + jnp.maximum(i - half, 0), 0)

    return [
        pl.BlockSpec((tile, width), lambda i, _: (jnp.minimum(i, half - 1), 0)),
        pl.BlockSpec((tile, width), later),
    ]


def cut_rows(info, array, count):
    rows = array.shape[0] // count

    def body(info_ref, in_ref, *outs):
        for index, out in enumerate(outs):
            out[...] = in_ref[index * rows : (index + 1) * rows]

    return small(body, [shape((rows, array.shape[1]), array.dtype)] * count, [], info, array)


def store_half(value, steps, first_ref, second_ref):
    early = pl.program_id(0) < steps // 2

    @pl.when(early)
    def _():
        first_ref[...] = value

    @pl.when(jnp.logical_not(early))
    def _():
        second_ref[...] = value


def down_sum(info, hidden, down, tile):
    width = down.shape[0]
    total, part = hidden.shape
    steps = total // tile

    def body(info_ref, hid_ref, weight, own_ref, other_ref):
        value = nt(hid_ref[...], weight[...]).astype(BF)
        store_half(value, steps, own_ref, other_ref)

    return call(
        body,
        (steps,),
        [pl.BlockSpec((tile, part), lambda i, _: (i, 0)), IN_VMEM],
        halves_spec(tile, width, steps, False),
        [shape((total // 2, width), BF)] * 2,
        [],
        info,
        hidden,
        down,
        mib=11,
    )


def backward(info, half, g, gate_factor, up_factor, gate_up, down, tile, step=256):
    part = down.shape[1]
    total, width = g.shape[0] // 2, g.shape[1]
    steps = total // tile
    spans = [(low, min(low + step, part)) for low in range(0, part, step)]

    def body(info_ref, g_ref, gate_ref, up_ref, gate_up_ref, down_ref, grad_ref, *back_refs):
        g = g_ref[...]
        for low, high in spans:
            grad = nn(g, down_ref[:, low:high])
            grad_ref[:, low:high] = (grad * gate_ref[:, low:high].astype(F32)).astype(BF)
            grad_ref[:, part + low : part + high] = (
                grad * up_ref[:, low:high].astype(F32)
            ).astype(BF)
        value = nt(grad_ref[...], gate_up_ref[...]).astype(BF)
        for number, back_ref in enumerate(back_refs):

            @pl.when(pl.program_id(0) == number)
            def _(back_ref=back_ref):
                back_ref[...] = value

    return call(
        body,
        (steps,),
        [pl.BlockSpec((tile, cols), lambda i, _: (half * steps + i, 0)) for cols in (width, part, part)]
        + [IN_VMEM] * 2,
        [pl.BlockSpec((tile, 2 * part), lambda i, _: (i, 0))] + [whole((tile, width))] * steps,
        [shape((total, 2 * part), BF)] + [shape((tile, width), BF)] * steps,
        [],
        info,
        g,
        gate_factor,
        up_factor,
        gate_up,
        down,
        mib=18,
    )


def rows_spec(block, rights, where):
    rows = rights[0].shape[0]
    return [
        pl.BlockSpec((rows, block), lambda i, info_ref, r=r: (r, info_ref[OFF + where(i)]))
        for r in range(len(rights))
    ]


def grads_of(info, left, rights, block, index, got=None, share=None):
    rows, cols = rights[0].shape
    parts = len(rights)
    cols = cols if share is None else cols // 2
    tile = next(t for t in (768, 512, 384, 256, 128) if cols % t == 0)
    first = 0 if share is None else share * (cols // tile)

    def body(info_ref, *refs):
        value = 0.0
        for r in range(parts):
            value = value + tn(refs[r][...], refs[parts + r][...])
        if got is not None:
            value = value + refs[2 * parts][...].astype(F32)
        refs[-1][...] = value.astype(BF)

    out = pl.BlockSpec((block, tile), lambda i, _: (0, i))
    taken = pl.BlockSpec((block, tile), lambda i, _: (0, first + i))
    return call(
        body,
        (cols // tile,),
        rows_spec(block, rights, lambda i: index)
        + [pl.BlockSpec((rows, tile), lambda i, _: (0, first + i))] * parts
        + ([] if got is None else [taken]),
        out,
        shape((block, cols), BF),
        [],
        info,
        *([left] * parts),
        *rights,
        *([] if got is None else [got]),
        mib=12,
    )


def grads_sent(info, left, right, block):
    total, cols = right.shape

    def body(info_ref, left_ref, right_ref, out_ref):
        out_ref[...] = tn(left_ref[...], right_ref[...]).astype(BF)

    return call(
        body,
        (2,),
        rows_spec(block, [right], lambda i: 2 + i) + [whole(right.shape)],
        pl.BlockSpec((block, cols), lambda i, _: (i, 0)),
        shape((2 * block, cols), BF),
        [],
        info,
        left,
        right,
        mib=14,
    )


def grads_kept(info, left, right, block, got):
    total, cols = right.shape

    def body(info_ref, left_ref, right_ref, got_ref, keep_ref, send_ref):
        value = (tn(left_ref[...], right_ref[...]) + got_ref[...].astype(F32)).astype(BF)
        store_half(value, 2, keep_ref, send_ref)

    return call(
        body,
        (2,),
        rows_spec(block, [right], lambda i: i)
        + [whole(right.shape), pl.BlockSpec((block, cols), lambda i, _: (i, 0))],
        [whole((block, cols))] * 2,
        [shape((block, cols), BF)] * 2,
        [],
        info,
        left,
        right,
        got,
        mib=14,
    )


def sum_split(info, block, count, keep_at, send_at, lefts, rights):
    cols = lefts[0].shape[1]
    pieces = len(lefts)
    wide = rights[0].shape[1]
    sizes = (lefts[0].shape[0], rights[0].shape[0])

    def rows_of(refs, size, low, high):
        which = low // size
        return refs[which][low - which * size : high - which * size].astype(F32)

    def body(info_ref, *refs):
        ins, outs = refs[:-2], refs[-2:]
        left_refs, right_refs = ins[:pieces], ins[pieces:]
        for out, (first, stride, along) in zip(outs, (keep_at, send_at)):
            for step in range(count):
                index = first + stride * step
                if along:
                    rows = pl.ds(pl.multiple_of(info_ref[NEIGHBOUR + index] * block, 16), block)
                    for number, right in enumerate(right_refs):
                        span = slice(number * wide, (number + 1) * wide)
                        total = left_refs[0][rows, span].astype(F32) + right[rows].astype(F32)
                        out[step * block : (step + 1) * block, span] = total.astype(BF)
                    continue
                low, high = index * block, (index + 1) * block
                while low < high:
                    end = min([high] + [(low // size + 1) * size for size in sizes])
                    total = rows_of(left_refs, sizes[0], low, end)
                    total = total + rows_of(right_refs, sizes[1], low, end)
                    start = step * block + low - index * block
                    out[start : start + end - low] = total.astype(BF)
                    low = end

    return small(
        body, [shape((count * block, cols), BF)] * 2, [], info, *lefts, *rights
    )


def sum_out(info, left, right, widths):
    rows = left.shape[0]

    def body(info_ref, left_ref, right_ref, *outs):
        total = left_ref[...].astype(F32) + right_ref[...].astype(F32)
        start = 0
        for out, cols in zip(outs, widths):
            out[...] = total[:, start : start + cols]
            start += cols

    return small(
        body,
        [shape((rows, cols), F32) for cols in widths],
        [],
        info,
        left,
        right,
    )


def sum_rows(info, own, got, first):
    def body(info_ref, own_ref, got_ref, out_ref):
        if first:
            out_ref[:first] = own_ref[:first]
        out_ref[first:] = own_ref[first:] + got_ref[first:]

    return small(body, shape(own.shape, F32), [], info, own, got)


def columns_out(info, kept, got, last, part, cols):
    rows = kept.shape[0] // 2
    count = kept.shape[1] // part

    def body(info_ref, kept_ref, got_ref, last_ref, *outs):
        pieces = [kept_ref[:rows], got_ref[:rows], last_ref[:rows], last_ref[rows:]]
        for place in range(LINE):
            low = place * part
            span = min(part, cols - low)
            for index, piece in enumerate(pieces):

                @pl.when(info_ref[INDEX + place] == index)
                def _(piece=piece, low=low, span=span):
                    for which, out in enumerate(outs):
                        start = which * part
                        out[:, low : low + span] = piece[:, start : start + span].astype(F32)

    return small(
        body,
        [shape((rows, cols), F32)] * count,
        [],
        info,
        kept,
        got,
        last,
    )


def sequence_info(length_row, places):
    seq_ends = jnp.cumsum(length_row)
    starts = seq_ends - length_row
    inside = (places[:, None] >= starts[None, :]) & (places[:, None] < seq_ends[None, :])
    return jnp.sum(jnp.where(inside, starts[None, :], 0), axis=1)


def per_device(
    tokens,
    out_grad,
    lengths,
    attn_gain,
    q_weight,
    q_bias,
    k_weight,
    k_bias,
    v_weight,
    v_bias,
    o_weight,
    mlp_gain,
    gate_weight,
    up_weight,
    down_weight,
):
    CLOCK[0] = None
    topo = Topo()
    info = topo.info
    line, square = topo.line, topo.square
    local_rows, width = tokens.shape
    shard_rows = q_weight.shape[0]
    block = width // LINE
    q_cols = q_weight.shape[1]
    kv_cols = k_weight.shape[1]
    qkv_cols = q_cols + 2 * kv_cols
    ff_cols = gate_weight.shape[1]
    part = -(-ff_cols // (LINE * LANES)) * LANES
    q_heads, kv_heads = q_cols // HEAD_DIM, kv_cols // HEAD_DIM
    tile = local_rows * LINE // 2

    attn_own_weight = beside(info, q_weight, k_weight, v_weight, o_weight)
    attn_one = topo.swap(attn_own_weight, line, 0)
    gate_up_send, gate_up_keep = cut_columns(info, part, gate_weight, up_weight)

    attn_joined = join(info, attn_own_weight, attn_one)
    attn_two = topo.swap(attn_joined, line, 1)
    bias_all = jnp.concatenate([q_bias, k_bias, v_bias]).astype(F32)[None, :]
    gains = jnp.stack([attn_gain, mlp_gain]).astype(F32)
    attn_own, inputs, gains = open_rows(info, tokens, gains)
    gain_one, gain_two = gains[0:1], gains[1:2]
    attn_other = topo.other_core(attn_own)
    out_grad_in = turn_rows(info, out_grad)
    row_ids = jnp.arange(local_rows, dtype=jnp.int32)
    places = jnp.concatenate(
        [topo.core * local_rows + row_ids, (1 - topo.core) * local_rows + row_ids]
    )
    starts = sequence_info(lengths[0], places)
    frequency = jnp.power(ROPE_BASE, -2.0 * jnp.arange(HEAD_DIM // 2, dtype=F32) / HEAD_DIM)
    angles = (places - starts).astype(F32)[:, None] * frequency[None, :]
    cosine_half, sine_half = jnp.cos(angles), jnp.sin(angles)
    cosine = jnp.concatenate([cosine_half, cosine_half], axis=1)
    sine = jnp.concatenate([-sine_half, sine_half], axis=1)
    row_info = jnp.stack([starts, places], axis=1)
    col_info = places[None, :]
    from_line = [(0, 0), (0, shard_rows), (1, 0), (1, shard_rows)]
    from_exchange = [(0, 0), (1, 0), (2, 0), (2, shard_rows)]

    attn_piece = placed(info, shard_rows, from_line, attn_joined, attn_two)
    attn_near = topo.swap(attn_piece, square, 0)
    gate_up_one = topo.swap(tie(info, gate_up_send), line, 0)
    attn_in = join(info, attn_own, attn_other)
    q_joined, o_joined = join_split(info, (qkv_cols, q_cols), attn_piece, attn_near)
    q_all = [q_joined, topo.swap(q_joined, square, 1)]
    o_all = [o_joined, topo.swap(o_joined, square, 1)]
    gate_up_two = topo.swap(second_chunks(info, gate_up_keep, gate_up_one), line, 1)

    mixed, linear, mass = attend(
        info, attn_in, q_all, bias_all, cosine, sine, row_info, col_info, q_heads, kv_heads
    )
    down_send, down_keep = cut_columns(info, part, down_weight)
    down_one = topo.swap(down_send, line, 0)
    gate_up_piece = placed(
        info, shard_rows, from_exchange, gate_up_keep, gate_up_one, gate_up_two
    )
    gate_up_near = topo.swap(gate_up_piece, square, 0)
    *other_attn, own_attn = project(info, mixed, o_all, width)
    gate_up_far = topo.swap(gate_up_piece, square, 1)
    other_attn = [topo.other_core(half_rows) for half_rows in other_attn]
    mlp_own, state = state_rows(info, inputs, own_attn, other_attn, gain_two)
    mlp_one = topo.swap(mlp_own, line, 0)

    down_two = topo.swap(second_chunks(info, down_keep, down_one), line, 1)
    mlp_half = join(info, mlp_own, mlp_one)
    mlp_two = topo.swap(mlp_half, line, 1)
    mlp_early = topo.other_core(mlp_half)
    down_piece = placed(info, shard_rows, from_exchange, down_keep, down_one, down_two)
    wait_for(info, gate_up_near, gate_up_far)
    gate_up_last = topo.swap(tie(info, gate_up_near), square, 1)
    down_near = topo.swap(down_piece, square, 0)
    wait_for(info, mlp_two)
    mlp_late = topo.other_core(tie(info, mlp_two))
    grad_out_one = topo.swap(tie(info, out_grad_in), line, 0)
    wait_for(info, gate_up_last)
    gate_up = in_square(
        info, [gate_up_piece, gate_up_near, gate_up_far, gate_up_last], width
    )
    down = [join(info, down_piece, down_near)]
    down.append(topo.swap(down[0], square, 1))
    mlp_in = join(info, mlp_half, mlp_two, mlp_early, mlp_late)
    grad_out_two = topo.swap(tie(info, out_grad_in), line, 1)

    hidden, gate_factor, up_factor = forward(info, mlp_in, gate_up, tile)
    wait_for(info, grad_out_one)
    grad_out_last = topo.swap(tie(info, grad_out_one), line, 1)
    wait_for(info, grad_out_two)
    down = in_square(info, down, width)
    out_own, out_other = down_sum(info, hidden, down, tile)
    out_other = [topo.other_core(part_rows) for part_rows in cut_rows(info, out_other, 2)]
    pair = (0, 1, False), (2, 1, False)
    single = (0, 1, False), (1, 1, False)
    chunks = (0, 2, True), (1, 2, True)
    rows = local_rows
    grad_out_halves = [join(info, out_grad_in, grad_out_one), join(info, grad_out_two, grad_out_last)]
    grad_out_others = [topo.other_core(half_rows) for half_rows in grad_out_halves]
    out_keep, out_send = sum_split(info, rows, 2, *pair, [out_own], out_other)
    out_one = topo.swap(out_send, line, 1)
    grad_out_all = join(info, *grad_out_halves, *grad_out_others)
    factors = (grad_out_all, gate_factor, up_factor, gate_up, down)
    grads_other, *back_other = backward(info, 1, *factors, tile)
    back_other = [topo.other_core(part_rows) for part_rows in back_other]
    down_grad = functools.partial(grads_of, info, grad_out_all, [hidden], block)
    down_first = topo.swap(down_grad(3), square, 1)
    down_next = topo.swap(down_grad(2), square, 1)
    wait_for(info, out_one)
    grads_own, *back_own = backward(info, 0, *factors, tile)
    back_keep, back_send = sum_split(info, rows, 2, *pair, back_own, back_other)
    back_one = topo.swap(back_send, line, 1)
    wait_for(info, down_first, down_next)
    gate_up_grad = functools.partial(grads_of, info, mlp_in, [grads_own, grads_other], block)
    gate_up_first = topo.swap(gate_up_grad(3), square, 1)
    gate_up_send = gate_up_grad(2)
    down_last = topo.swap(down_grad(1, down_first), square, 0)
    down_kept = down_grad(0, down_next)
    back_keep, back_send = sum_split(info, rows, 1, *single, [back_keep], [back_one])
    back_two = topo.swap(back_send, line, 0)
    down_keep, down_send = sum_split(info, shard_rows, 2, *chunks, [down_kept], [down_last])
    gate_up_next = topo.swap(tie(info, gate_up_send), square, 1)
    gate_up_last = [
        topo.swap(gate_up_grad(1, gate_up_first, share), square, 0) for share in range(2)
    ]

    grad_state_low, grad_state, gain_two_grad = norm_back(
        info, state, back_keep, back_two, out_grad_in, gain_two, False
    )
    state_other = topo.other_core(grad_state_low)
    out_keep, out_send = sum_split(info, rows, 1, *single, [out_keep], [out_one])
    out_two = topo.swap(out_send, line, 0)
    down_one = topo.swap(tie(info, down_send), line, 0)
    grad_state_all = join(info, grad_state_low, state_other)
    grad_linear, bias_grad, own_part, other_part = attend_back(
        info,
        grad_state_all,
        o_all,
        q_all,
        linear,
        mass,
        cosine,
        sine,
        row_info,
        col_info,
        q_heads,
        kv_heads,
    )
    part_other = topo.other_core(other_part)
    down_two = topo.swap(second_chunks(info, down_keep, down_one), line, 1)
    q_full = grads_sent(info, attn_in, grad_linear, block)
    q_got = topo.swap(q_full, square, 1)
    o_full = grads_sent(info, grad_state_all, mixed, block)
    o_got = topo.swap(o_full, square, 1)
    block_out = close_rows(info, state, out_keep, out_two)
    gate_up_kept = gate_up_grad(0, gate_up_next)
    gate_up_keep, gate_up_send = sum_split(
        info, shard_rows, 2, *chunks, [gate_up_kept], gate_up_last
    )
    gate_up_one = topo.swap(gate_up_send, line, 0)
    (down_grads,) = columns_out(info, down_keep, down_one, down_two, part, ff_cols)
    tokens_grad, gain_one_grad = norm_back(
        info, inputs, own_part, part_other, grad_state, gain_one, True
    )
    sums = jnp.concatenate([bias_grad, gain_one_grad, gain_two_grad], axis=1)
    sums = sums.reshape(-1, LANES)
    shared = qkv_cols // LANES
    sums_got = topo.other_core(sums)
    sums = sum_rows(info, sums, sums_got, shared)
    sums_got = topo.swap(sums, square, 0)

    gate_up_two = topo.swap(second_chunks(info, gate_up_keep, gate_up_one), line, 1)
    q_kept, q_send = grads_kept(info, attn_in, grad_linear, block, q_got)
    q_last = topo.swap(q_send, square, 0)
    o_kept, o_send = grads_kept(info, grad_state_all, mixed, block, o_got)
    o_last = topo.swap(o_send, square, 0)
    sums = sum_rows(info, sums, sums_got, 0)
    sums_got = topo.swap(sums, square, 1)
    ordered = (0, 1, True), (2, 1, True)
    q_keep, q_send = sum_split(info, shard_rows, 2, *ordered, [q_kept], [q_last])
    q_one = topo.swap(q_send, line, 1)
    o_keep, o_send = sum_split(info, shard_rows, 2, *ordered, [o_kept], [o_last])
    o_one = topo.swap(o_send, line, 1)
    gate_grads, up_grads = columns_out(
        info, gate_up_keep, gate_up_one, gate_up_two, part, ff_cols
    )
    sums = sum_rows(info, sums, sums_got, 0)
    sums_got = topo.swap(sums, line, 0)
    q_keep, q_send = sum_split(info, shard_rows, 1, *single, [q_keep], [q_one])
    q_two = topo.swap(q_send, line, 0)
    sums = sum_rows(info, sums, sums_got, 0)
    sums_got = topo.swap(sums, line, 1)
    o_keep, o_send = sum_split(info, shard_rows, 1, *single, [o_keep], [o_one])
    o_two = topo.swap(o_send, line, 0)
    q_grads, k_grads, v_grads = sum_out(info, q_keep, q_two, (q_cols, kv_cols, kv_cols))
    (o_grads,) = sum_out(info, o_keep, o_two, (q_cols,))
    sums = sum_rows(info, sums, sums_got, 0).reshape(-1)
    own_bias = sums[:qkv_cols]
    gain_sum = sums[qkv_cols:].reshape(2, width)
    CLOCK[0] = None
    return (
        block_out,
        tokens_grad,
        gain_sum[0],
        q_grads,
        own_bias[:q_cols],
        k_grads,
        own_bias[q_cols : q_cols + kv_cols],
        v_grads,
        own_bias[q_cols + kv_cols :],
        o_grads,
        gain_sum[1],
        gate_grads,
        up_grads,
        down_grads,
    )


def solution(mesh):
    rows = P(("dp", "tensor"), None)
    both = P("dp", "tensor")
    half = P("tensor")
    in_specs = (
        rows, rows, P("dp", None), P(), both, half, both, half, both, half, both, P(), both, both, both,
    )
    out_specs = (
        rows, rows, P(), both, half, both, half, both, half, both, P(), both, both, both,
    )
    fast = mesh.shape["dp"] == LINE * LINE and mesh.shape["tensor"] == 2
    return jax.shard_map(
        per_device if fast else plain_device,
        mesh=mesh,
        in_specs=in_specs,
        out_specs=out_specs,
        check_vma=False,
    )
```

```python
import functools
import math

import jax
import jax.numpy as jnp
from jax import lax
from jax.experimental import pallas as pl
from jax.experimental.pallas import tpu as pltpu
from jax.sharding import PartitionSpec as P

HEAD_DIM = 128
EPSILON = 1e-06
ROPE_BASE = 1000000.0
MASKED = -1e30
LINE = 4
LANES = 128
BF = jnp.bfloat16
F32 = jnp.float32
VMEM_BYTES = 56 * 2**20
ANY = pl.BlockSpec(memory_space=pl.ANY)


def normalize(values):
    factor = lax.rsqrt(jnp.mean(values * values, axis=1, keepdims=True) + EPSILON)
    return (values * factor, factor)


def plain_norm_back(grad_normed, normed, factor, gain_vec):
    scaled = grad_normed * gain_vec[None, :]
    row_inner = jnp.mean(scaled * normed, axis=1, keepdims=True)
    return (factor * (scaled - normed * row_inner), jnp.sum(grad_normed * normed, axis=0))


def rope_tables(positions, width):
    half_width = width // 2
    frequency = jnp.power(ROPE_BASE, -2.0 * jnp.arange(half_width, dtype=F32) / width)
    angles = positions.astype(F32)[:, None] * frequency[None, :]
    return (jnp.cos(angles), jnp.sin(angles))


def rotate(values, cosine_table, sine_table):
    half_width = values.shape[-1] // 2
    lower_half = values[..., :half_width]
    upper_half = values[..., half_width:]
    return jnp.concatenate(
        [
            lower_half * cosine_table - upper_half * sine_table,
            upper_half * cosine_table + lower_half * sine_table,
        ],
        axis=-1,
    )


def unrotate(values, cosine_table, sine_table):
    return rotate(values, cosine_table, -sine_table)


def segment_info(length_row, places):
    seq_ends = jnp.cumsum(length_row)
    starts = seq_ends - length_row
    segment = jnp.sum((places[:, None] >= seq_ends[None, :]).astype(jnp.int32), axis=1)
    slot_ids = jnp.arange(length_row.shape[0], dtype=jnp.int32)
    offset = jnp.sum(jnp.where(segment[:, None] == slot_ids[None, :], starts[None, :], 0), axis=1)
    return (segment, places - offset)


class PlainTopo:
    def __init__(self):
        self.dp = lax.axis_size("dp")
        self.square = self.dp // LINE
        self.me = lax.axis_index("dp")
        self.core = lax.axis_index("tensor")
        self.line_at = self.me // self.square
        self.square_at = self.me % self.square
        line_bits = [self.square << i for i in range(LINE.bit_length() - 1)]
        square_bits = [1 << i for i in range(self.square.bit_length() - 1)]
        self.line = (line_bits, line_bits[::-1])
        self.squares = (square_bits, square_bits[::-1])

    def swap(self, array, bits, phase):
        perm = []
        for place in range(self.dp):
            for core in range(2):
                perm.append((place * 2 + core, (place ^ bits[core][phase]) * 2 + core))
        return lax.ppermute(array, ("dp", "tensor"), perm)

    def other_core(self, array):
        return lax.ppermute(array, "tensor", [(0, 1), (1, 0)])

    def offset(self, bits, index, unit):
        totals = [0, 0]
        for core in range(2):
            for phase, bit in enumerate(bits[core]):
                if index >> phase & 1:
                    totals[core] ^= bit // unit
        return jnp.where(self.core == 0, totals[0], totals[1])

    def gather(self, own, bits):
        pieces = [own]
        for phase in range(len(bits[0])):
            pieces = pieces + [self.swap(piece, bits, phase) for piece in pieces]
        return pieces

    def gather_joined(self, own, bits):
        joined = own
        for phase in range(len(bits[0])):
            joined = jnp.concatenate([joined, self.swap(joined, bits, phase)], axis=0)
        return joined

    def scatter_sum(self, array, bits):
        for phase in reversed(range(len(bits[0]))):
            half = array.shape[0] // 2
            got = self.swap(array[half:], bits, phase)
            array = (array[:half].astype(F32) + got.astype(F32)).astype(BF)
        return array

    def total(self, array):
        for bits in (self.line, self.squares):
            for phase in range(len(bits[0])):
                array = array + self.swap(array, bits, phase)
        return array

    def exchange(self, chunks, bits):
        rows = chunks[0].shape[0]
        held = [chunk for chunk in chunks]
        for phase in range(len(bits[0])):
            step = 1 << phase
            keep = [i for i in range(len(chunks)) if not i & step]
            keep = [i for i in keep if held[i] is not None]
            sent = jnp.concatenate([held[i + step] for i in keep], axis=0)
            got = self.swap(sent, bits, phase)
            parts = jnp.split(got, len(keep), axis=0)
            for i, part in zip(keep, parts):
                held[i] = jnp.concatenate([held[i], part], axis=0)
                held[i + step] = None
        return jnp.split(held[0], len(chunks), axis=0)

    def ordered(self, pieces, bits, unit, at):
        count = len(pieces)
        tables = []
        for core in range(2):
            table = [0] * count
            for index in range(count):
                total = 0
                for phase, bit in enumerate(bits[core]):
                    if index >> phase & 1:
                        total ^= bit // unit
                table[total] = index
            tables.append(table)
        tables = jnp.asarray(tables, jnp.int32)[self.core]
        stacked = jnp.stack(pieces)
        return [
            lax.dynamic_index_in_dim(
                stacked, lax.dynamic_index_in_dim(tables, place ^ at, 0, False), 0, False
            )
            for place in range(count)
        ]


def to_inner(rows, topo):
    count, width = rows.shape
    rest = width // topo.dp
    cut = rows.reshape(count, LINE, topo.square, rest).transpose(2, 0, 1, 3)
    cut = cut.reshape(topo.square, count, LINE * rest)
    return jnp.concatenate(
        [
            lax.dynamic_index_in_dim(cut, topo.square_at ^ i, 0, False)
            for i in range(topo.square)
        ],
        axis=1,
    )


def to_outer(rows, topo):
    count, width = rows.shape
    rest = width // topo.dp
    cut = rows.reshape(count, topo.square, LINE * rest).transpose(1, 0, 2)
    cut = jnp.stack(
        [
            lax.dynamic_index_in_dim(cut, topo.square_at ^ i, 0, False)
            for i in range(topo.square)
        ]
    )
    cut = cut.reshape(topo.square, count, LINE, rest).transpose(1, 2, 0, 3)
    return cut.reshape(count, width)


def dot(left, right):
    return jnp.dot(left, right, preferred_element_type=F32)


def dot_t(left, right):
    return lax.dot_general(left, right, (((1,), (1,)), ((), ())), preferred_element_type=F32)


def t_dot(left, right):
    return lax.dot_general(left, right, (((0,), (0,)), ((), ())), preferred_element_type=F32)


def attention_scores(queries, key_rows, allowed):
    score_scale = 1.0 / math.sqrt(queries.shape[-1])
    raw_scores = jnp.einsum("qgpd,kgd->gpqk", queries, key_rows, preferred_element_type=F32)
    return jnp.where(allowed[None, None], raw_scores * score_scale, MASKED)


def plain_device(
    tokens,
    out_grad,
    lengths,
    attn_gain,
    q_weight,
    q_bias,
    k_weight,
    k_bias,
    v_weight,
    v_bias,
    o_weight,
    mlp_gain,
    gate_weight,
    up_weight,
    down_weight,
):
    topo = PlainTopo()
    local_rows, width = tokens.shape
    group_rows = 2 * local_rows
    q_cols = q_weight.shape[1]
    kv_cols = k_weight.shape[1]
    qkv_cols = q_cols + 2 * kv_cols
    ff_cols = gate_weight.shape[1]
    part = -(-ff_cols // (LINE * LANES)) * LANES
    kv_groups = kv_cols // HEAD_DIM
    per_group = q_cols // HEAD_DIM // kv_groups
    score_scale = 1.0 / math.sqrt(HEAD_DIM)

    def line_gather(shard):
        pieces = jnp.split(topo.gather_joined(shard, topo.line), LINE, axis=0)
        return jnp.concatenate(topo.ordered(pieces, topo.line, topo.square, topo.line_at), axis=0)

    def square_gather(shard):
        pieces = topo.gather(shard, topo.squares)
        return jnp.concatenate(topo.ordered(pieces, topo.squares, 1, 0), axis=0)

    def square_scatter(grads):
        pieces = jnp.split(grads.astype(BF), topo.square, axis=0)
        by_index = topo.ordered(pieces, tuple(b for b in topo.squares), 1, 0)
        return topo.scatter_sum(jnp.concatenate(by_index, axis=0), topo.squares)

    def line_offset(index):
        return topo.line_at ^ topo.offset(topo.line, index, topo.square)

    def columns_in(shards):
        padded = [jnp.pad(s, ((0, 0), (0, LINE * part - ff_cols))) for s in shards]
        chunks = []
        for index in range(LINE):
            start = line_offset(index) * part
            chunks.append(
                jnp.concatenate(
                    [lax.dynamic_slice_in_dim(s, start, part, axis=1) for s in padded], axis=1
                )
            )
        got = topo.exchange(chunks, topo.line)
        return jnp.concatenate(topo.ordered(got, topo.line, topo.square, topo.line_at), axis=0)

    def columns_out(piece, count):
        rows = piece.shape[0] // LINE
        chunks = [
            lax.dynamic_slice_in_dim(piece, line_offset(index) * rows, rows, axis=0)
            for index in range(LINE)
        ]
        got = topo.ordered(
            topo.exchange(chunks, topo.line), topo.line, topo.square, topo.line_at
        )
        return [
            jnp.concatenate([g[:, i * part : (i + 1) * part] for g in got], axis=1)[
                :, :ff_cols
            ].astype(F32)
            for i in range(count)
        ]

    def rows_out(piece):
        rows = piece.shape[0] // LINE
        chunks = [
            lax.dynamic_slice_in_dim(piece, line_offset(index) * rows, rows, axis=0)
            for index in range(LINE)
        ]
        return topo.scatter_sum(jnp.concatenate(chunks, axis=0), topo.line).astype(F32)

    def both_cores(rows):
        return jnp.concatenate([rows, topo.other_core(rows)], axis=0)

    def core_sum(rows):
        half = rows.shape[0] // 2
        return rows[:half] + topo.other_core(rows[half:].astype(BF)).astype(F32)

    def line_tokens(rows):
        return both_cores(topo.gather_joined(rows, topo.line))

    def line_sum(partial):
        return topo.scatter_sum(core_sum(partial).astype(BF), topo.line).astype(F32)

    row_ids = jnp.arange(local_rows, dtype=jnp.int32)
    places = jnp.concatenate(
        [topo.core * local_rows + row_ids, (1 - topo.core) * local_rows + row_ids]
    )
    segment, positions = segment_info(lengths[0], places)
    allowed = (segment[:, None] == segment[None, :]) & (places[None, :] <= places[:, None])
    cosine_table, sine_table = rope_tables(positions, HEAD_DIM)
    q_cosine = cosine_table[:, None, None, :]
    q_sine = sine_table[:, None, None, :]
    k_cosine = cosine_table[:, None, :]
    k_sine = sine_table[:, None, :]

    inputs_low = to_inner(tokens, topo)
    out_grad_low = to_inner(out_grad, topo)
    gains = to_inner(jnp.stack([attn_gain, mlp_gain]), topo).astype(F32)
    gain_one, gain_two = gains[0], gains[1]
    inputs = inputs_low.astype(F32)
    bias_all = jnp.concatenate([q_bias, k_bias, v_bias]).astype(F32)

    qkv_local = jnp.concatenate([q_weight, k_weight, v_weight], axis=1)
    qkv_all = square_gather(line_gather(qkv_local))
    o_all = square_gather(line_gather(o_weight))
    down_all = square_gather(columns_in([down_weight]))
    grad_out_all = line_tokens(out_grad_low)
    gate_up = square_gather(columns_in([gate_weight, up_weight]))

    normed_one, factor_one = normalize(inputs)
    attn_in = both_cores((normed_one * gain_one[None, :]).astype(BF))
    linear = dot(attn_in, qkv_all) + bias_all[None, :]
    queries = rotate(
        linear[:, :q_cols].reshape(group_rows, kv_groups, per_group, HEAD_DIM), q_cosine, q_sine
    ).astype(BF)
    key_rows = rotate(
        linear[:, q_cols : q_cols + kv_cols].reshape(group_rows, kv_groups, HEAD_DIM),
        k_cosine,
        k_sine,
    ).astype(BF)
    values = linear[:, q_cols + kv_cols :].reshape(group_rows, kv_groups, HEAD_DIM).astype(BF)
    scores = attention_scores(queries, key_rows, allowed)
    row_peak = jnp.max(scores, axis=-1, keepdims=True)
    exponent = jnp.exp(scores - row_peak)
    row_mass = jnp.sum(exponent, axis=-1, keepdims=True)
    log_mass = row_peak + jnp.log(row_mass)
    probs_low = (exponent / row_mass).astype(BF)
    mixed_heads = jnp.einsum("gpqk,kgd->qgpd", probs_low, values, preferred_element_type=F32)
    mixed_heads = mixed_heads.reshape(group_rows, q_cols).astype(BF)
    hidden_state = inputs + core_sum(dot_t(mixed_heads, o_all))
    normed_two, factor_two = normalize(hidden_state)

    mlp_in = line_tokens((normed_two * gain_two[None, :]).astype(BF))
    grad_hidden = dot(grad_out_all, down_all)
    gate_up_out = dot(mlp_in, gate_up)
    gate_val = gate_up_out[:, :part]
    up_val = gate_up_out[:, part:]
    sigmoid_gate = jax.nn.sigmoid(gate_val)
    activated = gate_val * sigmoid_gate
    hidden_units = (activated * up_val).astype(BF)
    grad_gate = (
        grad_hidden * up_val * sigmoid_gate * (1.0 + gate_val * (1.0 - sigmoid_gate))
    ).astype(BF)
    grad_up = (grad_hidden * activated).astype(BF)
    grad_gate_up = jnp.concatenate([grad_gate, grad_up], axis=1)
    grad_normed_two = line_sum(dot_t(grad_gate_up, gate_up))
    block_out = (hidden_state + line_sum(dot_t(hidden_units, down_all))).astype(BF)
    gate_grads, up_grads = columns_out(square_scatter(t_dot(mlp_in, grad_gate_up)), 2)
    (down_grads,) = columns_out(square_scatter(t_dot(grad_out_all, hidden_units)), 1)

    back_two, gain_two_grad = plain_norm_back(grad_normed_two, normed_two, factor_two, gain_two)
    grad_state = out_grad_low.astype(F32) + back_two
    grad_state_all = both_cores(grad_state.astype(BF))
    o_grads = rows_out(square_scatter(t_dot(grad_state_all, mixed_heads)))
    grad_mixed = dot(grad_state_all, o_all)
    grad_heads = grad_mixed.astype(BF).reshape(group_rows, kv_groups, per_group, HEAD_DIM)
    scores_again = attention_scores(queries, key_rows, allowed)
    prob_rows = jnp.exp(scores_again - log_mass)
    grad_probs = jnp.einsum("qgpd,kgd->gpqk", grad_heads, values, preferred_element_type=F32)
    row_inner = jnp.sum(prob_rows * grad_probs, axis=-1, keepdims=True)
    grad_scores = (prob_rows * (grad_probs - row_inner) * score_scale).astype(BF)
    grad_values = jnp.einsum(
        "gpqk,qgpd->kgd", prob_rows.astype(BF), grad_heads, preferred_element_type=F32
    )
    grad_queries = jnp.einsum("gpqk,kgd->qgpd", grad_scores, key_rows, preferred_element_type=F32)
    grad_keys = jnp.einsum("gpqk,qgpd->kgd", grad_scores, queries, preferred_element_type=F32)
    grad_linear = jnp.concatenate(
        [
            unrotate(grad_queries, q_cosine, q_sine).reshape(group_rows, q_cols),
            unrotate(grad_keys, k_cosine, k_sine).reshape(group_rows, kv_cols),
            grad_values.reshape(group_rows, kv_cols),
        ],
        axis=1,
    ).astype(BF)
    bias_grad = jnp.sum(grad_linear.astype(F32), axis=0)
    qkv_grads = rows_out(square_scatter(t_dot(attn_in, grad_linear)))
    grad_normed_one = core_sum(dot_t(grad_linear, qkv_all))
    back_one, gain_one_grad = plain_norm_back(grad_normed_one, normed_one, factor_one, gain_one)
    tokens_grad = (grad_state + back_one).astype(BF)
    gain_grads = to_outer(jnp.stack([gain_one_grad, gain_two_grad]), topo)
    gain_grads = gain_grads + topo.other_core(gain_grads)
    small = topo.total(jnp.concatenate([bias_grad, gain_grads.reshape(-1)]).reshape(-1, LANES))
    small = small.reshape(-1)
    own_bias = small[:qkv_cols]
    gain_sum = small[qkv_cols:].reshape(2, width)
    return (
        to_outer(block_out, topo),
        to_outer(tokens_grad, topo),
        gain_sum[0],
        qkv_grads[:, :q_cols],
        own_bias[:q_cols],
        qkv_grads[:, q_cols : q_cols + kv_cols],
        own_bias[q_cols : q_cols + kv_cols],
        qkv_grads[:, q_cols + kv_cols : qkv_cols],
        own_bias[q_cols + kv_cols :],
        o_grads,
        gain_sum[1],
        gate_grads,
        up_grads,
        down_grads,
    )


def nn(left, right):
    return jnp.dot(left, right, preferred_element_type=F32)


def nt(left, right):
    return lax.dot_general(left, right, (((1,), (1,)), ((), ())), preferred_element_type=F32)


def tn(left, right):
    return lax.dot_general(left, right, (((0,), (0,)), ((), ())), preferred_element_type=F32)


def shape(dims, kind):
    return jax.ShapeDtypeStruct(dims, kind)


def whole(dims):
    return pl.BlockSpec(dims, lambda *_: (0,) * len(dims))


OFF, NEIGHBOUR, INDEX, AT, OTHER = 0, 4, 8, 12, 13


class Topo:
    def __init__(self):
        self.dp = lax.axis_size("dp")
        me = lax.axis_index("dp")
        core = lax.axis_index("tensor")
        line_at, square_at = me >> 2, me & 3

        def by_core(index):
            return jnp.where(core == 0, index, (index >> 1) | ((index & 1) << 1))

        self.core = core
        self.square_at = square_at
        self.line = ((LINE, 2 * LINE), (2 * LINE, LINE))
        self.square = ((1, 2), (2, 1))
        count = jnp.arange(LINE, dtype=jnp.int32)
        self.info = jnp.concatenate(
            [
                by_core(count),
                line_at ^ by_core(count),
                by_core(line_at ^ count),
                jnp.stack([square_at, 1 - core]),
            ]
        ).astype(jnp.int32)

    def swap(self, array, bits, phase):
        perm = []
        for place in range(self.dp):
            for core in range(2):
                flip = bits[core][phase] if phase < 2 else bits[core][0] ^ bits[core][1]
                perm.append((place * 2 + core, (place ^ flip) * 2 + core))
        return lax.ppermute(array, ("dp", "tensor"), perm)

    def other_core(self, array):
        return lax.ppermute(array, "tensor", [(0, 1), (1, 0)])

    def both_ways(self, array):
        return lax.all_to_all(array, "tensor", 0, 0, tiled=True)


CLOCK = [None]
TOKEN = jax.ShapeDtypeStruct((8, 128), F32)
IN_VMEM = pl.BlockSpec(memory_space=pltpu.VMEM)
IN_SMEM = pl.BlockSpec(memory_space=pltpu.SMEM)


def in_order(body, ins, outs):
    taken = 0 if CLOCK[0] is None else 1

    def full(*refs):
        body(*refs[:ins], *refs[ins + taken : ins + taken + outs], *refs[ins + taken + outs + 1 :])

    return full


def run(kernel, single, args):
    taken = [] if CLOCK[0] is None else [CLOCK[0]]
    *out, CLOCK[0] = kernel(*args, *taken)
    return out[0] if single else out


def as_list(value):
    return list(value) if isinstance(value, (list, tuple)) else [value]


def call(body, grid, in_specs, out_specs, out_shape, scratch, info, *args, mib=32):
    outs = as_list(out_shape)
    late = 0 if CLOCK[0] is None else 1
    kernel = pl.pallas_call(
        in_order(body, 1 + len(in_specs), len(outs)),
        grid_spec=pltpu.PrefetchScalarGridSpec(
            num_scalar_prefetch=1,
            grid=grid,
            in_specs=list(in_specs) + [IN_VMEM] * late,
            out_specs=as_list(out_specs) + [IN_VMEM],
            scratch_shapes=list(scratch),
        ),
        out_shape=outs + [TOKEN],
        compiler_params=pltpu.CompilerParams(vmem_limit_bytes=mib * 2**20),
        cost_estimate=pl.CostEstimate(flops=1000, bytes_accessed=1000, transcendentals=0),
        name=body.__qualname__.split(".")[0],
    )
    return run(kernel, not isinstance(out_shape, (list, tuple)), (info,) + args)


def small(body, out_shape, scratch, info, *args, mib=10, out_spec=IN_VMEM):
    outs = as_list(out_shape)
    late = 0 if CLOCK[0] is None else 1
    kernel = pl.pallas_call(
        in_order(body, 1 + len(args), len(outs)),
        in_specs=[IN_SMEM] + [IN_VMEM] * (len(args) + late),
        out_specs=[out_spec] * len(outs) + [IN_VMEM],
        scratch_shapes=list(scratch),
        out_shape=outs + [TOKEN],
        compiler_params=pltpu.CompilerParams(vmem_limit_bytes=mib * 2**20),
        cost_estimate=pl.CostEstimate(flops=1000, bytes_accessed=1000, transcendentals=0),
        name=body.__qualname__.split(".")[0],
    )
    return run(kernel, not isinstance(out_shape, (list, tuple)), (info,) + args)


def tie(info, array):
    def body(info_ref, in_ref, out_ref):
        out_ref[...] = in_ref[...]

    return small(body, shape(array.shape, array.dtype), [], info, array)


def spacer(info, topo, array):
    wait_for(info, topo.other_core(tie(info, array)))


def wait_for(info, *arrays):
    def body(*refs):
        del refs

    late = 0 if CLOCK[0] is None else 1
    kernel = pl.pallas_call(
        body,
        in_specs=[ANY] * len(arrays) + [IN_VMEM] * late,
        out_specs=[IN_VMEM],
        out_shape=[TOKEN],
        compiler_params=pltpu.CompilerParams(vmem_limit_bytes=16 * 2**20),
        cost_estimate=pl.CostEstimate(flops=1, bytes_accessed=1, transcendentals=0),
        name="wait_for",
    )
    (CLOCK[0],) = kernel(*arrays, *([CLOCK[0]] if late else []))


def join(info, *args):
    def body(info_ref, *refs):
        start = 0
        for ref in refs[:-1]:
            refs[-1][start : start + ref.shape[0]] = ref[...]
            start += ref.shape[0]

    rows = sum(a.shape[0] for a in args)
    return small(body, shape((rows,) + args[0].shape[1:], args[0].dtype), [], info, *args)


def join_far(info, *args):
    def body(info_ref, *refs):
        ins, out, sems = refs[: len(args)], refs[len(args)], refs[-1]
        start = 0
        copies = []
        for index, ref in enumerate(ins):
            rows = ref.shape[0]
            copies.append(
                pltpu.make_async_copy(ref, out.at[pl.ds(start, rows)], sems.at[index])
            )
            start += rows
        for copy in copies:
            copy.start()
        for copy in copies:
            copy.wait()

    rows = sum(a.shape[0] for a in args)
    return small(
        body,
        shape((rows,) + args[0].shape[1:], args[0].dtype),
        [pltpu.SemaphoreType.DMA((len(args),))],
        info,
        *args,
        out_spec=ANY,
    )


def join_split(info, widths, *args):
    rows = sum(a.shape[0] for a in args)

    def body(info_ref, *refs):
        ins, outs = refs[: len(args)], refs[len(args) :]
        low = 0
        for ref in ins:
            start = 0
            for out, cols in zip(outs, widths):
                out[low : low + ref.shape[0]] = ref[:, start : start + cols]
                start += cols
            low += ref.shape[0]

    return small(body, [shape((rows, cols), BF) for cols in widths], [], info, *args)


def beside(info, *args):
    def body(info_ref, *refs):
        start = 0
        for ref in refs[:-1]:
            refs[-1][:, start : start + ref.shape[1]] = ref[...]
            start += ref.shape[1]

    cols = sum(a.shape[1] for a in args)
    return small(body, shape((args[0].shape[0], cols), args[0].dtype), [], info, *args)


def placed(info, rows, takes, *args):
    def body(info_ref, *refs):
        for index, (which, start) in enumerate(takes):
            target = pl.multiple_of(info_ref[NEIGHBOUR + index] * rows, 16)
            refs[-1][pl.ds(target, rows)] = refs[which][start : start + rows]

    return small(body, shape((LINE * rows, args[0].shape[1]), BF), [], info, *args)


def second_chunks(info, kept, got):
    rows = kept.shape[0] // 2

    def body(info_ref, kept_ref, got_ref, out_ref):
        out_ref[:rows] = kept_ref[rows:]
        out_ref[rows:] = got_ref[rows:]

    return small(body, shape(kept.shape, BF), [], info, kept, got)


def cut_columns(info, part, *weights):
    count = len(weights)
    rows, cols = weights[0].shape
    short = cols - (LINE - 1) * part

    def body(info_ref, *refs):
        ins, outs = refs[:count], refs[count:]
        for index in range(LINE):
            at = info_ref[NEIGHBOUR + index]
            out = outs[1 - index % 2]
            low = index // 2 * rows
            for which, ref in enumerate(ins):
                start = pl.multiple_of(at * part, LANES)
                first = which * part
                out[low : low + rows, first : first + short] = ref[:, pl.ds(start, short)]
                if short < part:
                    rest = pl.multiple_of(jnp.minimum(at, LINE - 2) * part + short, LANES)
                    tail = ref[:, pl.ds(rest, part - short)]
                    out[low : low + rows, first + short : first + part] = jnp.where(
                        at < LINE - 1, tail, jnp.zeros_like(tail)
                    )

    return small(body, [shape((2 * rows, count * part), BF)] * 2, [], info, *weights)


def square_blocks(info_ref, pieces, width):
    rows = width // LINE
    index = 0
    for piece in pieces:
        for block in range(piece.shape[0] // rows):
            start = pl.multiple_of(info_ref[OFF + index] * rows, LANES)
            yield pl.ds(start, rows), piece[block * rows : (block + 1) * rows]
            index += 1


def inward(values, at, store):
    width = values.shape[1]
    block = width // LINE
    rest = block // LINE
    for square in range(LINE):
        parts = [
            values[:, line * block + square * rest : line * block + (square + 1) * rest]
            for line in range(LINE)
        ]
        start = pl.multiple_of((square ^ at) * block, LANES)
        store(pl.ds(start, block), jnp.concatenate(parts, axis=1))


def outward(ref, at):
    width = ref.shape[1]
    block = width // LINE
    rest = block // LINE
    blocks = []
    for square in range(LINE):
        start = pl.multiple_of((square ^ at) * block, LANES)
        blocks.append(ref[:, pl.ds(start, block)])
    parts = []
    for line in range(LINE):
        for square in range(LINE):
            parts.append(blocks[square][:, line * rest : (line + 1) * rest])
    return jnp.concatenate(parts, axis=1)


def turn_rows(info, rows):
    def body(info_ref, rows_ref, out_ref, held):
        def store(cols, block):
            held[:, cols] = block

        inward(rows_ref[...].astype(F32), info_ref[AT], store)
        out_ref[...] = held[...].astype(BF)

    return small(body, shape(rows.shape, BF), [pltpu.VMEM(rows.shape, F32)], info, rows)


def open_rows(info, rows, gains):
    def body(info_ref, rows_ref, gains_ref, out_ref, in_ref, gain_ref, held):
        def store_gain(cols, block):
            gain_ref[:, cols] = block

        def store(cols, block):
            held[:, cols] = block

        inward(gains_ref[...], info_ref[AT], store_gain)
        inward(rows_ref[...].astype(F32), info_ref[AT], store)
        values = held[...]
        in_ref[...] = values.astype(BF)
        factor = lax.rsqrt(jnp.mean(values * values, axis=1, keepdims=True) + EPSILON)
        out_ref[...] = (values * factor * gain_ref[0:1, :]).astype(BF)

    return small(
        body,
        [shape(rows.shape, BF), shape(rows.shape, BF), shape(gains.shape, F32)],
        [pltpu.VMEM(rows.shape, F32)],
        info,
        rows,
        gains,
    )


def state_rows(info, rows, own, got, gain):
    def body(info_ref, rows_ref, own_ref, early_ref, late_ref, gain_ref, out_ref, state_ref):
        half = dims[0] // 2
        for start, got_ref in ((0, early_ref), (half, late_ref)):
            span = pl.ds(start, half)
            values = rows_ref[span].astype(F32) + (own_ref[span] + got_ref[...].astype(F32))
            state_ref[span] = values
            factor = lax.rsqrt(jnp.mean(values * values, axis=1, keepdims=True) + EPSILON)
            out_ref[span] = (values * factor * gain_ref[...]).astype(BF)

    dims = rows.shape
    return small(
        body, [shape(dims, BF), shape(dims, F32)], [], info, rows, own, *got, gain
    )


def close_rows(info, state, own, got):
    def body(info_ref, state_ref, own_ref, got_ref, out_ref, held):
        held[...] = state_ref[...] + (own_ref[...].astype(F32) + got_ref[...].astype(F32))
        out_ref[...] = outward(held, info_ref[AT]).astype(BF)

    dims = state.shape
    return small(
        body,
        shape(dims, BF),
        [pltpu.VMEM(dims, F32)],
        info,
        state,
        own,
        got,
    )


def norm_back(info, values, own, got, base, gain, turn):
    def body(info_ref, values_ref, own_ref, got_ref, base_ref, gain_ref, *refs):
        values = values_ref[...].astype(F32)
        factor = lax.rsqrt(jnp.mean(values * values, axis=1, keepdims=True) + EPSILON)
        normed = values * factor
        grad = own_ref[...].astype(F32) + got_ref[...].astype(F32)
        scaled = grad * gain_ref[...]
        row_inner = jnp.mean(scaled * normed, axis=1, keepdims=True)
        total = base_ref[...].astype(F32) + factor * (scaled - normed * row_inner)
        gain_grad = jnp.sum(grad * normed, axis=0, keepdims=True)
        if turn:
            out_ref, gain_out_ref, held, gain_held = refs
            held[...] = total
            out_ref[...] = outward(held, info_ref[AT]).astype(BF)
        else:
            low_ref, out_ref, gain_out_ref, gain_held = refs
            out_ref[...] = total
            low_ref[...] = total.astype(BF)
        gain_held[...] = gain_grad
        gain_out_ref[...] = outward(gain_held, info_ref[AT])

    dims = values.shape
    kinds = (BF,) if turn else (BF, F32)
    return small(
        body,
        [shape(dims, kind) for kind in kinds] + [shape(gain.shape, F32)],
        ([pltpu.VMEM(dims, F32)] if turn else []) + [pltpu.VMEM(gain.shape, F32)],
        info,
        values,
        own,
        got,
        base,
        gain,
    )


def turned(values, cosine, sine):
    return values * cosine + pltpu.roll(values, HEAD_DIM // 2, 1) * sine


def attend(info, rows, pieces, bias, cosine, sine, row_info, col_info, q_heads, kv_heads):
    count, cols = len(pieces), pieces[0].shape[1]
    group, width = rows.shape
    q_cols = q_heads * HEAD_DIM

    def body(info_ref, in_ref, *refs):
        pieces = refs[:count]
        bias_ref, cos_ref, sin_ref, row_ref, col_ref = refs[count : count + 5]
        mixed_ref, lin_ref, mass_ref = refs[count + 5 :]
        cosine, sine = cos_ref[...], sin_ref[...]
        scale = 1.0 / math.sqrt(HEAD_DIM)
        linear = bias_ref[...]
        for cols, piece in square_blocks(info_ref, pieces, width):
            linear = linear + nn(in_ref[:, cols], piece)
        for head in range(q_heads + 2 * kv_heads):
            cols = slice(head * HEAD_DIM, (head + 1) * HEAD_DIM)
            part = linear[:, cols]
            if head < q_heads + kv_heads:
                part = turned(part, cosine, sine)
            lin_ref[:, cols] = part.astype(BF)
        allowed = (row_ref[:, 0:1] <= col_ref[...]) & (col_ref[...] <= row_ref[:, 1:2])
        for head in range(q_heads):
            key = q_heads + head // (q_heads // kv_heads)
            value = key + kv_heads
            cols = slice(head * HEAD_DIM, (head + 1) * HEAD_DIM)
            raw = nt(lin_ref[:, cols], lin_ref[:, key * HEAD_DIM : (key + 1) * HEAD_DIM])
            scores = jnp.where(allowed, raw * scale, MASKED)
            peak = jnp.max(scores, axis=1, keepdims=True)
            exponent = jnp.exp(scores - peak)
            mass = jnp.sum(exponent, axis=1, keepdims=True)
            mass_ref[:, head : head + 1] = peak + jnp.log(mass)
            probs = (exponent * (1.0 / mass)).astype(BF)
            mixed_ref[:, cols] = nn(
                probs, lin_ref[:, value * HEAD_DIM : (value + 1) * HEAD_DIM]
            ).astype(BF)

    plain = (bias, cosine, sine, row_info, col_info)
    return small(
        body,
        [shape((group, q_cols), BF), shape((group, cols), BF), shape((group, LANES), F32)],
        [],
        info,
        rows,
        *pieces,
        *plain,
        mib=12,
    )


def project(info, rows, pieces, width):
    count, cols = len(pieces), pieces[0].shape[1]
    half = rows.shape[0] // 2

    def body(info_ref, in_ref, *refs):
        pieces = refs[:count]
        early_ref, late_ref, own_ref = refs[count:]
        for cols, piece in square_blocks(info_ref, pieces, width):
            both = nt(in_ref[...], piece)
            own_ref[:, cols] = both[:half]
            early_ref[:, cols] = both[half : half + half // 2].astype(BF)
            late_ref[:, cols] = both[half + half // 2 :].astype(BF)

    return small(
        body,
        [shape((half // 2, width), BF)] * 2 + [shape((half, width), F32)],
        [],
        info,
        rows,
        *pieces,
    )


def attend_back(
    info, state, o_pieces, pieces, linear, mass, cosine, sine, row_info, col_info, q_heads, kv_heads
):
    count, cols = len(pieces), pieces[0].shape[1]
    group, width = state.shape
    q_cols = q_heads * HEAD_DIM
    half = group // 2

    def body(info_ref, state_ref, *refs):
        o_refs, q_refs = refs[:count], refs[count : 2 * count]
        lin_ref, mass_ref, cos_ref, sin_ref, row_ref, col_ref = refs[2 * count : 2 * count + 6]
        grad_ref, bias_ref, own_ref, other_ref = refs[2 * count + 6 : 2 * count + 10]
        heads_ref = refs[-1]
        cosine, sine = cos_ref[...], -sin_ref[...]
        scale = 1.0 / math.sqrt(HEAD_DIM)
        heads = 0.0
        for cols, piece in square_blocks(info_ref, o_refs, width):
            heads = heads + nn(state_ref[:, cols], piece)
        heads_ref[...] = heads.astype(BF)
        allowed = (row_ref[:, 0:1] <= col_ref[...]) & (col_ref[...] <= row_ref[:, 1:2])
        per_group = q_heads // kv_heads
        for place in range(kv_heads):
            key_cols = slice((q_heads + place) * HEAD_DIM, (q_heads + place + 1) * HEAD_DIM)
            first = q_heads + kv_heads + place
            value_cols = slice(first * HEAD_DIM, (first + 1) * HEAD_DIM)
            keys, values = lin_ref[:, key_cols], lin_ref[:, value_cols]
            grad_keys, grad_values = 0.0, 0.0
            for head in range(place * per_group, (place + 1) * per_group):
                cols = slice(head * HEAD_DIM, (head + 1) * HEAD_DIM)
                queries, grads = lin_ref[:, cols], heads_ref[:, cols]
                scores = jnp.where(allowed, nt(queries, keys) * scale, MASKED)
                probs = jnp.exp(scores - mass_ref[:, head : head + 1])
                grad_probs = nt(grads, values)
                inner = jnp.sum(probs * grad_probs, axis=1, keepdims=True)
                grad_scores = (probs * (grad_probs - inner) * scale).astype(BF)
                grad_values += tn(probs.astype(BF), grads)
                grad_keys += tn(grad_scores, queries)
                grad_ref[:, cols] = turned(nn(grad_scores, keys), cosine, sine).astype(BF)
            grad_ref[:, key_cols] = turned(grad_keys, cosine, sine).astype(BF)
            grad_ref[:, value_cols] = grad_values.astype(BF)
        bias_ref[...] = jnp.sum(grad_ref[...].astype(F32), axis=0, keepdims=True)
        for cols, piece in square_blocks(info_ref, q_refs, width):
            both = nt(grad_ref[...], piece)
            own_ref[:, cols] = both[:half]
            other_ref[:, cols] = both[half:].astype(BF)

    plain = (linear, mass, cosine, sine, row_info, col_info)
    return small(
        body,
        [
            shape((group, cols), BF),
            shape((1, cols), F32),
            shape((half, width), F32),
            shape((half, width), BF),
        ],
        [pltpu.VMEM((group, q_cols), BF)],
        info,
        state,
        *o_pieces,
        *pieces,
        *plain,
        mib=14,
    )


def in_square(info, pieces, width):
    def body(info_ref, *refs):
        for rows, block in square_blocks(info_ref, refs[:-1], width):
            refs[-1][rows] = block

    return small(body, shape((width, pieces[0].shape[1]), BF), [], info, *pieces)


def forward(info, x, gate_up, tile, step=256):
    part = gate_up.shape[1] // 2
    total, width = x.shape
    spans = [(low, min(low + step, part)) for low in range(0, part, step)]

    def body(info_ref, x_ref, weight, hid_ref, gate_ref, up_ref):
        x = x_ref[...]
        for low, high in spans:
            gate = nn(x, weight[:, low:high])
            up = nn(x, weight[:, part + low : part + high])
            share = 1.0 / (1.0 + jnp.exp(-gate))
            active = gate * share
            hid_ref[:, low:high] = (active * up).astype(BF)
            gate_ref[:, low:high] = (up * share * (1.0 + gate * (1.0 - share))).astype(BF)
            up_ref[:, low:high] = active.astype(BF)

    return call(
        body,
        (total // tile,),
        [pl.BlockSpec((tile, width), lambda i, _: (i, 0)), IN_VMEM],
        [pl.BlockSpec((tile, part), lambda i, _: (i, 0))] * 3,
        [shape((total, part), BF)] * 3,
        [],
        info,
        x,
        gate_up,
        mib=12,
    )


def halves_spec(tile, width, steps, spread):
    half = steps // 2

    def later(i, info_ref):
        first = info_ref[OTHER] * half if spread else 0
        return (first + jnp.maximum(i - half, 0), 0)

    return [
        pl.BlockSpec((tile, width), lambda i, _: (jnp.minimum(i, half - 1), 0)),
        pl.BlockSpec((tile, width), later),
    ]


def cut_rows(info, array, count):
    rows = array.shape[0] // count

    def body(info_ref, in_ref, *outs):
        for index, out in enumerate(outs):
            out[...] = in_ref[index * rows : (index + 1) * rows]

    return small(body, [shape((rows, array.shape[1]), array.dtype)] * count, [], info, array)


def store_half(value, steps, first_ref, second_ref):
    early = pl.program_id(0) < steps // 2

    @pl.when(early)
    def _():
        first_ref[...] = value

    @pl.when(jnp.logical_not(early))
    def _():
        second_ref[...] = value


def down_sum(info, hidden, down, tile):
    width = down.shape[0]
    total, part = hidden.shape
    steps = total // tile

    def body(info_ref, hid_ref, weight, own_ref, other_ref):
        value = nt(hid_ref[...], weight[...]).astype(BF)
        store_half(value, steps, own_ref, other_ref)

    return call(
        body,
        (steps,),
        [pl.BlockSpec((tile, part), lambda i, _: (i, 0)), IN_VMEM],
        halves_spec(tile, width, steps, False),
        [shape((total // 2, width), BF)] * 2,
        [],
        info,
        hidden,
        down,
        mib=11,
    )


def backward(info, half, g, gate_factor, up_factor, gate_up, down, tile, step=256):
    part = down.shape[1]
    total, width = g.shape[0] // 2, g.shape[1]
    steps = total // tile
    spans = [(low, min(low + step, part)) for low in range(0, part, step)]

    def body(info_ref, g_ref, gate_ref, up_ref, gate_up_ref, down_ref, grad_ref, *back_refs):
        g = g_ref[...]
        for low, high in spans:
            grad = nn(g, down_ref[:, low:high])
            grad_ref[:, low:high] = (grad * gate_ref[:, low:high].astype(F32)).astype(BF)
            grad_ref[:, part + low : part + high] = (
                grad * up_ref[:, low:high].astype(F32)
            ).astype(BF)
        value = nt(grad_ref[...], gate_up_ref[...]).astype(BF)
        for number, back_ref in enumerate(back_refs):

            @pl.when(pl.program_id(0) == number)
            def _(back_ref=back_ref):
                back_ref[...] = value

    return call(
        body,
        (steps,),
        [pl.BlockSpec((tile, cols), lambda i, _: (half * steps + i, 0)) for cols in (width, part, part)]
        + [IN_VMEM] * 2,
        [pl.BlockSpec((tile, 2 * part), lambda i, _: (i, 0))] + [whole((tile, width))] * steps,
        [shape((total, 2 * part), BF)] + [shape((tile, width), BF)] * steps,
        [],
        info,
        g,
        gate_factor,
        up_factor,
        gate_up,
        down,
        mib=18,
    )


def rows_spec(block, rights, where):
    rows = rights[0].shape[0]
    return [
        pl.BlockSpec((rows, block), lambda i, info_ref, r=r: (r, info_ref[OFF + where(i)]))
        for r in range(len(rights))
    ]


def grads_of(info, left, rights, block, index, got=None, share=None):
    rows, cols = rights[0].shape
    parts = len(rights)
    cols = cols if share is None else cols // 2
    tile = next(t for t in (768, 512, 384, 256, 128) if cols % t == 0)
    first = 0 if share is None else share * (cols // tile)

    def body(info_ref, *refs):
        value = 0.0
        for r in range(parts):
            value = value + tn(refs[r][...], refs[parts + r][...])
        if got is not None:
            value = value + refs[2 * parts][...].astype(F32)
        refs[-1][...] = value.astype(BF)

    out = pl.BlockSpec((block, tile), lambda i, _: (0, i))
    taken = pl.BlockSpec((block, tile), lambda i, _: (0, first + i))
    return call(
        body,
        (cols // tile,),
        rows_spec(block, rights, lambda i: index)
        + [pl.BlockSpec((rows, tile), lambda i, _: (0, first + i))] * parts
        + ([] if got is None else [taken]),
        out,
        shape((block, cols), BF),
        [],
        info,
        *([left] * parts),
        *rights,
        *([] if got is None else [got]),
        mib=12,
    )


def grads_sent(info, left, right, block):
    total, cols = right.shape

    def body(info_ref, left_ref, right_ref, out_ref):
        out_ref[...] = tn(left_ref[...], right_ref[...]).astype(BF)

    return call(
        body,
        (2,),
        rows_spec(block, [right], lambda i: 2 + i) + [whole(right.shape)],
        pl.BlockSpec((block, cols), lambda i, _: (i, 0)),
        shape((2 * block, cols), BF),
        [],
        info,
        left,
        right,
        mib=14,
    )


def grads_kept(info, left, right, block, got):
    total, cols = right.shape

    def body(info_ref, left_ref, right_ref, got_ref, keep_ref, send_ref):
        value = (tn(left_ref[...], right_ref[...]) + got_ref[...].astype(F32)).astype(BF)
        store_half(value, 2, keep_ref, send_ref)

    return call(
        body,
        (2,),
        rows_spec(block, [right], lambda i: i)
        + [whole(right.shape), pl.BlockSpec((block, cols), lambda i, _: (i, 0))],
        [whole((block, cols))] * 2,
        [shape((block, cols), BF)] * 2,
        [],
        info,
        left,
        right,
        got,
        mib=14,
    )


def sum_split(info, block, count, keep_at, send_at, lefts, rights, spare=0):
    cols = lefts[0].shape[1]
    pieces = len(lefts)
    wide = rights[0].shape[1]
    sizes = (lefts[0].shape[0], rights[0].shape[0])

    def rows_of(refs, size, low, high):
        which = low // size
        return refs[which][low - which * size : high - which * size].astype(F32)

    def body(info_ref, *refs):
        ins, outs = refs[:-2], refs[-2:]
        left_refs, right_refs = ins[:pieces], ins[pieces:]
        for out, (first, stride, along) in zip(outs, (keep_at, send_at)):
            for step in range(count):
                index = first + stride * step
                if along:
                    rows = pl.ds(pl.multiple_of(info_ref[NEIGHBOUR + index] * block, 16), block)
                    for number, right in enumerate(right_refs):
                        span = slice(number * wide, (number + 1) * wide)
                        total = left_refs[0][rows, span].astype(F32) + right[rows].astype(F32)
                        out[step * block : (step + 1) * block, span] = total.astype(BF)
                    continue
                low, high = index * block, (index + 1) * block
                while low < high:
                    end = min([high] + [(low // size + 1) * size for size in sizes])
                    total = rows_of(left_refs, sizes[0], low, end)
                    total = total + rows_of(right_refs, sizes[1], low, end)
                    start = step * block + low - index * block
                    out[start : start + end - low] = total.astype(BF)
                    low = end

    sizes_out = (count * block, count * block + spare)
    return small(
        body, [shape((size, cols), BF) for size in sizes_out], [], info, *lefts, *rights
    )


def sum_out(info, left, right, widths):
    rows = left.shape[0]

    def body(info_ref, left_ref, right_ref, *outs):
        total = left_ref[...].astype(F32) + right_ref[...].astype(F32)
        start = 0
        for out, cols in zip(outs, widths):
            out[...] = total[:, start : start + cols]
            start += cols

    return small(
        body,
        [shape((rows, cols), F32) for cols in widths],
        [],
        info,
        left,
        right,
    )


def sum_rows(info, own, got, first):
    def body(info_ref, own_ref, got_ref, out_ref):
        if first:
            out_ref[:first] = own_ref[:first]
        out_ref[first:] = own_ref[first:] + got_ref[first:]

    return small(body, shape(own.shape, F32), [], info, own, got)


def columns_out(info, kept, got, last, part, cols):
    rows = kept.shape[0] // 2
    count = kept.shape[1] // part

    def body(info_ref, kept_ref, got_ref, last_ref, *outs):
        pieces = [kept_ref[:rows], got_ref[:rows], last_ref[:rows], last_ref[rows:]]
        for place in range(LINE):
            low = place * part
            span = min(part, cols - low)
            for index, piece in enumerate(pieces):

                @pl.when(info_ref[INDEX + place] == index)
                def _(piece=piece, low=low, span=span):
                    for which, out in enumerate(outs):
                        start = which * part
                        out[:, low : low + span] = piece[:, start : start + span].astype(F32)

    return small(
        body,
        [shape((rows, cols), F32)] * count,
        [],
        info,
        kept,
        got,
        last,
    )


def sequence_info(length_row, places):
    seq_ends = jnp.cumsum(length_row)
    starts = seq_ends - length_row
    inside = (places[:, None] >= starts[None, :]) & (places[:, None] < seq_ends[None, :])
    return jnp.sum(jnp.where(inside, starts[None, :], 0), axis=1)


def per_device(
    tokens,
    out_grad,
    lengths,
    attn_gain,
    q_weight,
    q_bias,
    k_weight,
    k_bias,
    v_weight,
    v_bias,
    o_weight,
    mlp_gain,
    gate_weight,
    up_weight,
    down_weight,
):
    CLOCK[0] = None
    topo = Topo()
    info = topo.info
    line, square = topo.line, topo.square
    local_rows, width = tokens.shape
    shard_rows = q_weight.shape[0]
    block = width // LINE
    q_cols = q_weight.shape[1]
    kv_cols = k_weight.shape[1]
    qkv_cols = q_cols + 2 * kv_cols
    ff_cols = gate_weight.shape[1]
    part = -(-ff_cols // (LINE * LANES)) * LANES
    q_heads, kv_heads = q_cols // HEAD_DIM, kv_cols // HEAD_DIM
    tile = local_rows * LINE // 2

    attn_own_weight = beside(info, q_weight, k_weight, v_weight, o_weight)
    attn_one = topo.swap(attn_own_weight, line, 0)
    gate_up_send, gate_up_keep = cut_columns(info, part, gate_weight, up_weight)

    attn_joined = join(info, attn_own_weight, attn_one)
    attn_two = topo.swap(attn_joined, line, 1)
    bias_all = jnp.concatenate([q_bias, k_bias, v_bias]).astype(F32)[None, :]
    gains = jnp.stack([attn_gain, mlp_gain]).astype(F32)
    attn_own, inputs, gains = open_rows(info, tokens, gains)
    gain_one, gain_two = gains[0:1], gains[1:2]
    attn_other = topo.other_core(attn_own)
    out_grad_in = turn_rows(info, out_grad)
    row_ids = jnp.arange(local_rows, dtype=jnp.int32)
    places = jnp.concatenate(
        [topo.core * local_rows + row_ids, (1 - topo.core) * local_rows + row_ids]
    )
    starts = sequence_info(lengths[0], places)
    frequency = jnp.power(ROPE_BASE, -2.0 * jnp.arange(HEAD_DIM // 2, dtype=F32) / HEAD_DIM)
    angles = (places - starts).astype(F32)[:, None] * frequency[None, :]
    cosine_half, sine_half = jnp.cos(angles), jnp.sin(angles)
    cosine = jnp.concatenate([cosine_half, cosine_half], axis=1)
    sine = jnp.concatenate([-sine_half, sine_half], axis=1)
    row_info = jnp.stack([starts, places], axis=1)
    col_info = places[None, :]
    from_line = [(0, 0), (0, shard_rows), (1, 0), (1, shard_rows)]
    from_exchange = [(0, 0), (1, 0), (2, 0), (2, shard_rows)]

    attn_piece = placed(info, shard_rows, from_line, attn_joined, attn_two)
    attn_near = topo.swap(attn_piece, square, 0)
    gate_up_one = topo.swap(tie(info, gate_up_send), line, 0)
    attn_in = join(info, attn_own, attn_other)
    q_joined, o_joined = join_split(info, (qkv_cols, q_cols), attn_piece, attn_near)
    q_all = [q_joined, topo.swap(q_joined, square, 1)]
    o_all = [o_joined, topo.swap(o_joined, square, 1)]
    gate_up_two = topo.swap(second_chunks(info, gate_up_keep, gate_up_one), line, 1)

    mixed, linear, mass = attend(
        info, attn_in, q_all, bias_all, cosine, sine, row_info, col_info, q_heads, kv_heads
    )
    down_send, down_keep = cut_columns(info, part, down_weight)
    down_one = topo.swap(down_send, line, 0)
    gate_up_piece = placed(
        info, shard_rows, from_exchange, gate_up_keep, gate_up_one, gate_up_two
    )
    gate_up_near = topo.swap(gate_up_piece, square, 0)
    *other_attn, own_attn = project(info, mixed, o_all, width)
    gate_up_far = topo.swap(gate_up_piece, square, 1)
    other_attn = [topo.other_core(half_rows) for half_rows in other_attn]
    mlp_own, state = state_rows(info, inputs, own_attn, other_attn, gain_two)
    mlp_one = topo.swap(mlp_own, line, 0)

    down_two = topo.swap(second_chunks(info, down_keep, down_one), line, 1)
    mlp_half = join(info, mlp_own, mlp_one)
    mlp_two = topo.swap(mlp_half, line, 1)
    mlp_early = topo.other_core(mlp_half)
    down_piece = placed(info, shard_rows, from_exchange, down_keep, down_one, down_two)
    wait_for(info, gate_up_near, gate_up_far)
    gate_up_last = topo.swap(tie(info, gate_up_near), square, 1)
    down_near = topo.swap(down_piece, square, 0)
    wait_for(info, mlp_two)
    mlp_late = topo.other_core(tie(info, mlp_two))
    grad_out_one = topo.swap(tie(info, out_grad_in), line, 0)
    wait_for(info, gate_up_last)
    gate_up = in_square(
        info, [gate_up_piece, gate_up_near, gate_up_far, gate_up_last], width
    )
    down = [join(info, down_piece, down_near)]
    down.append(topo.swap(down[0], square, 1))
    mlp_in = join(info, mlp_half, mlp_two, mlp_early, mlp_late)
    grad_out_two = topo.swap(tie(info, out_grad_in), line, 1)

    hidden, gate_factor, up_factor = forward(info, mlp_in, gate_up, tile)
    wait_for(info, grad_out_one)
    grad_out_last = topo.swap(tie(info, grad_out_one), line, 1)
    wait_for(info, grad_out_two)
    down = in_square(info, down, width)
    out_own, out_other = down_sum(info, hidden, down, tile)
    out_other = [topo.other_core(part_rows) for part_rows in cut_rows(info, out_other, 2)]
    pair = (0, 1, False), (2, 1, False)
    single = (0, 1, False), (1, 1, False)
    chunks = (0, 2, True), (1, 2, True)
    rows = local_rows
    grad_out_halves = [join(info, out_grad_in, grad_out_one), join(info, grad_out_two, grad_out_last)]
    grad_out_others = [topo.other_core(half_rows) for half_rows in grad_out_halves]
    out_keep, out_send = sum_split(info, rows, 2, *pair, [out_own], out_other, spare=16)
    out_one = topo.swap(out_send, line, 1)
    grad_out_all = join(info, *grad_out_halves, *grad_out_others)
    factors = (grad_out_all, gate_factor, up_factor, gate_up, down)
    down_grad = functools.partial(grads_of, info, grad_out_all, [hidden], block)
    down_first = topo.swap(down_grad(3), square, 1)
    down_next = topo.swap(down_grad(2), square, 1)
    grads_other, *back_other = backward(info, 1, *factors, tile)
    back_other = [topo.other_core(part_rows) for part_rows in back_other]
    grads_own, *back_own = backward(info, 0, *factors, tile)
    wait_for(info, out_one)
    back_keep, back_send = sum_split(info, rows, 2, *pair, back_own, back_other)
    back_one = topo.swap(back_send, line, 1)
    gate_up_grad = functools.partial(grads_of, info, mlp_in, [grads_own, grads_other], block)
    gate_up_first = topo.swap(gate_up_grad(3), square, 1)
    wait_for(info, down_first, down_next)
    gate_up_send = gate_up_grad(2)
    down_last = topo.swap(down_grad(1, down_first), square, 0)
    down_kept = down_grad(0, down_next)
    back_keep, back_send = sum_split(info, rows, 1, *single, [back_keep], [back_one])
    back_two = topo.swap(back_send, line, 0)
    down_keep, down_send = sum_split(info, shard_rows, 2, *chunks, [down_kept], [down_last])
    gate_up_next = topo.swap(tie(info, gate_up_send), square, 1)
    gate_up_last = [
        topo.swap(gate_up_grad(1, gate_up_first, share), square, 0) for share in range(2)
    ]

    grad_state_low, grad_state, gain_two_grad = norm_back(
        info, state, back_keep, back_two, out_grad_in, gain_two, False
    )
    state_other = topo.other_core(grad_state_low)
    out_keep, out_send = sum_split(info, rows, 1, *single, [out_keep], [out_one])
    out_two = topo.swap(out_send, line, 0)
    down_one = topo.swap(tie(info, down_send), line, 0)
    grad_state_all = join(info, grad_state_low, state_other)
    grad_linear, bias_grad, own_part, other_part = attend_back(
        info,
        grad_state_all,
        o_all,
        q_all,
        linear,
        mass,
        cosine,
        sine,
        row_info,
        col_info,
        q_heads,
        kv_heads,
    )
    part_other = topo.other_core(other_part)
    down_two = topo.swap(second_chunks(info, down_keep, down_one), line, 1)
    q_full = grads_sent(info, attn_in, grad_linear, block)
    q_got = topo.swap(q_full, square, 1)
    o_full = grads_sent(info, grad_state_all, mixed, block)
    o_got = topo.swap(o_full, square, 1)
    block_out = close_rows(info, state, out_keep, out_two)
    gate_up_kept = gate_up_grad(0, gate_up_next)
    gate_up_keep, gate_up_send = sum_split(
        info, shard_rows, 2, *chunks, [gate_up_kept], gate_up_last
    )
    gate_up_one = topo.swap(gate_up_send, line, 0)
    (down_grads,) = columns_out(info, down_keep, down_one, down_two, part, ff_cols)
    tokens_grad, gain_one_grad = norm_back(
        info, inputs, own_part, part_other, grad_state, gain_one, True
    )
    sums = jnp.concatenate([bias_grad, gain_one_grad, gain_two_grad], axis=1)
    sums = sums.reshape(-1, LANES)
    shared = qkv_cols // LANES
    sums_got = topo.other_core(sums)
    sums = sum_rows(info, sums, sums_got, shared)
    sums_got = topo.swap(sums, square, 0)

    gate_up_two = topo.swap(second_chunks(info, gate_up_keep, gate_up_one), line, 1)
    q_kept, q_send = grads_kept(info, attn_in, grad_linear, block, q_got)
    q_last = topo.swap(q_send, square, 0)
    o_kept, o_send = grads_kept(info, grad_state_all, mixed, block, o_got)
    o_last = topo.swap(o_send, square, 0)
    sums = sum_rows(info, sums, sums_got, 0)
    sums_got = topo.swap(sums, square, 1)
    ordered = (0, 1, True), (2, 1, True)
    q_keep, q_send = sum_split(info, shard_rows, 2, *ordered, [q_kept], [q_last])
    q_one = topo.swap(q_send, line, 1)
    o_keep, o_send = sum_split(info, shard_rows, 2, *ordered, [o_kept], [o_last])
    o_one = topo.swap(o_send, line, 1)
    gate_grads, up_grads = columns_out(
        info, gate_up_keep, gate_up_one, gate_up_two, part, ff_cols
    )
    sums = sum_rows(info, sums, sums_got, 0)
    sums_got = topo.swap(sums, line, 0)
    q_keep, q_send = sum_split(info, shard_rows, 1, *single, [q_keep], [q_one])
    q_two = topo.swap(q_send, line, 0)
    sums = sum_rows(info, sums, sums_got, 0)
    sums_got = topo.swap(sums, line, 1)
    o_keep, o_send = sum_split(info, shard_rows, 1, *single, [o_keep], [o_one])
    o_two = topo.swap(o_send, line, 0)
    q_grads, k_grads, v_grads = sum_out(info, q_keep, q_two, (q_cols, kv_cols, kv_cols))
    (o_grads,) = sum_out(info, o_keep, o_two, (q_cols,))
    sums = sum_rows(info, sums, sums_got, 0).reshape(-1)
    own_bias = sums[:qkv_cols]
    gain_sum = sums[qkv_cols:].reshape(2, width)
    CLOCK[0] = None
    return (
        block_out,
        tokens_grad,
        gain_sum[0],
        q_grads,
        own_bias[:q_cols],
        k_grads,
        own_bias[q_cols : q_cols + kv_cols],
        v_grads,
        own_bias[q_cols + kv_cols :],
        o_grads,
        gain_sum[1],
        gate_grads,
        up_grads,
        down_grads,
    )


def solution(mesh):
    rows = P(("dp", "tensor"), None)
    both = P("dp", "tensor")
    half = P("tensor")
    in_specs = (
        rows, rows, P("dp", None), P(), both, half, both, half, both, half, both, P(), both, both, both,
    )
    out_specs = (
        rows, rows, P(), both, half, both, half, both, half, both, P(), both, both, both,
    )
    fast = mesh.shape["dp"] == LINE * LINE and mesh.shape["tensor"] == 2
    return jax.shard_map(
        per_device if fast else plain_device,
        mesh=mesh,
        in_specs=in_specs,
        out_specs=out_specs,
        check_vma=False,
    )
```
